256 devices in a mesh: dp: 32 (over y, z), tensor: 8 (over x, core).
Axes of the slice: x: 4, y: 4, z: 8, core: 2. Of those that a mesh axis runs over, the one named last changes fastest.
Arguments:
- hidden: bfloat16 [8192, 14336], P('dp', 'tensor'), may hold values from -6 to 6
- cotangent: bfloat16 [8192, 4096], P(('dp', 'tensor')), may hold values from -0.375 to 0.375
- error_buf: bfloat16 [14336, 4096], P('tensor', 'dp'), may hold values from -24 to 24
- q_start: float32 [4096, 64], replicated, may hold values from -6 to 6
Outputs:
- scaled_basis: float32 [14336, 64], P('tensor')
- q_new: float32 [4096, 64], replicated
The draws below stay inside these ranges and needn't reach their ends.
All inputs are finite; a program needn't handle non-finite values.
Results may differ from the reference program's by a relative error of at most 0.0003.
Values may be sent and summed in bfloat16 or wider, within the bound.
No kernel may reach another device: no remote copies, remote signals or barrier semaphores. Data moves between devices by JAX's collectives and lax.ppermute only.
A program may use at most 128 MiB of HBM per device.

```python
import math
import jax
import jax.numpy as jnp
from jax import lax

D = 4096
FF = 14336
RANK = 64
TOK = 256
TOKENS = 8192
N_DP = 32


def level_of(rng, extent, pieces, least, top_value):
    def one(position, parts):
        steps = jax.random.uniform(jax.random.fold_in(jax.random.fold_in(rng, 6), position), (parts,), jnp.float32, least / len(pieces), top_value / len(pieces))
        return jnp.repeat(jnp.exp(steps), extent[position] // parts).reshape((-1,) + (1,) * (len(extent) - position - 1))

    level = one(*pieces[0])
    for cut in pieces[1:]:
        level = level * one(*cut)
    return level


def scatter_about(stream_key, extent, spread, reach, shards=(), held_as=jnp.bfloat16):
    drawn = jax.random.normal(stream_key, extent, jnp.float32) * spread
    if len(shards) > 0:
        drawn = level_of(stream_key, extent, shards, -0.22, 0.18) * drawn
    return jnp.clip(drawn, min=-reach, max=reach).astype(held_as)


def setup_inputs(seed: int = 0) -> dict:
    arg_keys = jax.random.split(jax.random.key(seed), 5)
    hidden = scatter_about(arg_keys[0], (TOKENS, FF), 1.0, 6.0, ((0, 32), (1, 8)))
    cotangent = scatter_about(arg_keys[1], (TOKENS, D), TOK ** -0.5, 0.375, ((0, 256),))
    error_buf = scatter_about(arg_keys[2], (FF, D), 4.0, 24.0, ((0, 8), (1, 32)))
    q_start = scatter_about(arg_keys[3], (D, RANK), 1.0, 6.0, (), jnp.float32)
    return {"hidden": hidden, "cotangent": cotangent, "error_buf": error_buf, "q_start": q_start}


highest = lax.Precision.HIGHEST

def cholesky_step(factor):
    gram_matrix = jnp.dot(factor.T, factor, precision=highest)
    lower_factor = jnp.linalg.cholesky(gram_matrix)
    return jax.scipy.linalg.solve_triangular(lower_factor, factor.T, lower=True).T

def reference(hidden, cotangent, error_buf, q_start):
    hidden_sets = hidden.reshape(N_DP, TOK, FF)
    cot_sets = cotangent.reshape(N_DP, TOK, D)
    errors = error_buf.astype(jnp.float32)

    def p_term(running, items):
        hid_set, cot_set = items
        projected = jnp.dot(cot_set.astype(jnp.float32), q_start, precision=highest)
        term = jnp.dot(hid_set.astype(jnp.float32).T, projected, precision=highest)
        return (running + term, None)
    p_sum, _ = lax.scan(p_term, jnp.dot(errors, q_start, precision=highest), (hidden_sets, cot_sets))
    ortho_basis = cholesky_step(cholesky_step(p_sum))

    def q_term(running, items):
        hid_set, cot_set = items
        mixed_rows = jnp.dot(hid_set.astype(jnp.float32), ortho_basis, precision=highest)
        term = jnp.dot(cot_set.astype(jnp.float32).T, mixed_rows, precision=highest)
        return (running + term, None)
    q_sum, _ = lax.scan(q_term, jnp.dot(errors.T, ortho_basis, precision=highest), (hidden_sets, cot_sets))
    q_new = q_sum / N_DP
    return (ortho_basis * math.sqrt(FF), q_new)
```

```python
import functools
import math

import jax
import jax.numpy as jnp
from jax import lax
from jax.experimental import pallas as pl
from jax.experimental.pallas import tpu as pltpu
from jax.sharding import Mesh
from jax.sharding import PartitionSpec as P

FF = 14336
D = 4096
RANK = 64
N_DP = 32
TOK = 256
NY, NZ, NX, NC = 4, 8, 4, 2
FB = FF // (NX * NC)
DB = D // (NX * NC)
EB = D // N_DP
TB = TOK // (NX * NC)
f32, bf16 = jnp.float32, jnp.bfloat16
HIGHEST = lax.Precision.HIGHEST
NN = (((1,), (0,)), ((), ()))
NT = (((1,), (1,)), ((), ()))


def split3(a):
    hi = a.astype(bf16)
    rest = a - hi.astype(f32)
    mid = rest.astype(bf16)
    low = (rest - mid.astype(f32)).astype(bf16)
    return jnp.concatenate([hi, mid, low], axis=0)


def add3(a):
    n = a.shape[0] // 3
    return a[:n] + (a[n : 2 * n] + a[2 * n :])


def dot3(a, b, dims):
    return add3(lax.dot_general(a, b, dims, preferred_element_type=f32))


def gram3(a3):
    g = lax.dot_general(a3, a3, NT, preferred_element_type=f32)
    r = RANK
    g00, g01, g02 = g[:r, :r], g[:r, r : 2 * r], g[:r, 2 * r :]
    g10, g11, g20 = g[r : 2 * r, :r], g[r : 2 * r, r : 2 * r], g[2 * r :, :r]
    return g00 + ((g01 + g10) + (g11 + (g02 + g20)))


def inverse_factor(gram):
    rows = lax.broadcasted_iota(jnp.int32, (RANK, RANK), 0)
    cols = lax.broadcasted_iota(jnp.int32, (RANK, RANK), 1)
    eye = jnp.where(rows == cols, 1.0, 0.0).astype(f32)
    both = jnp.concatenate([gram, eye], axis=1)
    sub = lax.broadcasted_iota(jnp.int32, (8, 2 * RANK), 0)
    tiles = [both[8 * i : 8 * i + 8] for i in range(RANK // 8)]
    for k in range(RANK - 1):
        at, s = divmod(k, 8)
        row = tiles[at][s : s + 1]
        scaled = row * (1.0 / row[:, k : k + 1])
        for i in range(at, RANK // 8):
            if i == at and s == 7:
                continue
            new = tiles[i] - tiles[i][:, k : k + 1] * scaled
            tiles[i] = jnp.where(sub > s, new, tiles[i]) if i == at else new
    done = jnp.concatenate(tiles, axis=0)
    diagonal = jnp.sum(jnp.where(rows == cols, done[:, :RANK], 0.0), axis=1, keepdims=True)
    return done[:, RANK:] * lax.rsqrt(diagonal)


def call(kernel, out_shape, *args, scratch=(), any_at=()):
    vmem = pl.BlockSpec(memory_space=pltpu.VMEM)
    many = isinstance(out_shape, list)
    shapes = [jax.ShapeDtypeStruct(*s) for s in (out_shape if many else [out_shape])]
    return pl.pallas_call(
        kernel,
        out_shape=shapes if many else shapes[0],
        in_specs=[pl.BlockSpec(memory_space=pl.ANY) if i in any_at else vmem for i in range(len(args))],
        out_specs=[vmem] * len(shapes) if many else vmem,
        scratch_shapes=list(scratch),
        compiler_params=pltpu.CompilerParams(vmem_limit_bytes=32 * 1024 * 1024),
    )(*args)


def project_kernel(cot_ref, qt_ref, out_ref):
    got = lax.dot_general(cot_ref[...], split3(qt_ref[...]), NT, preferred_element_type=f32)
    own = got[:, :RANK] + (got[:, RANK : 2 * RANK] + got[:, 2 * RANK :])
    packed = jnp.concatenate([own[: TB // 2], own[TB // 2 :]], axis=1)
    for i in range(NX * NC):
        out_ref[i] = packed


def left_kernel(proj_ref, hidden_ref, qt_ref, err_ref, out_ref):
    packed = proj_ref[...].reshape(TOK // 2, 2 * RANK).T
    proj = jnp.concatenate([packed[:RANK], packed[RANK:]], axis=1)
    h = hidden_ref[...].reshape(NX * NC, 2, TB // 2, FB)
    h = jnp.concatenate([h[:, 0].reshape(TOK // 2, FB), h[:, 1].reshape(TOK // 2, FB)], axis=0)
    at = lax.axis_index("y") * NZ + lax.axis_index("z")
    q_own = qt_ref[:, pl.ds(pl.multiple_of(at * EB, EB), EB)]
    part = dot3(split3(proj), h, NN) + dot3(split3(q_own), err_ref[...], NT)
    out_ref[...] = part.reshape(NY, RANK // NY, FB)


def sum_y_kernel(in_ref, out_ref):
    total = (in_ref[0] + in_ref[1]) + (in_ref[2] + in_ref[3])
    for i in range(NZ):
        out_ref[i] = total[2 * i : 2 * i + 2]


def sum_z_kernel(in_ref, out_ref):
    a = [in_ref[i] for i in range(NZ)]
    while len(a) > 1:
        a = [a[i] + a[i + 1] for i in range(0, len(a), 2)]
    for i in range(NZ):
        out_ref[i] = a[0]


def spread_y_kernel(in_ref, out_ref):
    block = jnp.concatenate([in_ref[i] for i in range(NZ)], axis=0)
    for i in range(NY):
        out_ref[i] = block


def mixed_kernel(p_ref, hidden_ref, err_ref, keep_ref, send_ref, all_ref):
    p3 = split3(p_ref[...].reshape(RANK, FB))
    all_ref[:, :TOK] = dot3(p3, hidden_ref[...], NT)
    all_ref[:, TOK : TOK + EB] = dot3(p3, err_ref[...], NN)
    all_ref[:, TOK + EB :] = jnp.concatenate([gram3(p3), jnp.zeros((RANK, RANK), f32)], axis=1)
    c, half = lax.axis_index("c"), RANK // 2
    keep_ref[...] = all_ref[pl.ds(pl.multiple_of(c * half, half), half), :]
    send_ref[...] = all_ref[pl.ds(pl.multiple_of((1 - c) * half, half), half), :]


def pair_kernel(a_ref, b_ref, out_ref):
    total = a_ref[...] + b_ref[...]
    for i in range(NX):
        out_ref[i] = total


def sum_x_kernel(in_ref, out_ref):
    out_ref[...] = (in_ref[0] + in_ref[1]) + (in_ref[2] + in_ref[3])


def right_kernel(own_ref, other_ref, p_ref, cot_ref, s_ref, basis_ref, inv_ref, gram_ref, both_ref, cols_ref, sem):
    x, c = lax.axis_index("x"), lax.axis_index("c")
    at, block, half = lax.axis_index("y") * NZ + lax.axis_index("z"), x * NC + c, RANK // 2
    fetch = pltpu.make_async_copy(cot_ref.at[:, pl.ds(pl.multiple_of(block * DB, DB), DB)], cols_ref, sem)
    fetch.start()
    both_ref[pl.ds(pl.multiple_of(c * half, half), half), :] = own_ref[...]
    both_ref[pl.ds(pl.multiple_of((1 - c) * half, half), half), :] = other_ref[...]
    inverse = inverse_factor(both_ref[:, TOK + EB : TOK + EB + RANK])
    inv_ref[...] = inverse
    basis = jnp.dot(inverse, p_ref[...].reshape(RANK, FB), precision=HIGHEST, preferred_element_type=f32)
    basis_ref[...] = basis
    gram_ref[...] = jnp.concatenate([gram3(split3(basis)), jnp.zeros((RANK, RANK), f32)], axis=1)
    err_q = both_ref[:, TOK : TOK + EB]
    mixed = split3(both_ref[:, :TOK])
    fetch.wait()
    part = dot3(mixed, cols_ref[...], NN)
    here = [jnp.where(at == block * (DB // EB) + i, err_q, 0.0) for i in range(DB // EB)]
    part = part + jnp.concatenate(here, axis=1)
    for i in range(N_DP):
        s_ref[i] = part[2 * i : 2 * i + 2]


def sum_dp_kernel(in_ref, out_ref):
    a = [in_ref[i] for i in range(N_DP)]
    while len(a) > 1:
        a = [a[i] + a[i + 1] for i in range(0, len(a), 2)]
    for i in range(N_DP):
        out_ref[i] = a[0]


def spread_x_kernel(in_ref, gram_ref, other_ref, out_ref):
    block = jnp.concatenate([in_ref[i] for i in range(N_DP)], axis=0)
    gram = gram_ref[...] + other_ref[...]
    for i in range(NX):
        out_ref[i, :, :DB] = block
        out_ref[i, :, DB:] = gram


def basis_kernel(got_ref, basis_ref, inv_ref, out_ref, total_ref):
    g = [got_ref[i, :, DB : DB + RANK] for i in range(NX)]
    inverse = inverse_factor((g[0] + g[1]) + (g[2] + g[3]))
    dot = functools.partial(jnp.dot, precision=HIGHEST, preferred_element_type=f32)
    total_ref[...] = dot(inverse, inv_ref[...]) * (1.0 / N_DP)
    out_ref[...] = dot(inverse * math.sqrt(FF), basis_ref[...])


def new_kernel(own_ref, other_ref, total_ref, out_ref):
    c = lax.axis_index("c")
    total = total_ref[...]
    for i in range(NX):
        for ref, core in ((own_ref, c), (other_ref, 1 - c)):
            got = jnp.dot(total, ref[i, :, :DB], precision=HIGHEST, preferred_element_type=f32)
            out_ref[:, pl.ds(pl.multiple_of((i * NC + core) * DB, DB), DB)] = got


def swap(a):
    return lax.ppermute(a, "c", [(0, 1), (1, 0)])


def exchange(a, axes):
    return lax.all_to_all(a, axes, 0, 0)


def shards(hidden, cotangent, error_buf, q_start):
    qt = q_start.T
    cot_all = lax.all_gather(cotangent, ("x", "c"), axis=0, tiled=True)
    proj = exchange(call(project_kernel, ((NX * NC, TB // 2, 2 * RANK), f32), cotangent, qt), ("x", "c"))
    p = exchange(call(left_kernel, ((NY, RANK // NY, FB), f32), proj, hidden, qt, error_buf), "y")
    p = exchange(call(sum_y_kernel, ((NZ, 2, FB), f32), p), "z")
    p = exchange(call(sum_z_kernel, ((NZ, 2, FB), f32), p), "z")
    p = exchange(call(spread_y_kernel, ((NY, RANK // NY, FB), f32), p), "y")
    half = ((RANK // 2, DB), f32)
    keep, send = call(mixed_kernel, [half, half], p, hidden, error_buf, scratch=[pltpu.VMEM((RANK, DB), f32)])
    mixed = exchange(call(pair_kernel, ((NX, RANK // 2, DB), f32), keep, swap(send)), "x")
    mixed = call(sum_x_kernel, half, mixed)
    s, basis, inverse, gram = call(
        right_kernel,
        [((N_DP, 2, DB), f32), ((RANK, FB), f32), ((RANK, RANK), f32), ((RANK, 2 * RANK), f32)],
        mixed, swap(mixed), p, cot_all,
        scratch=[pltpu.VMEM((RANK, DB), f32), pltpu.VMEM((TOK, DB), bf16), pltpu.SemaphoreType.DMA],
        any_at=(3,),
    )
    gram_other = swap(gram)
    s = exchange(s, ("y", "z"))
    s = exchange(call(sum_dp_kernel, ((N_DP, 2, DB), f32), s), ("y", "z"))
    s = exchange(call(spread_x_kernel, ((NX, RANK, DB + 2 * RANK), f32), s, gram, gram_other), "x")
    s_other = swap(s)
    scaled, total = call(basis_kernel, [((RANK, FB), f32), ((RANK, RANK), f32)], s, basis, inverse)
    q_new = call(new_kernel, ((RANK, D), f32), s, s_other, total)
    return scaled.T, q_new.T


def solution(mesh):
    fine = Mesh(mesh.devices.reshape(NY, NZ, NX, NC), ("y", "z", "x", "c"))
    dp, tensor = ("y", "z"), ("x", "c")
    placed = (P(dp, tensor), P(dp + tensor, None), P(tensor, dp), P())
    return jax.shard_map(
        shards, mesh=fine, in_specs=placed, out_specs=(P(tensor, None), P()), check_vma=False
    )
```

```python
import functools
import math

import jax
import jax.numpy as jnp
from jax import lax
from jax.experimental import pallas as pl
from jax.experimental.pallas import tpu as pltpu
from jax.sharding import Mesh
from jax.sharding import PartitionSpec as P

FF = 14336
D = 4096
RANK = 64
N_DP = 32
TOK = 256
NY, NZ, NX, NC = 4, 8, 4, 2
FB = FF // (NX * NC)
DB = D // (NX * NC)
EB = D // N_DP
TB = TOK // (NX * NC)
f32, bf16 = jnp.float32, jnp.bfloat16
HIGHEST = lax.Precision.HIGHEST
NN = (((1,), (0,)), ((), ()))
NT = (((1,), (1,)), ((), ()))
TN = (((0,), (0,)), ((), ()))


def split3(a):
    hi = a.astype(bf16)
    rest = a - hi.astype(f32)
    mid = rest.astype(bf16)
    low = (rest - mid.astype(f32)).astype(bf16)
    return jnp.concatenate([hi, mid, low], axis=0)


def add3(a):
    n = a.shape[0] // 3
    return a[:n] + (a[n : 2 * n] + a[2 * n :])


def dot3(a, b, dims):
    return add3(lax.dot_general(a, b, dims, preferred_element_type=f32))


def gram3(a3):
    g = lax.dot_general(a3, a3, NT, preferred_element_type=f32)
    r = RANK
    g00, g01, g02 = g[:r, :r], g[:r, r : 2 * r], g[:r, 2 * r :]
    g10, g11, g20 = g[r : 2 * r, :r], g[r : 2 * r, r : 2 * r], g[2 * r :, :r]
    return g00 + ((g01 + g10) + (g11 + (g02 + g20)))


def inverse_factor(gram):
    rows = lax.broadcasted_iota(jnp.int32, (RANK, RANK), 0)
    cols = lax.broadcasted_iota(jnp.int32, (RANK, RANK), 1)
    eye = jnp.where(rows == cols, 1.0, 0.0).astype(f32)
    both = jnp.concatenate([gram, eye], axis=1)
    sub = lax.broadcasted_iota(jnp.int32, (8, 2 * RANK), 0)
    tiles = [both[8 * i : 8 * i + 8] for i in range(RANK // 8)]
    for k in range(RANK - 1):
        at, s = divmod(k, 8)
        row = tiles[at][s : s + 1]
        scaled = row * (1.0 / row[:, k : k + 1])
        for i in range(at, RANK // 8):
            if i == at and s == 7:
                continue
            new = tiles[i] - tiles[i][:, k : k + 1] * scaled
            tiles[i] = jnp.where(sub > s, new, tiles[i]) if i == at else new
    done = jnp.concatenate(tiles, axis=0)
    diagonal = jnp.sum(jnp.where(rows == cols, done[:, :RANK], 0.0), axis=1, keepdims=True)
    return done[:, RANK:] * lax.rsqrt(diagonal)


def call(kernel, out_shape, *args, scratch=(), hbm=(), out_hbm=False):
    vmem, far = pl.BlockSpec(memory_space=pltpu.VMEM), pl.BlockSpec(memory_space=pltpu.HBM)
    many = isinstance(out_shape, list)
    shapes = [jax.ShapeDtypeStruct(*s) for s in (out_shape if many else [out_shape])]
    out = far if out_hbm else vmem
    return pl.pallas_call(
        kernel,
        out_shape=shapes if many else shapes[0],
        in_specs=[far if i in hbm else vmem for i in range(len(args))],
        out_specs=[out] * len(shapes) if many else out,
        scratch_shapes=list(scratch),
        compiler_params=pltpu.CompilerParams(vmem_limit_bytes=32 * 1024 * 1024),
    )(*args)


def rows_at(index, size):
    return pl.ds(pl.multiple_of(index * size, size), size)


def in_order(index, refs):
    for k, ref in enumerate(refs):
        yield lax.rem(index + 4 - k, 4), ref


def sum_in_order(slots_ref, index, refs):
    for place, ref in in_order(index, refs):
        slots_ref[place] = ref[...]
    return (slots_ref[0] + slots_ref[1]) + (slots_ref[2] + slots_ref[3])


def scatter(whole_ref, index, refs):
    size = whole_ref.shape[0] // 4
    for k, ref in enumerate(refs):
        ref[...] = whole_ref[rows_at(lax.rem(index + k, 4), size), :]


def project_kernel(cot_ref, qt_ref, hidden_ref, err_ref, out_ref, h_ref, e_ref, cot, qt, sems):
    pairs = ((qt_ref, qt), (cot_ref, cot), (hidden_ref, h_ref), (err_ref, e_ref))
    copies = [pltpu.make_async_copy(a, b, sems.at[i]) for i, (a, b) in enumerate(pairs)]
    for copy in copies:
        copy.start()
    copies[0].wait()
    copies[1].wait()
    c = cot[...]
    got = lax.dot_general(c, split3(qt[...]), NT, preferred_element_type=f32)
    own = got[:, :RANK] + (got[:, RANK : 2 * RANK] + got[:, 2 * RANK :])
    pieces = split3(own)
    wide = jnp.concatenate([pieces[i * TB : (i + 1) * TB] for i in range(3)] + [jnp.zeros((TB, RANK), bf16)], axis=1)
    for i in range(NX * NC):
        out_ref[i, :, :DB] = c[:, i * DB : (i + 1) * DB]
        out_ref[i, :, DB:] = wide
    copies[2].wait()
    copies[3].wait()


def left_kernel(got_ref, hidden_ref, err_ref, qt_ref, own_ref, a_ref, b_ref, c_ref, whole_ref, q_ref, sem):
    at = lax.axis_index("y") * NZ + lax.axis_index("z")
    fetch = pltpu.make_async_copy(qt_ref.at[:, rows_at(at, EB)], q_ref, sem)
    fetch.start()
    proj = got_ref[:, :, DB : DB + 4 * RANK].reshape(TOK, 4 * RANK)
    part = lax.dot_general(proj, hidden_ref[...], TN, preferred_element_type=f32)
    fetch.wait()
    whole_ref[...] = add3(part[: 3 * RANK]) + dot3(split3(q_ref[...]), err_ref[...], NT)
    scatter(whole_ref, lax.axis_index("y"), (own_ref, a_ref, b_ref, c_ref))


def halve_kernel(own_ref, a_ref, b_ref, c_ref, keep_ref, send_ref, slots_ref, both_ref):
    both_ref[...] = sum_in_order(slots_ref, lax.axis_index("y"), (own_ref, a_ref, b_ref, c_ref))
    bit, half = lax.rem(lax.axis_index("z"), 2), keep_ref.shape[0]
    keep_ref[...] = both_ref[rows_at(bit, half), :]
    send_ref[...] = both_ref[rows_at(1 - bit, half), :]


def add_kernel(a_ref, b_ref, out_ref):
    out_ref[...] = a_ref[...] + b_ref[...]


def sum_z_kernel(own_ref, a_ref, b_ref, c_ref, out_ref, slots_ref):
    out_ref[...] = sum_in_order(slots_ref, lax.axis_index("z") // 2, (own_ref, a_ref, b_ref, c_ref))


def sum_x_kernel(own_ref, a_ref, b_ref, c_ref, out_ref, slots_ref):
    out_ref[...] = sum_in_order(slots_ref, lax.axis_index("x"), (own_ref, a_ref, b_ref, c_ref))


def join_z_kernel(own_ref, other_ref, out_ref):
    bit, half = lax.rem(lax.axis_index("z"), 2), own_ref.shape[0]
    out_ref[rows_at(bit, half), :] = own_ref[...]
    out_ref[rows_at(1 - bit, half), :] = other_ref[...]


def mixed_kernel(own_ref, a_ref, b_ref, c_ref, hidden_ref, err_ref, p_ref, keep_ref, send_ref, all_ref):
    for place, ref in in_order(lax.axis_index("y"), (own_ref, a_ref, b_ref, c_ref)):
        p_ref[rows_at(place, RANK // NY), :] = ref[...]
    p3 = split3(p_ref[...])
    all_ref[:, :TOK] = dot3(p3, hidden_ref[...], NT)
    all_ref[:, TOK : TOK + EB] = dot3(p3, err_ref[...], NN)
    all_ref[:, TOK + EB :] = jnp.concatenate([gram3(p3), jnp.zeros((RANK, RANK), f32)], axis=1)
    c, half = lax.axis_index("c"), RANK // 2
    keep_ref[...] = all_ref[rows_at(c, half), :]
    send_ref[...] = all_ref[rows_at(1 - c, half), :]


def right_kernel(mine_ref, other_ref, got_ref, own_ref, a_ref, b_ref, c_ref, both_ref, whole_ref):
    x, c, half = lax.axis_index("x"), lax.axis_index("c"), RANK // 2
    at, block = lax.axis_index("y") * NZ + lax.axis_index("z"), x * NC + c
    both_ref[rows_at(c, half), :] = mine_ref[:, : TOK + EB]
    both_ref[rows_at(1 - c, half), :] = other_ref[:, : TOK + EB]
    err_q = both_ref[:, TOK:]
    part = dot3(split3(both_ref[:, :TOK]), got_ref[:, :, :DB].reshape(TOK, DB), NN)
    here = [jnp.where(at == block * (DB // EB) + i, err_q, 0.0) for i in range(DB // EB)]
    whole_ref[...] = part + jnp.concatenate(here, axis=1)
    scatter(whole_ref, lax.axis_index("y"), (own_ref, a_ref, b_ref, c_ref))


def first_kernel(mine_ref, other_ref, p_ref, basis_ref, inv_ref, gram_ref, both_ref):
    c, half = lax.axis_index("c"), RANK // 2
    both_ref[rows_at(c, half), :] = mine_ref[:, TOK + EB :]
    both_ref[rows_at(1 - c, half), :] = other_ref[:, TOK + EB :]
    inverse = inverse_factor(both_ref[:, :RANK])
    inv_ref[...] = inverse
    basis = jnp.dot(inverse, p_ref[...], precision=HIGHEST, preferred_element_type=f32)
    basis_ref[...] = basis
    gram = gram3(split3(basis))
    gram_ref[...] = jnp.concatenate([gram[:half], gram[half:]], axis=1)


def second_kernel(own_ref, a_ref, b_ref, c_ref, basis_ref, inv_ref, out_ref, total_ref, slots_ref):
    gram = sum_in_order(slots_ref, lax.axis_index("x"), (own_ref, a_ref, b_ref, c_ref))
    inverse = inverse_factor(jnp.concatenate([gram[:, :RANK], gram[:, RANK:]], axis=0))
    dot = functools.partial(jnp.dot, precision=HIGHEST, preferred_element_type=f32)
    total_ref[...] = dot(inverse, inv_ref[...]) * (1.0 / N_DP)
    out_ref[...] = dot(inverse * math.sqrt(FF), basis_ref[...])


def block_kernel(own_ref, a_ref, b_ref, c_ref, total_ref, out_ref, whole_ref):
    for place, ref in in_order(lax.axis_index("y"), (own_ref, a_ref, b_ref, c_ref)):
        whole_ref[rows_at(place, RANK // NY), :] = ref[...]
    out_ref[...] = jnp.dot(total_ref[...], whole_ref[...], precision=HIGHEST, preferred_element_type=f32)


def new_kernel(*refs):
    out_ref, sems = refs[8:]
    x, c = lax.axis_index("x"), lax.axis_index("c")
    copies = []
    for half, core in ((refs[:4], c), (refs[4:8], 1 - c)):
        for place, ref in in_order(x, half):
            to = out_ref.at[:, rows_at(place * NC + core, DB)]
            copies.append(pltpu.make_async_copy(ref, to, sems.at[len(copies)]))
            copies[-1].start()
    for copy in copies:
        copy.wait()


def swap(a):
    return lax.ppermute(a, "c", [(0, 1), (1, 0)])


def swap_z(a):
    return lax.ppermute(a, "z", [(i, i ^ 1) for i in range(NZ)])


def shift(a, axis, k):
    size, step = {"y": (NY, 1), "z": (NZ, 2), "x": (NX, 1)}[axis]
    return lax.ppermute(a, axis, [(i, (i + k * step) % size) for i in range(size)])


def deal(blocks, axis):
    return [blocks[0]] + [shift(blocks[k], axis, k) for k in (1, 2, 3)]


def share(block, axis):
    return deal([block] * 4, axis)


def sum_dp(parts, width):
    quarter, eighth = ((RANK // NY, width), f32), ((RANK // NY // 2, width), f32)
    slots = pltpu.VMEM((4, *eighth[0]), f32)
    keep, send = call(
        halve_kernel, [eighth, eighth], *deal(parts, "y"),
        scratch=[pltpu.VMEM((4, *quarter[0]), f32), pltpu.VMEM(*quarter)],
    )
    pair = call(add_kernel, eighth, keep, swap_z(send))
    own = call(sum_z_kernel, eighth, *share(pair, "z"), scratch=[slots])
    return call(join_z_kernel, quarter, own, swap_z(own))


def shards(hidden, cotangent, error_buf, q_start):
    qt = q_start.T
    dma = pltpu.SemaphoreType.DMA
    got, hid, err = call(
        project_kernel,
        [((NX * NC, TB, DB + 4 * RANK), bf16), ((TOK, FB), bf16), ((FB, EB), bf16)],
        cotangent, qt, hidden, error_buf,
        scratch=[pltpu.VMEM((TB, D), bf16), pltpu.VMEM((RANK, D), f32), dma((4,))],
        hbm=(0, 1, 2, 3),
    )
    got = lax.all_to_all(got, ("x", "c"), 0, 0)
    quarter = ((RANK // NY, FB), f32)
    parts = call(
        left_kernel, [quarter] * 4, got, hid, err, qt,
        scratch=[pltpu.VMEM((RANK, FB), f32), pltpu.VMEM((RANK, EB), f32), dma], hbm=(3,),
    )
    p = sum_dp(parts, FB)
    half = ((RANK // 2, DB), f32)
    p, keep, send = call(
        mixed_kernel, [((RANK, FB), f32), half, half], *share(p, "y"), hid, err, scratch=[pltpu.VMEM((RANK, DB), f32)]
    )
    mixed = call(add_kernel, half, keep, swap(send))
    mixed = call(sum_x_kernel, half, *share(mixed, "x"), scratch=[pltpu.VMEM((4, RANK // 2, DB), f32)])
    other = swap(mixed)
    parts = call(
        right_kernel, [((RANK // NY, DB), f32)] * 4, mixed, other, got,
        scratch=[pltpu.VMEM((RANK, TOK + EB), f32), pltpu.VMEM((RANK, DB), f32)],
    )
    packed = ((RANK // 2, 2 * RANK), f32)
    basis, inverse, gram = call(
        first_kernel, [((RANK, FB), f32), ((RANK, RANK), f32), packed], mixed, other, p, scratch=[pltpu.VMEM((RANK, 2 * RANK), f32)]
    )
    gram = call(add_kernel, packed, gram, swap(gram))
    scaled, total = call(
        second_kernel, [((RANK, FB), f32), ((RANK, RANK), f32)], *share(gram, "x"), basis, inverse,
        scratch=[pltpu.VMEM((4, RANK // 2, 2 * RANK), f32)],
    )
    s = sum_dp(parts, DB)
    s = call(block_kernel, ((RANK, DB), f32), *share(s, "y"), total, scratch=[pltpu.VMEM((RANK, DB), f32)])
    blocks = share(s, "x")
    q_new = call(new_kernel, ((RANK, D), f32), *blocks, *[swap(b) for b in blocks], scratch=[dma((8,))], out_hbm=True)
    return scaled.T, q_new.T


def solution(mesh):
    fine = Mesh(mesh.devices.reshape(NY, NZ, NX, NC), ("y", "z", "x", "c"))
    dp, tensor = ("y", "z"), ("x", "c")
    placed = (P(dp, tensor), P(dp + tensor, None), P(tensor, dp), P())
    return jax.shard_map(
        shards, mesh=fine, in_specs=placed, out_specs=(P(tensor, None), P()), check_vma=False
    )
```

```python
import functools
import math

import jax
import jax.numpy as jnp
from jax import lax
from jax.experimental import pallas as pl
from jax.experimental.pallas import tpu as pltpu
from jax.sharding import Mesh
from jax.sharding import PartitionSpec as P

FF = 14336
D = 4096
RANK = 64
N_DP = 32
TOK = 256
NY, NZ, NX, NC = 4, 8, 4, 2
FB = FF // (NX * NC)
CB = D // NX
EB = D // N_DP
TB = TOK // (NX * NC)
f32, bf16 = jnp.float32, jnp.bfloat16
HIGHEST = lax.Precision.HIGHEST
NN = (((1,), (0,)), ((), ()))
NT = (((1,), (1,)), ((), ()))
TN = (((0,), (0,)), ((), ()))


def split3(a):
    hi = a.astype(bf16)
    rest = a - hi.astype(f32)
    mid = rest.astype(bf16)
    low = (rest - mid.astype(f32)).astype(bf16)
    return jnp.concatenate([hi, mid, low], axis=0)


def add3(a):
    n = a.shape[0] // 3
    return a[:n] + (a[n : 2 * n] + a[2 * n :])


def dot3(a, b, dims):
    return add3(lax.dot_general(a, b, dims, preferred_element_type=f32))


def gram3(a3):
    g = lax.dot_general(a3, a3, NT, preferred_element_type=f32)
    r = RANK
    g00, g01, g02 = g[:r, :r], g[:r, r : 2 * r], g[:r, 2 * r :]
    g10, g11, g20 = g[r : 2 * r, :r], g[r : 2 * r, r : 2 * r], g[2 * r :, :r]
    return g00 + ((g01 + g10) + (g11 + (g02 + g20)))


def wide(column):
    return jnp.broadcast_to(column, (8, 2 * RANK))


def inverse_factor(gram):
    rows = lax.broadcasted_iota(jnp.int32, (RANK, RANK), 0)
    cols = lax.broadcasted_iota(jnp.int32, (RANK, RANK), 1)
    both = jnp.concatenate([gram, jnp.where(rows == cols, 1.0, 0.0).astype(f32)], axis=1)
    sub = lax.broadcasted_iota(jnp.int32, (8, 2 * RANK), 0)
    count = RANK // 8
    tiles = [both[8 * i : 8 * i + 8] for i in range(count)]
    for p in range(count):
        columns = [[wide(tiles[i][:, 8 * p + j : 8 * p + j + 1]) for j in range(8)] for i in range(p, count)]
        panel, own, pivots, scales = tiles[p], columns[0], jnp.ones((8, 2 * RANK), f32), []
        for s in range(8):
            pivot = own[s][s : s + 1]
            scales.append(1.0 / pivot)
            pivots = jnp.where(sub == s, pivot, pivots)
            factor = jnp.where(sub > s, own[s] * scales[s], 0.0)
            panel = panel - factor * panel[s : s + 1]
            for j in range(s + 1, 8):
                own[j] = own[j] - factor * own[j][s : s + 1]
        for i in range(p + 1, count):
            below, tile = columns[i - p], tiles[i]
            for s in range(8):
                factor = below[s] * scales[s]
                tile = tile - factor * panel[s : s + 1]
                for j in range(s + 1, 8):
                    below[j] = below[j] - factor * own[j][s : s + 1]
            tiles[i] = tile
        tiles[p] = panel * lax.rsqrt(pivots)
    return jnp.concatenate(tiles, axis=0)[:, RANK:]


def near_inverse_factor(off):
    rows = lax.broadcasted_iota(jnp.int32, (RANK, RANK), 0)
    cols = lax.broadcasted_iota(jnp.int32, (RANK, RANK), 1)
    lower = jnp.where(rows > cols, 1.0, jnp.where(rows == cols, 0.5, 0.0)).astype(f32)
    first = off * lower
    second = -lower * lax.dot_general(first, first, NT, precision=HIGHEST, preferred_element_type=f32)
    square = jnp.dot(first, first, precision=HIGHEST, preferred_element_type=f32)
    eye = jnp.where(rows == cols, 1.0, 0.0).astype(f32)
    return eye - first + (square - second)


def dot6(a, b3):
    hi = a.astype(bf16).astype(f32)
    mid = (a - hi).astype(bf16).astype(f32)
    low = a - hi - mid
    one = jnp.concatenate([hi, hi, hi, mid], axis=1).astype(bf16)
    two = jnp.concatenate([mid, low], axis=1).astype(bf16)
    high, middle = b3[:RANK], b3[RANK : 2 * RANK]
    out = jnp.dot(one, jnp.concatenate([b3, high], axis=0), preferred_element_type=f32)
    return out + jnp.dot(two, jnp.concatenate([middle, high], axis=0), preferred_element_type=f32)


def pack(square):
    return jnp.concatenate([square[: RANK // 2], square[RANK // 2 :]], axis=1)


def unpack(packed):
    return jnp.concatenate([packed[:, :RANK], packed[:, RANK:]], axis=0)


def call(kernel, out_shape, *args, scratch=(), hbm=(), unread=()):
    vmem, far, anywhere = (pl.BlockSpec(memory_space=m) for m in (pltpu.VMEM, pltpu.HBM, pl.ANY))
    many = isinstance(out_shape, list)
    shapes = [jax.ShapeDtypeStruct(*s) for s in (out_shape if many else [out_shape])]
    return pl.pallas_call(
        kernel,
        out_shape=shapes if many else shapes[0],
        in_specs=[far if i in hbm else anywhere if i in unread else vmem for i in range(len(args))],
        out_specs=[vmem] * len(shapes) if many else vmem,
        scratch_shapes=list(scratch),
        compiler_params=pltpu.CompilerParams(vmem_limit_bytes=32 * 1024 * 1024),
    )(*args)


def rows_at(index, size):
    return pl.ds(pl.multiple_of(index * size, size), size)


def in_order(index, refs):
    for k, ref in enumerate(refs):
        yield lax.rem(index + 4 - k, 4), ref


def sum_in_order(slots_ref, index, refs):
    for place, ref in in_order(index, refs):
        slots_ref[place] = ref[...]
    return (slots_ref[0] + slots_ref[1]) + (slots_ref[2] + slots_ref[3])


def scatter(whole_ref, index, refs):
    size = whole_ref.shape[0] // 4
    for k, ref in enumerate(refs):
        ref[...] = whole_ref[rows_at(lax.rem(index + k, 4), size), :]


def project_kernel(cot_ref, qt_ref, hidden_ref, err_ref, out_ref, c_ref, h_ref, e_ref, qt, sems):
    pairs = ((qt_ref, qt), (cot_ref, c_ref), (hidden_ref, h_ref), (err_ref, e_ref))
    copies = [pltpu.make_async_copy(a, b, sems.at[i]) for i, (a, b) in enumerate(pairs)]
    for copy in copies:
        copy.start()
    copies[0].wait()
    q3 = split3(qt[...])
    copies[1].wait()
    got = lax.dot_general(c_ref[...], q3, NT, preferred_element_type=f32)
    pieces = split3(got[:, :RANK] + (got[:, RANK : 2 * RANK] + got[:, 2 * RANK :]))
    pieces = [pieces[i * TB : (i + 1) * TB] for i in range(3)]
    out_ref[...] = jnp.concatenate(pieces + [jnp.zeros((TB, RANK), bf16)], axis=1)
    copies[2].wait()
    copies[3].wait()


def join_c_kernel(own_ref, other_ref, out_ref):
    c, half = lax.axis_index("c"), own_ref.shape[0]
    out_ref[rows_at(c, half), :] = own_ref[...]
    out_ref[rows_at(1 - c, half), :] = other_ref[...]


def columns_kernel(shifts, own_ref, other_ref, after_ref, *out_refs):
    x, c = lax.axis_index("x"), lax.axis_index("c")
    for k, ref in zip(shifts, out_refs, strict=True):
        cols = rows_at(lax.rem(x + k, NX), CB)
        ref[rows_at(c, TB), :] = own_ref[:, cols]
        ref[rows_at(1 - c, TB), :] = other_ref[:, cols]


def left_kernel(
    got_ref, a_got_ref, b_got_ref, c_got_ref, hidden_ref, err_ref, qt_ref, cot_ref,
    own_ref, a_ref, b_ref, c_ref, pass_ref, slots_ref, whole_ref, q_ref, sem,
):
    at = lax.axis_index("y") * NZ + lax.axis_index("z")
    fetch = pltpu.make_async_copy(qt_ref.at[:, rows_at(at, EB)], q_ref, sem)
    fetch.start()
    for place, ref in in_order(lax.axis_index("x"), (got_ref, a_got_ref, b_got_ref, c_got_ref)):
        slots_ref[place] = ref[...]
    proj = slots_ref[...].reshape(TOK, 4 * RANK)
    part = lax.dot_general(proj, hidden_ref[...], TN, preferred_element_type=f32)
    pass_ref[...] = cot_ref[...]
    fetch.wait()
    whole_ref[...] = add3(part[: 3 * RANK]) + dot3(split3(q_ref[...]), err_ref[...], NT)
    scatter(whole_ref, lax.axis_index("y"), (own_ref, a_ref, b_ref, c_ref))


def halve_kernel(own_ref, a_ref, b_ref, c_ref, keep_ref, send_ref, slots_ref, both_ref):
    both_ref[...] = sum_in_order(slots_ref, lax.axis_index("y"), (own_ref, a_ref, b_ref, c_ref))
    bit, half = lax.rem(lax.axis_index("z"), 2), keep_ref.shape[0]
    keep_ref[...] = both_ref[rows_at(bit, half), :]
    send_ref[...] = both_ref[rows_at(1 - bit, half), :]


def add_kernel(a_ref, b_ref, out_ref):
    out_ref[...] = a_ref[...] + b_ref[...]


def sum_z_kernel(own_ref, a_ref, b_ref, c_ref, out_ref, slots_ref):
    out_ref[...] = sum_in_order(slots_ref, lax.axis_index("z") // 2, (own_ref, a_ref, b_ref, c_ref))


def sum_z_after_kernel(own_ref, a_ref, b_ref, c_ref, *rest):
    sum_z_kernel(own_ref, a_ref, b_ref, c_ref, *rest[-2:])


def sum_x_kernel(own_ref, a_ref, b_ref, c_ref, out_ref, slots_ref):
    out_ref[...] = sum_in_order(slots_ref, lax.axis_index("x"), (own_ref, a_ref, b_ref, c_ref))


def join_z_kernel(own_ref, other_ref, out_ref):
    bit, half = lax.rem(lax.axis_index("z"), 2), own_ref.shape[0]
    out_ref[rows_at(bit, half), :] = own_ref[...]
    out_ref[rows_at(1 - bit, half), :] = other_ref[...]


def mixed_kernel(own_ref, a_ref, b_ref, c_ref, hidden_ref, err_ref, after_ref, p3_ref, keep_ref, send_ref, p_ref, all_ref):
    for place, ref in in_order(lax.axis_index("y"), (own_ref, a_ref, b_ref, c_ref)):
        p_ref[rows_at(place, RANK // NY), :] = ref[...]
    p3 = split3(p_ref[...])
    p3_ref[...] = p3
    all_ref[:, :TOK] = dot3(p3, hidden_ref[...], NT)
    all_ref[:, TOK:] = dot3(p3, err_ref[...], NN)
    gram = pack(gram3(p3))
    c, half = lax.axis_index("c"), RANK // 2
    for ref, core in ((keep_ref, c), (send_ref, 1 - c)):
        ref[:, : TOK + EB] = all_ref[rows_at(core, half), :]
        ref[:, TOK + EB :] = gram


def right_kernel(mixed_ref, cot_ref, a_cot_ref, b_cot_ref, c_cot_ref, own_ref, a_ref, b_ref, c_ref, slots_ref, whole_ref):
    x, at = lax.axis_index("x"), lax.axis_index("y") * NZ + lax.axis_index("z")
    for place, ref in in_order(x, (cot_ref, a_cot_ref, b_cot_ref, c_cot_ref)):
        slots_ref[place] = ref[...]
    part = dot3(split3(mixed_ref[:, :TOK]), slots_ref[...].reshape(TOK, CB), NN)
    err_q = mixed_ref[:, TOK : TOK + EB]
    here = [jnp.where(at == x * (CB // EB) + i, err_q, 0.0) for i in range(CB // EB)]
    whole_ref[...] = part + jnp.concatenate(here, axis=1)
    scatter(whole_ref, lax.axis_index("y"), (own_ref, a_ref, b_ref, c_ref))


def first_kernel(mixed_ref, after_ref, inv_ref):
    inv_ref[...] = inverse_factor(unpack(mixed_ref[:, TOK + EB :]))


def basis_kernel(inv_ref, p3_ref, b3_ref, gram_ref):
    b3 = split3(dot6(inv_ref[...], p3_ref[...]))
    b3_ref[...] = b3
    gram_ref[...] = pack(gram3(b3))


def sum_y_kernel(own_ref, a_ref, b_ref, c_ref, after_ref, out_ref, slots_ref):
    out_ref[...] = sum_in_order(slots_ref, lax.axis_index("y"), (own_ref, a_ref, b_ref, c_ref))


def add_after_kernel(a_ref, b_ref, after_ref, out_ref):
    out_ref[...] = a_ref[...] + b_ref[...]


def block_kernel(own_ref, a_ref, b_ref, c_ref, gram_ref, other_ref, out_ref):
    for place, ref in in_order(lax.axis_index("y"), (own_ref, a_ref, b_ref, c_ref)):
        out_ref[rows_at(place, RANK // 2 // NY), :CB] = ref[...]
    out_ref[:, CB:] = gram_ref[...] + other_ref[...]


def second_kernel(own_ref, a_ref, b_ref, c_ref, b3_ref, inv_ref, out_ref, total_ref, slots_ref, inverse_ref):
    for place, ref in in_order(lax.axis_index("x"), (own_ref, a_ref, b_ref, c_ref)):
        slots_ref[place] = ref[:, CB:]
    gram = unpack((slots_ref[0] + slots_ref[1]) + (slots_ref[2] + slots_ref[3]))
    rows = lax.broadcasted_iota(jnp.int32, (RANK, RANK), 0)
    cols = lax.broadcasted_iota(jnp.int32, (RANK, RANK), 1)
    off = gram - jnp.where(rows == cols, 1.0, 0.0).astype(f32)
    near = jnp.max(jnp.abs(off)) < 1e-3

    @pl.when(near)
    def _():
        inverse_ref[...] = near_inverse_factor(off)

    @pl.when(jnp.logical_not(near))
    def _():
        inverse_ref[...] = inverse_factor(gram)

    inverse = inverse_ref[...]
    total_ref[...] = jnp.dot(inverse, inv_ref[...], precision=HIGHEST, preferred_element_type=f32) * (1.0 / N_DP)
    out_ref[...] = dot6(inverse * math.sqrt(FF), b3_ref[...])


def new_kernel(*refs):
    total_ref, out_ref, s_ref = refs[8:]
    x, c, half = lax.axis_index("x"), lax.axis_index("c"), RANK // 2
    total = total_ref[...]
    for k in range(NX):
        s_ref[rows_at(c, half), :] = refs[k][:, :CB]
        s_ref[rows_at(1 - c, half), :] = refs[NX + k][:, :CB]
        out_ref[:, rows_at(lax.rem(x + NX - k, NX), CB)] = dot6(total, split3(s_ref[...]))


def swap(a):
    return lax.ppermute(a, "c", [(0, 1), (1, 0)])


def swap_z(a):
    return lax.ppermute(a, "z", [(i, i ^ 1) for i in range(NZ)])


def shift(a, axis, k):
    size, step = {"y": (NY, 1), "z": (NZ, 2), "x": (NX, 1)}[axis]
    return lax.ppermute(a, axis, [(i, (i + k * step) % size) for i in range(size)])


def deal(blocks, axis):
    return [blocks[0]] + [shift(blocks[k], axis, k) for k in (1, 2, 3)]


def share(block, axis):
    return deal([block] * 4, axis)


def shards(hidden, cotangent, error_buf, q_start):
    qt = q_start.T
    dma, half = pltpu.SemaphoreType.DMA, RANK // 2
    pinned = [pltpu.with_memory_space_constraint(a, pltpu.HBM) for a in (cotangent, qt, hidden, error_buf)]
    proj, cot, hid, err = call(
        project_kernel,
        [((TB, 4 * RANK), bf16), ((TB, D), bf16), ((TOK, FB), bf16), ((FB, EB), bf16)], *pinned,
        scratch=[pltpu.VMEM((RANK, D), f32), dma((4,))], hbm=(0, 1, 2, 3),
    )
    proj = call(join_c_kernel, ((2 * TB, 4 * RANK), bf16), proj, swap(proj))
    quarter, eighth = ((RANK // NY, FB), f32), ((RANK // NY // 2, FB), f32)
    *parts, cot = call(
        left_kernel, [quarter] * 4 + [((TB, D), bf16)], *share(proj, "x"), hid, err, pinned[1], cot,
        scratch=[pltpu.VMEM((4, 2 * TB, 4 * RANK), bf16), pltpu.VMEM((RANK, FB), f32), pltpu.VMEM((RANK, EB), f32), dma],
        hbm=(6,),
    )
    cot_other, block = swap(cot), ((2 * TB, CB), bf16)

    keep, send = call(
        halve_kernel, [eighth, eighth], *deal(parts, "y"), scratch=[pltpu.VMEM((4, *quarter[0]), f32), pltpu.VMEM(*quarter)]
    )
    p = call(add_after_kernel, eighth, keep, swap_z(send), cot_other, unread=(2,))
    cot1, cot2 = call(functools.partial(columns_kernel, (1, 2)), [block] * 2, cot, cot_other, p, unread=(2,))
    cot1, cot2 = shift(cot1, "x", 1), shift(cot2, "x", 2)
    p = call(
        sum_z_after_kernel, eighth, *share(p, "z"), cot1, cot2, scratch=[pltpu.VMEM((4, *eighth[0]), f32)], unread=(4, 5)
    )
    cot0, cot3 = call(functools.partial(columns_kernel, (0, 3)), [block] * 2, cot, cot_other, p, unread=(2,))
    cot = (cot0, cot1, cot2, shift(cot3, "x", 3))
    p = call(join_z_kernel, quarter, p, swap_z(p))

    halves = ((half, TOK + EB + 2 * RANK), f32)
    p3, keep, send = call(
        mixed_kernel, [((3 * RANK, FB), bf16), halves, halves], *share(p, "y"), hid, err, cot[3],
        scratch=[pltpu.VMEM((RANK, FB), f32), pltpu.VMEM((RANK, TOK + EB), f32)], unread=(6,),
    )
    mixed = call(add_kernel, halves, keep, swap(send))
    mixed = call(sum_x_kernel, halves, *share(mixed, "x"), scratch=[pltpu.VMEM((4, *halves[0]), f32)])

    piece = ((half // NY, CB), f32)
    parts = call(
        right_kernel, [piece] * 4, mixed, *cot, scratch=[pltpu.VMEM((4, 2 * TB, CB), bf16), pltpu.VMEM((half, CB), f32)]
    )
    inverse = call(first_kernel, ((RANK, RANK), f32), mixed, parts[0], unread=(1,))
    s = call(sum_y_kernel, piece, *deal(parts, "y"), inverse, scratch=[pltpu.VMEM((4, *piece[0]), f32)], unread=(4,))
    b3, gram = call(basis_kernel, [((3 * RANK, FB), bf16), ((half, 2 * RANK), f32)], inverse, p3)
    s = call(add_after_kernel, piece, s, swap_z(s), gram, unread=(2,))
    s = call(sum_z_kernel, piece, *share(s, "z"), scratch=[pltpu.VMEM((4, *piece[0]), f32)])
    s = call(block_kernel, ((half, CB + 2 * RANK), f32), *share(s, "y"), gram, swap(gram))
    blocks = share(s, "x")
    scaled, total = call(
        second_kernel, [((RANK, FB), f32), ((RANK, RANK), f32)], *blocks, b3, inverse,
        scratch=[pltpu.VMEM((4, half, 2 * RANK), f32), pltpu.VMEM((RANK, RANK), f32)],
    )
    q_new = call(
        new_kernel, ((RANK, D), f32), *blocks, *[swap(b) for b in blocks], total, scratch=[pltpu.VMEM((RANK, CB), f32)]
    )
    return scaled.T, q_new.T


def solution(mesh):
    fine = Mesh(mesh.devices.reshape(NY, NZ, NX, NC), ("y", "z", "x", "c"))
    dp, tensor = ("y", "z"), ("x", "c")
    placed = (P(dp, tensor), P(dp + tensor, None), P(tensor, dp), P())
    return jax.shard_map(
        shards, mesh=fine, in_specs=placed, out_specs=(P(tensor, None), P()), check_vma=False
    )
```

```python
import functools
import math

import jax
import jax.numpy as jnp
from jax import lax
from jax.experimental import pallas as pl
from jax.experimental.pallas import tpu as pltpu
from jax.sharding import Mesh
from jax.sharding import PartitionSpec as P

FF = 14336
D = 4096
RANK = 64
N_DP = 32
TOK = 256
NY, NZ, NX, NC = 4, 8, 4, 2
FB = FF // (NX * NC)
CB = D // NX
EB = D // N_DP
TB = TOK // (NX * NC)
f32, bf16 = jnp.float32, jnp.bfloat16
HIGHEST = lax.Precision.HIGHEST
NN = (((1,), (0,)), ((), ()))
NT = (((1,), (1,)), ((), ()))
TN = (((0,), (0,)), ((), ()))


def split3(a):
    hi = a.astype(bf16)
    rest = a - hi.astype(f32)
    mid = rest.astype(bf16)
    low = (rest - mid.astype(f32)).astype(bf16)
    return jnp.concatenate([hi, mid, low], axis=0)


def add3(a):
    n = a.shape[0] // 3
    return a[:n] + (a[n : 2 * n] + a[2 * n :])


def dot3(a, b, dims):
    return add3(lax.dot_general(a, b, dims, preferred_element_type=f32))


def gram3(a3):
    g = lax.dot_general(a3, a3, NT, preferred_element_type=f32)
    r = RANK
    g00, g01, g02 = g[:r, :r], g[:r, r : 2 * r], g[:r, 2 * r :]
    g10, g11, g20 = g[r : 2 * r, :r], g[r : 2 * r, r : 2 * r], g[2 * r :, :r]
    return g00 + ((g01 + g10) + (g11 + (g02 + g20)))


def wide(column):
    return jnp.broadcast_to(column, (8, 2 * RANK))


def inverse_factor(gram):
    rows = lax.broadcasted_iota(jnp.int32, (RANK, RANK), 0)
    cols = lax.broadcasted_iota(jnp.int32, (RANK, RANK), 1)
    both = jnp.concatenate([gram, jnp.where(rows == cols, 1.0, 0.0).astype(f32)], axis=1)
    sub = lax.broadcasted_iota(jnp.int32, (8, 2 * RANK), 0)
    count = RANK // 8
    tiles = [both[8 * i : 8 * i + 8] for i in range(count)]
    for p in range(count):
        columns = [[wide(tiles[i][:, 8 * p + j : 8 * p + j + 1]) for j in range(8)] for i in range(p, count)]
        panel, own, pivots, scales = tiles[p], columns[0], jnp.ones((8, 2 * RANK), f32), []
        for s in range(8):
            pivot = own[s][s : s + 1]
            scales.append(1.0 / pivot)
            pivots = jnp.where(sub == s, pivot, pivots)
            factor = jnp.where(sub > s, own[s] * scales[s], 0.0)
            panel = panel - factor * panel[s : s + 1]
            for j in range(s + 1, 8):
                own[j] = own[j] - factor * own[j][s : s + 1]
        for i in range(p + 1, count):
            below, tile = columns[i - p], tiles[i]
            for s in range(8):
                factor = below[s] * scales[s]
                tile = tile - factor * panel[s : s + 1]
                for j in range(s + 1, 8):
                    below[j] = below[j] - factor * own[j][s : s + 1]
            tiles[i] = tile
        tiles[p] = panel * lax.rsqrt(pivots)
    return jnp.concatenate(tiles, axis=0)[:, RANK:]


def near_inverse_factor(off):
    rows = lax.broadcasted_iota(jnp.int32, (RANK, RANK), 0)
    cols = lax.broadcasted_iota(jnp.int32, (RANK, RANK), 1)
    lower = jnp.where(rows > cols, 1.0, jnp.where(rows == cols, 0.5, 0.0)).astype(f32)
    first = off * lower
    second = -lower * lax.dot_general(first, first, NT, precision=HIGHEST, preferred_element_type=f32)
    square = jnp.dot(first, first, precision=HIGHEST, preferred_element_type=f32)
    eye = jnp.where(rows == cols, 1.0, 0.0).astype(f32)
    return eye - first + (square - second)


def dot6(a, b3):
    hi = a.astype(bf16).astype(f32)
    mid = (a - hi).astype(bf16).astype(f32)
    low = a - hi - mid
    one = jnp.concatenate([hi, hi, hi, mid], axis=1).astype(bf16)
    two = jnp.concatenate([mid, low], axis=1).astype(bf16)
    high, middle = b3[:RANK], b3[RANK : 2 * RANK]
    out = jnp.dot(one, jnp.concatenate([b3, high], axis=0), preferred_element_type=f32)
    return out + jnp.dot(two, jnp.concatenate([middle, high], axis=0), preferred_element_type=f32)


def pack(square):
    return jnp.concatenate([square[: RANK // 2], square[RANK // 2 :]], axis=1)


def unpack(packed):
    return jnp.concatenate([packed[:, :RANK], packed[:, RANK:]], axis=0)


def call(kernel, out_shape, *args, scratch=(), hbm=(), unread=(), out_hbm=False):
    vmem, far, anywhere = (pl.BlockSpec(memory_space=m) for m in (pltpu.VMEM, pltpu.HBM, pl.ANY))
    many = isinstance(out_shape, list)
    shapes = [jax.ShapeDtypeStruct(*s) for s in (out_shape if many else [out_shape])]
    return pl.pallas_call(
        kernel,
        out_shape=shapes if many else shapes[0],
        in_specs=[far if i in hbm else anywhere if i in unread else vmem for i in range(len(args))],
        out_specs=[vmem] * len(shapes) if many else far if out_hbm else vmem,
        scratch_shapes=list(scratch),
        compiler_params=pltpu.CompilerParams(vmem_limit_bytes=32 * 1024 * 1024),
    )(*args)


def rows_at(index, size):
    return pl.ds(pl.multiple_of(index * size, size), size)


def in_order(index, refs):
    for k, ref in enumerate(refs):
        yield lax.rem(index + 4 - k, 4), ref


def sum_in_order(slots_ref, index, refs):
    for place, ref in in_order(index, refs):
        slots_ref[place] = ref[...]
    return (slots_ref[0] + slots_ref[1]) + (slots_ref[2] + slots_ref[3])


def scatter(whole_ref, index, refs):
    size = whole_ref.shape[0] // 4
    for k, ref in enumerate(refs):
        ref[...] = whole_ref[rows_at(lax.rem(index + k, 4), size), :]


def project_kernel(cot_ref, qt_ref, hidden_ref, err_ref, out_ref, c_ref, h_ref, e_ref, own_ref, qt, sems):
    at, cut, parts = lax.axis_index("y") * NZ + lax.axis_index("z"), 1024, []
    pairs = [(cot_ref, c_ref)]
    pairs += [(qt_ref.at[:, i : i + cut], qt.at[:, i : i + cut]) for i in range(0, D, cut)]
    pairs += [(qt_ref.at[:, rows_at(at, EB)], own_ref), (hidden_ref, h_ref), (err_ref, e_ref)]
    copies = [pltpu.make_async_copy(a, b, sems.at[i]) for i, (a, b) in enumerate(pairs)]
    for copy in copies:
        copy.start()
    copies[0].wait()
    for i in range(D // cut):
        copies[1 + i].wait()
        cols = slice(i * cut, (i + 1) * cut)
        parts.append(lax.dot_general(c_ref[:, cols], split3(qt[:, cols]), NT, preferred_element_type=f32))
    got = (parts[0] + parts[1]) + (parts[2] + parts[3])
    pieces = split3(got[:, :RANK] + (got[:, RANK : 2 * RANK] + got[:, 2 * RANK :]))
    pieces = [pieces[i * TB : (i + 1) * TB] for i in range(3)]
    out_ref[...] = jnp.concatenate(pieces + [jnp.zeros((TB, RANK), bf16)], axis=1)
    for copy in copies[1 + D // cut :]:
        copy.wait()


def join_c_kernel(own_ref, other_ref, out_ref):
    c, half = lax.axis_index("c"), own_ref.shape[0]
    out_ref[rows_at(c, half), :] = own_ref[...]
    out_ref[rows_at(1 - c, half), :] = other_ref[...]


def columns_kernel(shifts, own_ref, other_ref, after_ref, *out_refs):
    x = lax.axis_index("x")
    for k, ref in zip(shifts, out_refs, strict=True):
        cols = rows_at(lax.rem(x + k, NX), CB)
        ref[:TB, :] = other_ref[:, cols]
        ref[TB:, :] = own_ref[:, cols]


def left_kernel(
    got_ref, a_got_ref, b_got_ref, c_got_ref, hidden_ref, err_ref, q_ref, own_ref, a_ref, b_ref, c_ref, slots_ref, whole_ref
):
    for place, ref in in_order(lax.axis_index("x"), (got_ref, a_got_ref, b_got_ref, c_got_ref)):
        slots_ref[place] = ref[...]
    proj = slots_ref[...].reshape(TOK, 4 * RANK)
    part = lax.dot_general(proj, hidden_ref[...], TN, preferred_element_type=f32)
    whole_ref[...] = add3(part[: 3 * RANK]) + dot3(split3(q_ref[...]), err_ref[...], NT)
    scatter(whole_ref, lax.axis_index("y"), (own_ref, a_ref, b_ref, c_ref))


def halve_kernel(own_ref, a_ref, b_ref, c_ref, cot_ref, keep_ref, send_ref, pass_ref, slots_ref, both_ref):
    pass_ref[...] = cot_ref[...]
    both_ref[...] = sum_in_order(slots_ref, lax.axis_index("y"), (own_ref, a_ref, b_ref, c_ref))
    bit, half = lax.rem(lax.axis_index("z"), 2), keep_ref.shape[0]
    keep_ref[...] = both_ref[rows_at(bit, half), :]
    send_ref[...] = both_ref[rows_at(1 - bit, half), :]


def add_kernel(a_ref, b_ref, out_ref):
    out_ref[...] = a_ref[...] + b_ref[...]


def sum_z_kernel(own_ref, a_ref, b_ref, c_ref, out_ref, slots_ref):
    out_ref[...] = sum_in_order(slots_ref, lax.axis_index("z") // 2, (own_ref, a_ref, b_ref, c_ref))


def sum_z_after_kernel(own_ref, a_ref, b_ref, c_ref, *rest):
    sum_z_kernel(own_ref, a_ref, b_ref, c_ref, *rest[-2:])


def sum_x_kernel(own_ref, a_ref, b_ref, c_ref, out_ref, slots_ref):
    out_ref[...] = sum_in_order(slots_ref, lax.axis_index("x"), (own_ref, a_ref, b_ref, c_ref))


def join_z_kernel(own_ref, other_ref, out_ref):
    bit, half = lax.rem(lax.axis_index("z"), 2), own_ref.shape[0]
    out_ref[rows_at(bit, half), :] = own_ref[...]
    out_ref[rows_at(1 - bit, half), :] = other_ref[...]


def mixed_kernel(own_ref, a_ref, b_ref, c_ref, hidden_ref, err_ref, after_ref, p3_ref, all_ref, p_ref):
    for place, ref in in_order(lax.axis_index("y"), (own_ref, a_ref, b_ref, c_ref)):
        p_ref[rows_at(place, RANK // NY), :] = ref[...]
    p3 = split3(p_ref[...])
    p3_ref[...] = p3
    mixed = dot3(p3, hidden_ref[...], NT)
    all_ref[:RANK, :] = mixed[:, :EB]
    all_ref[RANK : 2 * RANK, :] = mixed[:, EB:]
    all_ref[2 * RANK : 3 * RANK, :] = dot3(p3, err_ref[...], NN)
    all_ref[3 * RANK :, :] = pack(gram3(p3))


def sum_x_kernel(own_ref, a_ref, b_ref, c_ref, out_ref, gram_ref, slots_ref):
    out_ref[...] = sum_in_order(slots_ref, lax.axis_index("x"), (own_ref, a_ref, b_ref, c_ref))
    gram_ref[...] = out_ref[3 * RANK :, :]


def right_kernel(mixed_ref, cot_ref, a_cot_ref, b_cot_ref, c_cot_ref, own_ref, a_ref, b_ref, c_ref, slots_ref, whole_ref):
    x, at = lax.axis_index("x"), lax.axis_index("y") * NZ + lax.axis_index("z")
    for place, ref in in_order(x, (cot_ref, a_cot_ref, b_cot_ref, c_cot_ref)):
        slots_ref[place] = ref[...]
    mixed = jnp.concatenate([mixed_ref[:RANK, :], mixed_ref[RANK : 2 * RANK, :]], axis=1)
    part = dot3(split3(mixed), slots_ref[...].reshape(TOK, CB), NN)
    err_q = mixed_ref[2 * RANK : 3 * RANK, :]
    here = [jnp.where(at == x * (CB // EB) + i, err_q, 0.0) for i in range(CB // EB)]
    whole_ref[...] = part + jnp.concatenate(here, axis=1)
    scatter(whole_ref, lax.axis_index("y"), (own_ref, a_ref, b_ref, c_ref))


def first_kernel(own_ref, other_ref, after_ref, inv_ref):
    inv_ref[...] = inverse_factor(unpack(jnp.where(lax.axis_index("c") == 1, own_ref[...], other_ref[...])))


def basis_kernel(inv_ref, p3_ref, b3_ref, gram_ref):
    b3 = split3(dot6(inv_ref[...], p3_ref[...]))
    b3_ref[...] = b3
    gram_ref[...] = pack(gram3(b3))


def sum_y_kernel(own_ref, a_ref, b_ref, c_ref, after_ref, out_ref, slots_ref):
    out_ref[...] = sum_in_order(slots_ref, lax.axis_index("y"), (own_ref, a_ref, b_ref, c_ref))


def add_after_kernel(a_ref, b_ref, after_ref, out_ref):
    out_ref[...] = a_ref[...] + b_ref[...]


def block_kernel(own_ref, a_ref, b_ref, c_ref, after_ref, out_ref):
    for place, ref in in_order(lax.axis_index("y"), (own_ref, a_ref, b_ref, c_ref)):
        out_ref[rows_at(place, RANK // NY), :] = ref[...]


def second_kernel(own_ref, a_ref, b_ref, c_ref, inverse_ref, slots_ref):
    gram = unpack(sum_in_order(slots_ref, lax.axis_index("x"), (own_ref, a_ref, b_ref, c_ref)))
    rows = lax.broadcasted_iota(jnp.int32, (RANK, RANK), 0)
    cols = lax.broadcasted_iota(jnp.int32, (RANK, RANK), 1)
    off = gram - jnp.where(rows == cols, 1.0, 0.0).astype(f32)
    here, near = lax.axis_index("c") == 0, jnp.max(jnp.abs(off)) < 1e-3

    @pl.when(jnp.logical_and(here, near))
    def _():
        inverse_ref[...] = near_inverse_factor(off)

    @pl.when(jnp.logical_and(here, jnp.logical_not(near)))
    def _():
        inverse_ref[...] = inverse_factor(gram)

    @pl.when(jnp.logical_not(here))
    def _():
        inverse_ref[...] = gram


def scaled_kernel(own_ref, other_ref, inv_ref, b3_ref, total_ref, out_ref):
    inverse = jnp.where(lax.axis_index("c") == 0, own_ref[...], other_ref[...])
    total_ref[...] = jnp.dot(inverse, inv_ref[...], precision=HIGHEST, preferred_element_type=f32) * (1.0 / N_DP)
    out_ref[...] = dot6(inverse * math.sqrt(FF), b3_ref[...])


def new_kernel(*refs):
    total_ref, out_ref, whole_ref, sems = refs[8:]
    x, core, total, copies = lax.axis_index("x"), lax.axis_index("c") == 1, total_ref[...], []
    for k in range(NX):
        cols = rows_at(lax.rem(x + NX - k, NX), CB)
        block = jnp.where(core, refs[k][...], refs[NX + k][...])
        whole_ref[k] = dot6(total, split3(block))
        copies.append(pltpu.make_async_copy(whole_ref.at[k], out_ref.at[:, cols], sems.at[k]))
        copies[k].start()
    for copy in copies:
        copy.wait()


def swap(a):
    return lax.ppermute(a, "c", [(0, 1), (1, 0)])


def hand_over(a, core):
    return lax.ppermute(a, "c", [(core, 1 - core)])


def swap_z(a, cores=(0, 1)):
    return lax.ppermute(a, ("z", "c"), [(i * NC + c, (i ^ 1) * NC + c) for i in range(NZ) for c in cores])


def shift(a, axis, k, cores=(0, 1)):
    size, step = {"y": (NY, 1), "z": (NZ, 2), "x": (NX, 1)}[axis]
    pairs = [(i * NC + c, (i + k * step) % size * NC + c) for i in range(size) for c in cores]
    return lax.ppermute(a, (axis, "c"), pairs)


def deal(blocks, axis, cores=(0, 1)):
    return [blocks[0]] + [shift(blocks[k], axis, k, cores) for k in (1, 2, 3)]


def share(block, axis, cores=(0, 1)):
    return deal([block] * 4, axis, cores)


def shards(hidden, cotangent, error_buf, q_start):
    dma = pltpu.SemaphoreType.DMA
    pinned = [pltpu.with_memory_space_constraint(a, pltpu.HBM) for a in (cotangent, q_start.T, hidden, error_buf)]
    proj, cot, hid, err, q_own = call(
        project_kernel,
        [((TB, 4 * RANK), bf16), ((TB, D), bf16), ((TOK, FB), bf16), ((FB, EB), bf16), ((RANK, EB), f32)], *pinned,
        scratch=[pltpu.VMEM((RANK, D), f32), dma((8,))], hbm=(0, 1, 2, 3),
    )
    proj = call(join_c_kernel, ((2 * TB, 4 * RANK), bf16), proj, swap(proj))
    quarter, eighth = ((RANK // NY, FB), f32), ((RANK // NY // 2, FB), f32)
    parts = call(
        left_kernel, [quarter] * 4, *share(proj, "x"), hid, err, q_own,
        scratch=[pltpu.VMEM((4, 2 * TB, 4 * RANK), bf16), pltpu.VMEM((RANK, FB), f32)],
    )

    keep, send, cot = call(
        halve_kernel, [eighth, eighth, ((TB, D), bf16)], *deal(parts, "y"), cot,
        scratch=[pltpu.VMEM((4, *quarter[0]), f32), pltpu.VMEM(*quarter)],
    )
    cot_other, block = hand_over(cot, 0), ((2 * TB, CB), bf16)
    p = call(add_kernel, eighth, keep, swap_z(send))
    cot1, cot2 = call(functools.partial(columns_kernel, (1, 2)), [block] * 2, cot, cot_other, p, unread=(2,))
    cot1, cot2 = shift(cot1, "x", 1, (1,)), shift(cot2, "x", 2, (1,))
    p = call(
        sum_z_after_kernel, eighth, *share(p, "z"), cot1, cot2, scratch=[pltpu.VMEM((4, *eighth[0]), f32)], unread=(4, 5)
    )
    cot0, cot3 = call(functools.partial(columns_kernel, (0, 3)), [block] * 2, cot, cot_other, p, unread=(2,))
    cot = (cot0, cot1, cot2, shift(cot3, "x", 3, (1,)))
    p = call(join_z_kernel, quarter, p, swap_z(p))

    mix, small = ((3 * RANK + RANK // 2, EB), f32), ((RANK // 2, 2 * RANK), f32)
    p3, mixed = call(
        mixed_kernel, [((3 * RANK, FB), bf16), mix], *share(p, "y"), hid, err, cot[3], scratch=[pltpu.VMEM((RANK, FB), f32)], unread=(6,)
    )
    mixed = call(add_kernel, mix, mixed, hand_over(mixed, 0))
    mixed, gram = call(sum_x_kernel, [mix, small], *share(mixed, "x", (1,)), scratch=[pltpu.VMEM((4, *mix[0]), f32)])

    piece, slots = ((RANK // NY, CB), f32), pltpu.VMEM((4, RANK // NY, CB), f32)
    parts = call(
        right_kernel, [piece] * 4, mixed, *cot, scratch=[pltpu.VMEM((4, 2 * TB, CB), bf16), pltpu.VMEM((RANK, CB), f32)]
    )
    inverse = call(first_kernel, ((RANK, RANK), f32), gram, hand_over(gram, 1), parts[0], unread=(2,))
    s = call(sum_y_kernel, piece, *deal(parts, "y", (1,)), inverse, scratch=[slots], unread=(4,))
    b3, gram = call(basis_kernel, [((3 * RANK, FB), bf16), small], inverse, p3)
    s = call(add_after_kernel, piece, s, swap_z(s, (1,)), gram, unread=(2,))
    gram = call(add_kernel, small, gram, hand_over(gram, 1))
    second = call(second_kernel, ((RANK, RANK), f32), *share(gram, "x", (0,)), scratch=[pltpu.VMEM((4, *small[0]), f32)])
    total, scaled = call(scaled_kernel, [((RANK, RANK), f32), ((RANK, FB), f32)], second, hand_over(second, 0), inverse, b3)
    s = call(sum_z_after_kernel, piece, *share(s, "z", (1,)), gram, scratch=[slots], unread=(4,))
    s = call(block_kernel, ((RANK, CB), f32), *share(s, "y", (1,)), total, unread=(4,))
    blocks = share(s, "x", (1,))
    q_new = call(
        new_kernel, ((RANK, D), f32), *blocks, *[hand_over(b, 1) for b in blocks], total,
        scratch=[pltpu.VMEM((NX, RANK, CB), f32), dma((NX,))], out_hbm=True,
    )
    return scaled.T, q_new.T


def solution(mesh):
    fine = Mesh(mesh.devices.reshape(NY, NZ, NX, NC), ("y", "z", "x", "c"))
    dp, tensor = ("y", "z"), ("x", "c")
    placed = (P(dp, tensor), P(dp + tensor, None), P(tensor, dp), P())
    return jax.shard_map(
        shards, mesh=fine, in_specs=placed, out_specs=(P(tensor, None), P()), check_vma=False
    )
```

```python
import functools
import math

import jax
import jax.numpy as jnp
from jax import lax
from jax.experimental import pallas as pl
from jax.experimental.pallas import tpu as pltpu
from jax.sharding import Mesh
from jax.sharding import PartitionSpec as P

FF = 14336
D = 4096
RANK = 64
N_DP = 32
TOK = 256
NY, NZ, NX, NC = 4, 8, 4, 2
FB = FF // (NX * NC)
CB = D // NX
EB = D // N_DP
TB = TOK // (NX * NC)
f32, bf16 = jnp.float32, jnp.bfloat16
HIGHEST = lax.Precision.HIGHEST
NN = (((1,), (0,)), ((), ()))
NT = (((1,), (1,)), ((), ()))
TN = (((0,), (0,)), ((), ()))


def split3(a):
    hi = a.astype(bf16)
    rest = a - hi.astype(f32)
    mid = rest.astype(bf16)
    low = (rest - mid.astype(f32)).astype(bf16)
    return jnp.concatenate([hi, mid, low], axis=0)


def add3(a):
    n = a.shape[0] // 3
    return a[:n] + (a[n : 2 * n] + a[2 * n :])


def dot3(a, b, dims):
    return add3(lax.dot_general(a, b, dims, preferred_element_type=f32))


def gram3(a3):
    g = lax.dot_general(a3, a3, NT, preferred_element_type=f32)
    r = RANK
    g00, g01, g02 = g[:r, :r], g[:r, r : 2 * r], g[:r, 2 * r :]
    g10, g11, g20 = g[r : 2 * r, :r], g[r : 2 * r, r : 2 * r], g[2 * r :, :r]
    return g00 + ((g01 + g10) + (g11 + (g02 + g20)))


def wide(column):
    return jnp.broadcast_to(column, (8, 2 * RANK))


def inverse_factor(gram):
    rows = lax.broadcasted_iota(jnp.int32, (RANK, RANK), 0)
    cols = lax.broadcasted_iota(jnp.int32, (RANK, RANK), 1)
    both = jnp.concatenate([gram, jnp.where(rows == cols, 1.0, 0.0).astype(f32)], axis=1)
    sub = lax.broadcasted_iota(jnp.int32, (8, 2 * RANK), 0)
    count = RANK // 8
    tiles = [both[8 * i : 8 * i + 8] for i in range(count)]
    for p in range(count):
        columns = [[wide(tiles[i][:, 8 * p + j : 8 * p + j + 1]) for j in range(8)] for i in range(p, count)]
        panel, own, pivots, scales = tiles[p], columns[0], jnp.ones((8, 2 * RANK), f32), []
        for s in range(8):
            pivot = own[s][s : s + 1]
            scales.append(1.0 / pivot)
            pivots = jnp.where(sub == s, pivot, pivots)
            factor = jnp.where(sub > s, own[s] * scales[s], 0.0)
            panel = panel - factor * panel[s : s + 1]
            for j in range(s + 1, 8):
                own[j] = own[j] - factor * own[j][s : s + 1]
        for i in range(p + 1, count):
            below, tile = columns[i - p], tiles[i]
            for s in range(8):
                factor = below[s] * scales[s]
                tile = tile - factor * panel[s : s + 1]
                for j in range(s + 1, 8):
                    below[j] = below[j] - factor * own[j][s : s + 1]
            tiles[i] = tile
        tiles[p] = panel * lax.rsqrt(pivots)
    return jnp.concatenate(tiles, axis=0)[:, RANK:]


def near_inverse_factor(off):
    rows = lax.broadcasted_iota(jnp.int32, (RANK, RANK), 0)
    cols = lax.broadcasted_iota(jnp.int32, (RANK, RANK), 1)
    lower = jnp.where(rows > cols, 1.0, jnp.where(rows == cols, 0.5, 0.0)).astype(f32)
    first = off * lower
    second = -lower * lax.dot_general(first, first, NT, precision=HIGHEST, preferred_element_type=f32)
    square = jnp.dot(first, first, precision=HIGHEST, preferred_element_type=f32)
    eye = jnp.where(rows == cols, 1.0, 0.0).astype(f32)
    return eye - first + (square - second)


def dot6(a, b3):
    hi = a.astype(bf16).astype(f32)
    mid = (a - hi).astype(bf16).astype(f32)
    low = a - hi - mid
    one = jnp.concatenate([hi, hi, hi, mid], axis=1).astype(bf16)
    two = jnp.concatenate([mid, low], axis=1).astype(bf16)
    high, middle = b3[:RANK], b3[RANK : 2 * RANK]
    out = jnp.dot(one, jnp.concatenate([b3, high], axis=0), preferred_element_type=f32)
    return out + jnp.dot(two, jnp.concatenate([middle, high], axis=0), preferred_element_type=f32)


def pack(square):
    return jnp.concatenate([square[: RANK // 2], square[RANK // 2 :]], axis=1)


def unpack(packed):
    return jnp.concatenate([packed[:, :RANK], packed[:, RANK:]], axis=0)


def call(kernel, out_shape, *args, scratch=(), hbm=(), unread=(), out_hbm=False):
    vmem, far, anywhere = (pl.BlockSpec(memory_space=m) for m in (pltpu.VMEM, pltpu.HBM, pl.ANY))
    many = isinstance(out_shape, list)
    shapes = [jax.ShapeDtypeStruct(*s) for s in (out_shape if many else [out_shape])]
    return pl.pallas_call(
        kernel,
        out_shape=shapes if many else shapes[0],
        in_specs=[far if i in hbm else anywhere if i in unread else vmem for i in range(len(args))],
        out_specs=[vmem] * len(shapes) if many else far if out_hbm else vmem,
        scratch_shapes=list(scratch),
        compiler_params=pltpu.CompilerParams(vmem_limit_bytes=32 * 1024 * 1024),
    )(*args)


def rows_at(index, size):
    return pl.ds(pl.multiple_of(index * size, size), size)


def in_order(index, refs):
    for k, ref in enumerate(refs):
        yield lax.rem(index + 4 - k, 4), ref


def sum_in_order(slots_ref, index, refs):
    for place, ref in in_order(index, refs):
        slots_ref[place] = ref[...]
    return (slots_ref[0] + slots_ref[1]) + (slots_ref[2] + slots_ref[3])


def scatter(whole_ref, index, refs):
    size = whole_ref.shape[0] // 4
    for k, ref in enumerate(refs):
        ref[...] = whole_ref[rows_at(lax.rem(index + k, 4), size), :]


def project_kernel(cot_ref, qt_ref, out_ref, c_ref, own_ref, qt, sems):
    at, cut, parts = lax.axis_index("y") * NZ + lax.axis_index("z"), 1024, []
    pairs = [(cot_ref, c_ref)]
    pairs += [(qt_ref.at[:, i : i + cut], qt.at[:, i : i + cut]) for i in range(0, D, cut)]
    pairs += [(qt_ref.at[:, rows_at(at, EB)], own_ref)]
    copies = [pltpu.make_async_copy(a, b, sems.at[i]) for i, (a, b) in enumerate(pairs)]
    for copy in copies:
        copy.start()
    copies[0].wait()
    for i in range(D // cut):
        copies[1 + i].wait()
        cols = slice(i * cut, (i + 1) * cut)
        parts.append(lax.dot_general(c_ref[:, cols], split3(qt[:, cols]), NT, preferred_element_type=f32))
    got = (parts[0] + parts[1]) + (parts[2] + parts[3])
    pieces = split3(got[:, :RANK] + (got[:, RANK : 2 * RANK] + got[:, 2 * RANK :]))
    pieces = [pieces[i * TB : (i + 1) * TB] for i in range(3)]
    out_ref[...] = jnp.concatenate(pieces + [jnp.zeros((TB, RANK), bf16)], axis=1)
    copies[1 + D // cut].wait()


def fetch_kernel(hidden_ref, err_ref, after_ref, h_ref, e_ref, sems):
    copies = [pltpu.make_async_copy(a, b, sems.at[i]) for i, (a, b) in enumerate(((hidden_ref, h_ref), (err_ref, e_ref)))]
    for copy in copies:
        copy.start()
    for copy in copies:
        copy.wait()


def join_c_kernel(own_ref, other_ref, out_ref):
    c, half = lax.axis_index("c"), own_ref.shape[0]
    out_ref[rows_at(c, half), :] = own_ref[...]
    out_ref[rows_at(1 - c, half), :] = other_ref[...]


def columns_kernel(own_ref, other_ref, after_ref, *out_refs):
    x, c = lax.axis_index("x"), lax.axis_index("c")
    for k, ref in enumerate(out_refs):
        cols = rows_at(lax.rem(x + k, NX), CB)
        ref[rows_at(c, TB), :] = own_ref[:, cols]
        ref[rows_at(1 - c, TB), :] = other_ref[:, cols]


def left_kernel(
    got_ref, a_got_ref, b_got_ref, c_got_ref, hidden_ref, err_ref, q_ref, cot_ref,
    own_ref, a_ref, b_ref, c_ref, pass_ref, slots_ref, whole_ref,
):
    for place, ref in in_order(lax.axis_index("x"), (got_ref, a_got_ref, b_got_ref, c_got_ref)):
        slots_ref[place] = ref[...]
    pass_ref[...] = cot_ref[...]
    proj = slots_ref[...].reshape(TOK, 4 * RANK)
    part = lax.dot_general(proj, hidden_ref[...], TN, preferred_element_type=f32)
    whole_ref[...] = add3(part[: 3 * RANK]) + dot3(split3(q_ref[...]), err_ref[...], NT)
    scatter(whole_ref, lax.axis_index("y"), (own_ref, a_ref, b_ref, c_ref))


def halve_kernel(own_ref, a_ref, b_ref, c_ref, after_ref, keep_ref, send_ref, slots_ref, both_ref):
    both_ref[...] = sum_in_order(slots_ref, lax.axis_index("y"), (own_ref, a_ref, b_ref, c_ref))
    bit, half = lax.rem(lax.axis_index("z"), 2), keep_ref.shape[0]
    keep_ref[...] = both_ref[rows_at(bit, half), :]
    send_ref[...] = both_ref[rows_at(1 - bit, half), :]


def add_kernel(a_ref, b_ref, out_ref):
    out_ref[...] = a_ref[...] + b_ref[...]


def sum_z_kernel(own_ref, a_ref, b_ref, c_ref, out_ref, slots_ref):
    out_ref[...] = sum_in_order(slots_ref, lax.axis_index("z") // 2, (own_ref, a_ref, b_ref, c_ref))


def sum_z_after_kernel(own_ref, a_ref, b_ref, c_ref, *rest):
    sum_z_kernel(own_ref, a_ref, b_ref, c_ref, *rest[-2:])


def sum_x_kernel(own_ref, a_ref, b_ref, c_ref, out_ref, slots_ref):
    out_ref[...] = sum_in_order(slots_ref, lax.axis_index("x"), (own_ref, a_ref, b_ref, c_ref))


def join_z_kernel(own_ref, other_ref, out_ref):
    bit, half = lax.rem(lax.axis_index("z"), 2), own_ref.shape[0]
    out_ref[rows_at(bit, half), :] = own_ref[...]
    out_ref[rows_at(1 - bit, half), :] = other_ref[...]


def mixed_kernel(own_ref, a_ref, b_ref, c_ref, hidden_ref, err_ref, after_ref, p3_ref, keep_ref, send_ref, p_ref, all_ref):
    for place, ref in in_order(lax.axis_index("y"), (own_ref, a_ref, b_ref, c_ref)):
        p_ref[rows_at(place, RANK // NY), :] = ref[...]
    p3 = split3(p_ref[...])
    p3_ref[...] = p3
    all_ref[:, :TOK] = dot3(p3, hidden_ref[...], NT)
    all_ref[:, TOK:] = dot3(p3, err_ref[...], NN)
    gram = pack(gram3(p3))
    c, half = lax.axis_index("c"), RANK // 2
    for ref, core in ((keep_ref, c), (send_ref, 1 - c)):
        ref[:, : TOK + EB] = all_ref[rows_at(core, half), :]
        ref[:, TOK + EB :] = gram


def right_kernel(mixed_ref, cot_ref, a_cot_ref, b_cot_ref, c_cot_ref, own_ref, a_ref, b_ref, c_ref, slots_ref, whole_ref):
    x, at = lax.axis_index("x"), lax.axis_index("y") * NZ + lax.axis_index("z")
    for place, ref in in_order(x, (cot_ref, a_cot_ref, b_cot_ref, c_cot_ref)):
        slots_ref[place] = ref[...]
    part = dot3(split3(mixed_ref[:, :TOK]), slots_ref[...].reshape(TOK, CB), NN)
    err_q = mixed_ref[:, TOK : TOK + EB]
    here = [jnp.where(at == x * (CB // EB) + i, err_q, 0.0) for i in range(CB // EB)]
    whole_ref[...] = part + jnp.concatenate(here, axis=1)
    scatter(whole_ref, lax.axis_index("y"), (own_ref, a_ref, b_ref, c_ref))


def first_kernel(mixed_ref, after_ref, inv_ref):
    inv_ref[...] = inverse_factor(unpack(mixed_ref[:, TOK + EB :]))


def basis_kernel(inv_ref, p3_ref, b3_ref, gram_ref):
    b3 = split3(dot6(inv_ref[...], p3_ref[...]))
    b3_ref[...] = b3
    gram_ref[...] = pack(gram3(b3))


def sum_y_kernel(own_ref, a_ref, b_ref, c_ref, after_ref, out_ref, slots_ref):
    out_ref[...] = sum_in_order(slots_ref, lax.axis_index("y"), (own_ref, a_ref, b_ref, c_ref))


def add_after_kernel(a_ref, b_ref, after_ref, out_ref):
    out_ref[...] = a_ref[...] + b_ref[...]


def block_kernel(own_ref, a_ref, b_ref, c_ref, gram_ref, other_ref, out_ref):
    for place, ref in in_order(lax.axis_index("y"), (own_ref, a_ref, b_ref, c_ref)):
        out_ref[rows_at(place, RANK // 2 // NY), :CB] = ref[...]
    out_ref[:, CB:] = gram_ref[...] + other_ref[...]


def second_kernel(own_ref, a_ref, b_ref, c_ref, b3_ref, inv_ref, out_ref, total_ref, slots_ref, inverse_ref):
    for place, ref in in_order(lax.axis_index("x"), (own_ref, a_ref, b_ref, c_ref)):
        slots_ref[place] = ref[:, CB:]
    gram = unpack((slots_ref[0] + slots_ref[1]) + (slots_ref[2] + slots_ref[3]))
    rows = lax.broadcasted_iota(jnp.int32, (RANK, RANK), 0)
    cols = lax.broadcasted_iota(jnp.int32, (RANK, RANK), 1)
    off = gram - jnp.where(rows == cols, 1.0, 0.0).astype(f32)
    near = jnp.max(jnp.abs(off)) < 1e-3

    @pl.when(near)
    def _():
        inverse_ref[...] = near_inverse_factor(off)

    @pl.when(jnp.logical_not(near))
    def _():
        inverse_ref[...] = inverse_factor(gram)

    inverse = inverse_ref[...]
    total_ref[...] = jnp.dot(inverse, inv_ref[...], precision=HIGHEST, preferred_element_type=f32) * (1.0 / N_DP)
    out_ref[...] = dot6(inverse * math.sqrt(FF), b3_ref[...])


def new_kernel(*refs):
    total_ref, out_ref, s_ref, whole_ref, sems = refs[8:]
    x, c, half, total, copies = lax.axis_index("x"), lax.axis_index("c"), RANK // 2, total_ref[...], []
    for k in range(NX):
        s_ref[k, rows_at(c, half), :] = refs[k][:, :CB]
        s_ref[k, rows_at(1 - c, half), :] = refs[NX + k][:, :CB]
        whole_ref[k] = dot6(total, split3(s_ref[k]))
        cols = rows_at(lax.rem(x + NX - k, NX), CB)
        copies.append(pltpu.make_async_copy(whole_ref.at[k], out_ref.at[:, cols], sems.at[k]))
        copies[k].start()
    for copy in copies:
        copy.wait()


def swap(a):
    return lax.ppermute(a, "c", [(0, 1), (1, 0)])


def swap_z(a):
    return lax.ppermute(a, "z", [(i, i ^ 1) for i in range(NZ)])


def shift(a, axis, k):
    size, step = {"y": (NY, 1), "z": (NZ, 2), "x": (NX, 1)}[axis]
    return lax.ppermute(a, axis, [(i, (i + k * step) % size) for i in range(size)])


def deal(blocks, axis):
    return [blocks[0]] + [shift(blocks[k], axis, k) for k in (1, 2, 3)]


def share(block, axis):
    return deal([block] * 4, axis)


def shards(hidden, cotangent, error_buf, q_start):
    qt = q_start.T
    dma, half = pltpu.SemaphoreType.DMA, RANK // 2
    cot, qt, hid, err = (pltpu.with_memory_space_constraint(a, pltpu.HBM) for a in (cotangent, q_start.T, hidden, error_buf))
    proj, cot, q_own = call(
        project_kernel, [((TB, 4 * RANK), bf16), ((TB, D), bf16), ((RANK, EB), f32)], cot, qt,
        scratch=[pltpu.VMEM((RANK, D), f32), dma((6,))], hbm=(0, 1),
    )
    hid, err = call(
        fetch_kernel, [((TOK, FB), bf16), ((FB, EB), bf16)], hid, err, proj, scratch=[dma((2,))], hbm=(0, 1), unread=(2,)
    )
    proj = call(join_c_kernel, ((2 * TB, 4 * RANK), bf16), proj, swap(proj))
    quarter, eighth = ((RANK // NY, FB), f32), ((RANK // NY // 2, FB), f32)
    *parts, cot = call(
        left_kernel, [quarter] * 4 + [((TB, D), bf16)], *share(proj, "x"), hid, err, q_own, cot,
        scratch=[pltpu.VMEM((4, 2 * TB, 4 * RANK), bf16), pltpu.VMEM((RANK, FB), f32)],
    )

    parts = deal(parts, "y")
    blocks = call(columns_kernel, [((2 * TB, CB), bf16)] * NX, cot, swap(cot), parts[1], unread=(2,))
    cot = deal(blocks, "x")
    keep, send = call(
        halve_kernel, [eighth, eighth], *parts, cot[0], scratch=[pltpu.VMEM((4, *quarter[0]), f32), pltpu.VMEM(*quarter)], unread=(4,)
    )
    p = call(add_kernel, eighth, keep, swap_z(send))
    p = call(
        sum_z_after_kernel, eighth, *share(p, "z"), cot[1], cot[3], scratch=[pltpu.VMEM((4, *eighth[0]), f32)], unread=(4, 5)
    )
    p = call(join_z_kernel, quarter, p, swap_z(p))

    halves = ((half, TOK + EB + 2 * RANK), f32)
    p3, keep, send = call(
        mixed_kernel, [((3 * RANK, FB), bf16), halves, halves], *share(p, "y"), hid, err, cot[2],
        scratch=[pltpu.VMEM((RANK, FB), f32), pltpu.VMEM((RANK, TOK + EB), f32)], unread=(6,),
    )
    mixed = call(add_kernel, halves, keep, swap(send))
    mixed = call(sum_x_kernel, halves, *share(mixed, "x"), scratch=[pltpu.VMEM((4, *halves[0]), f32)])

    piece = ((half // NY, CB), f32)
    parts = call(
        right_kernel, [piece] * 4, mixed, *cot, scratch=[pltpu.VMEM((4, 2 * TB, CB), bf16), pltpu.VMEM((half, CB), f32)]
    )
    inverse = call(first_kernel, ((RANK, RANK), f32), mixed, parts[0], unread=(1,))
    s = call(sum_y_kernel, piece, *deal(parts, "y"), inverse, scratch=[pltpu.VMEM((4, *piece[0]), f32)], unread=(4,))
    b3, gram = call(basis_kernel, [((3 * RANK, FB), bf16), ((half, 2 * RANK), f32)], inverse, p3)
    s = call(add_after_kernel, piece, s, swap_z(s), gram, unread=(2,))
    s = call(sum_z_kernel, piece, *share(s, "z"), scratch=[pltpu.VMEM((4, *piece[0]), f32)])
    s = call(block_kernel, ((half, CB + 2 * RANK), f32), *share(s, "y"), gram, swap(gram))
    blocks = share(s, "x")
    scaled, total = call(
        second_kernel, [((RANK, FB), f32), ((RANK, RANK), f32)], *blocks, b3, inverse,
        scratch=[pltpu.VMEM((4, half, 2 * RANK), f32), pltpu.VMEM((RANK, RANK), f32)],
    )
    q_new = call(
        new_kernel, ((RANK, D), f32), *blocks, *[swap(b) for b in blocks], total,
        scratch=[pltpu.VMEM((NX, RANK, CB), f32), pltpu.VMEM((NX, RANK, CB), f32), dma((NX,))], out_hbm=True,
    )
    return scaled.T, q_new.T


def solution(mesh):
    fine = Mesh(mesh.devices.reshape(NY, NZ, NX, NC), ("y", "z", "x", "c"))
    dp, tensor = ("y", "z"), ("x", "c")
    placed = (P(dp, tensor), P(dp + tensor, None), P(tensor, dp), P())
    return jax.shard_map(
        shards, mesh=fine, in_specs=placed, out_specs=(P(tensor, None), P()), check_vma=False
    )
```

```python
import functools
import math

import jax
import jax.numpy as jnp
from jax import lax
from jax.experimental import pallas as pl
from jax.experimental.pallas import tpu as pltpu
from jax.sharding import Mesh
from jax.sharding import PartitionSpec as P

FF = 14336
D = 4096
RANK = 64
N_DP = 32
TOK = 256
NY, NZ, NX, NC = 4, 8, 4, 2
FB = FF // (NX * NC)
CB = D // NX
EB = D // N_DP
TB = TOK // (NX * NC)
f32, bf16 = jnp.float32, jnp.bfloat16
HIGHEST = lax.Precision.HIGHEST
NN = (((1,), (0,)), ((), ()))
NT = (((1,), (1,)), ((), ()))
TN = (((0,), (0,)), ((), ()))


def split3(a):
    hi = a.astype(bf16)
    rest = a - hi.astype(f32)
    mid = rest.astype(bf16)
    low = (rest - mid.astype(f32)).astype(bf16)
    return jnp.concatenate([hi, mid, low], axis=0)


def add3(a):
    n = a.shape[0] // 3
    return a[:n] + (a[n : 2 * n] + a[2 * n :])


def dot3(a, b, dims):
    return add3(lax.dot_general(a, b, dims, preferred_element_type=f32))


def gram3(a3):
    g = lax.dot_general(a3, a3, NT, preferred_element_type=f32)
    r = RANK
    g00, g01, g02 = g[:r, :r], g[:r, r : 2 * r], g[:r, 2 * r :]
    g10, g11, g20 = g[r : 2 * r, :r], g[r : 2 * r, r : 2 * r], g[2 * r :, :r]
    return g00 + ((g01 + g10) + (g11 + (g02 + g20)))


def wide(column):
    return jnp.broadcast_to(column, (8, 2 * RANK))


def inverse_factor(gram):
    rows = lax.broadcasted_iota(jnp.int32, (RANK, RANK), 0)
    cols = lax.broadcasted_iota(jnp.int32, (RANK, RANK), 1)
    both = jnp.concatenate([gram, jnp.where(rows == cols, 1.0, 0.0).astype(f32)], axis=1)
    sub = lax.broadcasted_iota(jnp.int32, (8, 2 * RANK), 0)
    count = RANK // 8
    tiles = [both[8 * i : 8 * i + 8] for i in range(count)]
    for p in range(count):
        columns = [[wide(tiles[i][:, 8 * p + j : 8 * p + j + 1]) for j in range(8)] for i in range(p, count)]
        panel, own, pivots, scales = tiles[p], columns[0], jnp.ones((8, 2 * RANK), f32), []
        for s in range(8):
            pivot = own[s][s : s + 1]
            scales.append(1.0 / pivot)
            pivots = jnp.where(sub == s, pivot, pivots)
            factor = jnp.where(sub > s, own[s] * scales[s], 0.0)
            panel = panel - factor * panel[s : s + 1]
            for j in range(s + 1, 8):
                own[j] = own[j] - factor * own[j][s : s + 1]
        for i in range(p + 1, count):
            below, tile = columns[i - p], tiles[i]
            for s in range(8):
                factor = below[s] * scales[s]
                tile = tile - factor * panel[s : s + 1]
                for j in range(s + 1, 8):
                    below[j] = below[j] - factor * own[j][s : s + 1]
            tiles[i] = tile
        tiles[p] = panel * lax.rsqrt(pivots)
    return jnp.concatenate(tiles, axis=0)[:, RANK:]


def near_inverse_factor(off):
    rows = lax.broadcasted_iota(jnp.int32, (RANK, RANK), 0)
    cols = lax.broadcasted_iota(jnp.int32, (RANK, RANK), 1)
    lower = jnp.where(rows > cols, 1.0, jnp.where(rows == cols, 0.5, 0.0)).astype(f32)
    first = off * lower
    second = -lower * lax.dot_general(first, first, NT, precision=HIGHEST, preferred_element_type=f32)
    square = jnp.dot(first, first, precision=HIGHEST, preferred_element_type=f32)
    eye = jnp.where(rows == cols, 1.0, 0.0).astype(f32)
    return eye - first + (square - second)


def dot6(a, b3):
    hi = a.astype(bf16).astype(f32)
    mid = (a - hi).astype(bf16).astype(f32)
    low = a - hi - mid
    one = jnp.concatenate([hi, hi, hi, mid], axis=1).astype(bf16)
    two = jnp.concatenate([mid, low], axis=1).astype(bf16)
    high, middle = b3[:RANK], b3[RANK : 2 * RANK]
    out = jnp.dot(one, jnp.concatenate([b3, high], axis=0), preferred_element_type=f32)
    return out + jnp.dot(two, jnp.concatenate([middle, high], axis=0), preferred_element_type=f32)


def pack(square):
    return jnp.concatenate([square[: RANK // 2], square[RANK // 2 :]], axis=1)


def unpack(packed):
    return jnp.concatenate([packed[:, :RANK], packed[:, RANK:]], axis=0)


def call(kernel, out_shape, *args, scratch=(), hbm=(), unread=(), out_hbm=False):
    vmem, far, anywhere = (pl.BlockSpec(memory_space=m) for m in (pltpu.VMEM, pltpu.HBM, pl.ANY))
    many = isinstance(out_shape, list)
    shapes = [jax.ShapeDtypeStruct(*s) for s in (out_shape if many else [out_shape])]
    return pl.pallas_call(
        kernel,
        out_shape=shapes if many else shapes[0],
        in_specs=[far if i in hbm else anywhere if i in unread else vmem for i in range(len(args))],
        out_specs=[vmem] * len(shapes) if many else far if out_hbm else vmem,
        scratch_shapes=list(scratch),
        compiler_params=pltpu.CompilerParams(vmem_limit_bytes=32 * 1024 * 1024),
    )(*args)


DEALT = (0, 2, 1, 3)


def rows_at(index, size):
    return pl.ds(pl.multiple_of(index * size, size), size)


def in_order(index, refs, ks=(0, 1, 3, 2)):
    for k, ref in zip(ks, refs, strict=True):
        yield lax.rem(index + 4 - k, 4), ref


def sum_in_order(slots_ref, index, refs, ks=(0, 1, 3, 2)):
    for place, ref in in_order(index, refs, ks):
        slots_ref[place] = ref[...]
    return (slots_ref[0] + slots_ref[1]) + (slots_ref[2] + slots_ref[3])


def scatter(whole_ref, index, refs):
    size = whole_ref.shape[0] // 4
    for k, ref in zip(DEALT, refs, strict=True):
        ref[...] = whole_ref[rows_at(lax.rem(index + k, 4), size), :]


def project_kernel(cot_ref, qt_ref, out_ref, c_ref, own_ref, qt, sems):
    at, cut, parts = lax.axis_index("y") * NZ + lax.axis_index("z"), 1024, []
    pairs = [(cot_ref, c_ref)]
    pairs += [(qt_ref.at[:, i : i + cut], qt.at[:, i : i + cut]) for i in range(0, D, cut)]
    pairs += [(qt_ref.at[:, rows_at(at, EB)], own_ref)]
    copies = [pltpu.make_async_copy(a, b, sems.at[i]) for i, (a, b) in enumerate(pairs)]
    for copy in copies:
        copy.start()
    copies[0].wait()
    for i in range(D // cut):
        copies[1 + i].wait()
        cols = slice(i * cut, (i + 1) * cut)
        parts.append(lax.dot_general(c_ref[:, cols], split3(qt[:, cols]), NT, preferred_element_type=f32))
    got = (parts[0] + parts[1]) + (parts[2] + parts[3])
    pieces = split3(got[:, :RANK] + (got[:, RANK : 2 * RANK] + got[:, 2 * RANK :]))
    pieces = [pieces[i * TB : (i + 1) * TB] for i in range(3)]
    out_ref[...] = jnp.concatenate(pieces + [jnp.zeros((TB, RANK), bf16)], axis=1)
    copies[1 + D // cut].wait()


def fetch_kernel(hidden_ref, err_ref, after_ref, h_ref, e_ref, sems):
    copies = [pltpu.make_async_copy(a, b, sems.at[i]) for i, (a, b) in enumerate(((hidden_ref, h_ref), (err_ref, e_ref)))]
    for copy in copies:
        copy.start()
    for copy in copies:
        copy.wait()


def join_c_kernel(own_ref, other_ref, out_ref):
    c, half = lax.axis_index("c"), own_ref.shape[0]
    out_ref[rows_at(c, half), :] = own_ref[...]
    out_ref[rows_at(1 - c, half), :] = other_ref[...]


def columns_kernel(own_ref, other_ref, after_ref, *out_refs):
    x, c = lax.axis_index("x"), lax.axis_index("c")
    for k, ref in zip(DEALT, out_refs, strict=True):
        cols = rows_at(lax.rem(x + k, NX), CB)
        ref[rows_at(c, TB), :] = own_ref[:, cols]
        ref[rows_at(1 - c, TB), :] = other_ref[:, cols]


def left_kernel(
    got_ref, a_got_ref, b_got_ref, c_got_ref, hidden_ref, err_ref, q_ref, cot_ref,
    own_ref, a_ref, b_ref, c_ref, pass_ref, slots_ref, whole_ref,
):
    for place, ref in in_order(lax.axis_index("x"), (got_ref, a_got_ref, b_got_ref, c_got_ref)):
        slots_ref[place] = ref[...]
    pass_ref[...] = cot_ref[...]
    proj = slots_ref[...].reshape(TOK, 4 * RANK)
    part = lax.dot_general(proj, hidden_ref[...], TN, preferred_element_type=f32)
    whole_ref[...] = add3(part[: 3 * RANK]) + dot3(split3(q_ref[...]), err_ref[...], NT)
    scatter(whole_ref, lax.axis_index("y"), (own_ref, a_ref, b_ref, c_ref))


def halve_kernel(own_ref, a_ref, b_ref, c_ref, after_ref, keep_ref, send_ref, slots_ref, both_ref):
    both_ref[...] = sum_in_order(slots_ref, lax.axis_index("y"), (own_ref, a_ref, b_ref, c_ref), DEALT)
    bit, half = lax.rem(lax.axis_index("z"), 2), keep_ref.shape[0]
    keep_ref[...] = both_ref[rows_at(bit, half), :]
    send_ref[...] = both_ref[rows_at(1 - bit, half), :]


def add_kernel(a_ref, b_ref, out_ref):
    out_ref[...] = a_ref[...] + b_ref[...]


def sum_z_kernel(own_ref, a_ref, b_ref, c_ref, out_ref, slots_ref):
    out_ref[...] = sum_in_order(slots_ref, lax.axis_index("z") // 2, (own_ref, a_ref, b_ref, c_ref))


def sum_z_after_kernel(own_ref, a_ref, b_ref, c_ref, *rest):
    sum_z_kernel(own_ref, a_ref, b_ref, c_ref, *rest[-2:])


def sum_x_kernel(own_ref, a_ref, b_ref, c_ref, out_ref, slots_ref):
    out_ref[...] = sum_in_order(slots_ref, lax.axis_index("x"), (own_ref, a_ref, b_ref, c_ref))


def join_z_kernel(own_ref, other_ref, out_ref):
    bit, half = lax.rem(lax.axis_index("z"), 2), own_ref.shape[0]
    out_ref[rows_at(bit, half), :] = own_ref[...]
    out_ref[rows_at(1 - bit, half), :] = other_ref[...]


def mixed_kernel(own_ref, a_ref, b_ref, c_ref, hidden_ref, err_ref, after_ref, p3_ref, keep_ref, send_ref, p_ref, all_ref):
    for place, ref in in_order(lax.axis_index("y"), (own_ref, a_ref, b_ref, c_ref)):
        p_ref[rows_at(place, RANK // NY), :] = ref[...]
    p3 = split3(p_ref[...])
    p3_ref[...] = p3
    all_ref[:, :TOK] = dot3(p3, hidden_ref[...], NT)
    all_ref[:, TOK:] = dot3(p3, err_ref[...], NN)
    gram = pack(gram3(p3))
    c, half = lax.axis_index("c"), RANK // 2
    for ref, core in ((keep_ref, c), (send_ref, 1 - c)):
        ref[:, : TOK + EB] = all_ref[rows_at(core, half), :]
        ref[:, TOK + EB :] = gram


def right_kernel(mixed_ref, cot_ref, a_cot_ref, b_cot_ref, c_cot_ref, own_ref, a_ref, b_ref, c_ref, slots_ref, whole_ref):
    x, at = lax.axis_index("x"), lax.axis_index("y") * NZ + lax.axis_index("z")
    for place, ref in in_order(x, (cot_ref, a_cot_ref, b_cot_ref, c_cot_ref), DEALT):
        slots_ref[place] = ref[...]
    part = dot3(split3(mixed_ref[:, :TOK]), slots_ref[...].reshape(TOK, CB), NN)
    err_q = mixed_ref[:, TOK : TOK + EB]
    here = [jnp.where(at == x * (CB // EB) + i, err_q, 0.0) for i in range(CB // EB)]
    whole_ref[...] = part + jnp.concatenate(here, axis=1)
    scatter(whole_ref, lax.axis_index("y"), (own_ref, a_ref, b_ref, c_ref))


def first_kernel(mixed_ref, after_ref, inv_ref):
    inv_ref[...] = inverse_factor(unpack(mixed_ref[:, TOK + EB :]))


def basis_kernel(inv_ref, p3_ref, b3_ref, gram_ref):
    b3 = split3(dot6(inv_ref[...], p3_ref[...]))
    b3_ref[...] = b3
    gram_ref[...] = pack(gram3(b3))


def sum_y_kernel(own_ref, a_ref, b_ref, c_ref, after_ref, out_ref, slots_ref):
    out_ref[...] = sum_in_order(slots_ref, lax.axis_index("y"), (own_ref, a_ref, b_ref, c_ref), DEALT)


def add_after_kernel(a_ref, b_ref, after_ref, out_ref):
    out_ref[...] = a_ref[...] + b_ref[...]


def block_kernel(own_ref, a_ref, b_ref, c_ref, gram_ref, other_ref, out_ref):
    for place, ref in in_order(lax.axis_index("y"), (own_ref, a_ref, b_ref, c_ref)):
        out_ref[rows_at(place, RANK // 2 // NY), :CB] = ref[...]
    out_ref[:, CB:] = gram_ref[...] + other_ref[...]


def second_kernel(own_ref, a_ref, b_ref, c_ref, b3_ref, inv_ref, out_ref, total_ref, slots_ref, inverse_ref):
    for place, ref in in_order(lax.axis_index("x"), (own_ref, a_ref, b_ref, c_ref)):
        slots_ref[place] = ref[:, CB:]
    gram = unpack((slots_ref[0] + slots_ref[1]) + (slots_ref[2] + slots_ref[3]))
    rows = lax.broadcasted_iota(jnp.int32, (RANK, RANK), 0)
    cols = lax.broadcasted_iota(jnp.int32, (RANK, RANK), 1)
    off = gram - jnp.where(rows == cols, 1.0, 0.0).astype(f32)
    near = jnp.max(jnp.abs(off)) < 1e-3

    @pl.when(near)
    def _():
        inverse_ref[...] = near_inverse_factor(off)

    @pl.when(jnp.logical_not(near))
    def _():
        inverse_ref[...] = inverse_factor(gram)

    inverse = inverse_ref[...]
    total_ref[...] = jnp.dot(inverse, inv_ref[...], precision=HIGHEST, preferred_element_type=f32) * (1.0 / N_DP)
    out_ref[...] = dot6(inverse * math.sqrt(FF), b3_ref[...])


def new_kernel(*refs):
    total_ref, out_ref, s_ref, whole_ref, sems = refs[8:]
    x, c, half, total, copies = lax.axis_index("x"), lax.axis_index("c"), RANK // 2, total_ref[...], []
    for k, (place, ref) in enumerate(in_order(x, refs[:NX])):
        s_ref[k, rows_at(c, half), :] = ref[:, :CB]
        s_ref[k, rows_at(1 - c, half), :] = refs[NX + k][:, :CB]
        whole_ref[k] = dot6(total, split3(s_ref[k]))
        cols = rows_at(place, CB)
        copies.append(pltpu.make_async_copy(whole_ref.at[k], out_ref.at[:, cols], sems.at[k]))
        copies[k].start()
    for copy in copies:
        copy.wait()


def swap(a):
    return lax.ppermute(a, "c", [(0, 1), (1, 0)])


def swap_z(a):
    return lax.ppermute(a, "z", [(i, i ^ 1) for i in range(NZ)])


def shift(a, axis, k):
    size, step = {"y": (NY, 1), "z": (NZ, 2), "x": (NX, 1)}[axis]
    return lax.ppermute(a, axis, [(i, (i + k * step) % size) for i in range(size)])


def deal(blocks, axis):
    return [blocks[0]] + [shift(block, axis, k) for k, block in zip(DEALT[1:], blocks[1:], strict=True)]


def share(block, axis):
    return [block] + [shift(block, axis, k) for k in (1, 3, 2)]


def shards(hidden, cotangent, error_buf, q_start):
    qt = q_start.T
    dma, half = pltpu.SemaphoreType.DMA, RANK // 2
    cot, qt, hid, err = (pltpu.with_memory_space_constraint(a, pltpu.HBM) for a in (cotangent, q_start.T, hidden, error_buf))
    proj, cot, q_own = call(
        project_kernel, [((TB, 4 * RANK), bf16), ((TB, D), bf16), ((RANK, EB), f32)], cot, qt,
        scratch=[pltpu.VMEM((RANK, D), f32), dma((6,))], hbm=(0, 1),
    )
    hid, err = call(
        fetch_kernel, [((TOK, FB), bf16), ((FB, EB), bf16)], hid, err, proj, scratch=[dma((2,))], hbm=(0, 1), unread=(2,)
    )
    proj = call(join_c_kernel, ((2 * TB, 4 * RANK), bf16), proj, swap(proj))
    quarter, eighth = ((RANK // NY, FB), f32), ((RANK // NY // 2, FB), f32)
    *parts, cot = call(
        left_kernel, [quarter] * 4 + [((TB, D), bf16)], *share(proj, "x"), hid, err, q_own, cot,
        scratch=[pltpu.VMEM((4, 2 * TB, 4 * RANK), bf16), pltpu.VMEM((RANK, FB), f32)],
    )

    parts = deal(parts, "y")
    blocks = call(columns_kernel, [((2 * TB, CB), bf16)] * NX, cot, swap(cot), parts[2], unread=(2,))
    cot = deal(blocks, "x")
    keep, send = call(
        halve_kernel, [eighth, eighth], *parts, cot[0], scratch=[pltpu.VMEM((4, *quarter[0]), f32), pltpu.VMEM(*quarter)], unread=(4,)
    )
    p = call(add_kernel, eighth, keep, swap_z(send))
    p = call(
        sum_z_after_kernel, eighth, *share(p, "z"), cot[2], cot[3], scratch=[pltpu.VMEM((4, *eighth[0]), f32)], unread=(4, 5)
    )
    p = call(join_z_kernel, quarter, p, swap_z(p))

    halves = ((half, TOK + EB + 2 * RANK), f32)
    p3, keep, send = call(
        mixed_kernel, [((3 * RANK, FB), bf16), halves, halves], *share(p, "y"), hid, err, cot[1],
        scratch=[pltpu.VMEM((RANK, FB), f32), pltpu.VMEM((RANK, TOK + EB), f32)], unread=(6,),
    )
    mixed = call(add_kernel, halves, keep, swap(send))
    mixed = call(sum_x_kernel, halves, *share(mixed, "x"), scratch=[pltpu.VMEM((4, *halves[0]), f32)])

    piece = ((half // NY, CB), f32)
    parts = call(
        right_kernel, [piece] * 4, mixed, *cot, scratch=[pltpu.VMEM((4, 2 * TB, CB), bf16), pltpu.VMEM((half, CB), f32)]
    )
    inverse = call(first_kernel, ((RANK, RANK), f32), mixed, parts[0], unread=(1,))
    s = call(sum_y_kernel, piece, *deal(parts, "y"), inverse, scratch=[pltpu.VMEM((4, *piece[0]), f32)], unread=(4,))
    b3, gram = call(basis_kernel, [((3 * RANK, FB), bf16), ((half, 2 * RANK), f32)], inverse, p3)
    s = call(add_after_kernel, piece, s, swap_z(s), gram, unread=(2,))
    s = call(sum_z_kernel, piece, *share(s, "z"), scratch=[pltpu.VMEM((4, *piece[0]), f32)])
    s = call(block_kernel, ((half, CB + 2 * RANK), f32), *share(s, "y"), gram, swap(gram))
    blocks = share(s, "x")
    scaled, total = call(
        second_kernel, [((RANK, FB), f32), ((RANK, RANK), f32)], *blocks, b3, inverse,
        scratch=[pltpu.VMEM((4, half, 2 * RANK), f32), pltpu.VMEM((RANK, RANK), f32)],
    )
    q_new = call(
        new_kernel, ((RANK, D), f32), *blocks, *[swap(b) for b in blocks], total,
        scratch=[pltpu.VMEM((NX, RANK, CB), f32), pltpu.VMEM((NX, RANK, CB), f32), dma((NX,))], out_hbm=True,
    )
    return scaled.T, q_new.T


def solution(mesh):
    fine = Mesh(mesh.devices.reshape(NY, NZ, NX, NC), ("y", "z", "x", "c"))
    dp, tensor = ("y", "z"), ("x", "c")
    placed = (P(dp, tensor), P(dp + tensor, None), P(tensor, dp), P())
    return jax.shard_map(
        shards, mesh=fine, in_specs=placed, out_specs=(P(tensor, None), P()), check_vma=False
    )
```

```python
import functools
import math

import jax
import jax.numpy as jnp
from jax import lax
from jax.experimental import pallas as pl
from jax.experimental.pallas import tpu as pltpu
from jax.sharding import Mesh
from jax.sharding import PartitionSpec as P

FF = 14336
D = 4096
RANK = 64
N_DP = 32
TOK = 256
NY, NZ, NX, NC = 4, 8, 4, 2
FB = FF // (NX * NC)
CB = D // NX
EB = D // N_DP
TB = TOK // (NX * NC)
f32, bf16 = jnp.float32, jnp.bfloat16
HIGHEST = lax.Precision.HIGHEST
NN = (((1,), (0,)), ((), ()))
NT = (((1,), (1,)), ((), ()))


def split3(a):
    hi = a.astype(bf16)
    rest = a - hi.astype(f32)
    mid = rest.astype(bf16)
    low = (rest - mid.astype(f32)).astype(bf16)
    return jnp.concatenate([hi, mid, low], axis=0)


def add3(a):
    n = a.shape[0] // 3
    return a[:n] + (a[n : 2 * n] + a[2 * n :])


def dot3(a, b, dims):
    return add3(lax.dot_general(a, b, dims, preferred_element_type=f32))


def gram3(a3):
    g = lax.dot_general(a3, a3, NT, preferred_element_type=f32)
    r = RANK
    g00, g01, g02 = g[:r, :r], g[:r, r : 2 * r], g[:r, 2 * r :]
    g10, g11, g20 = g[r : 2 * r, :r], g[r : 2 * r, r : 2 * r], g[2 * r :, :r]
    return g00 + ((g01 + g10) + (g11 + (g02 + g20)))


def wide(column):
    return jnp.broadcast_to(column, (8, 2 * RANK))


def with_identity(gram):
    rows = lax.broadcasted_iota(jnp.int32, (RANK, RANK), 0)
    cols = lax.broadcasted_iota(jnp.int32, (RANK, RANK), 1)
    return jnp.concatenate([gram, jnp.where(rows == cols, 1.0, 0.0).astype(f32)], axis=1)


def eliminate(both, first, last):
    sub = lax.broadcasted_iota(jnp.int32, (8, 2 * RANK), 0)
    count = RANK // 8
    tiles = [both[8 * i : 8 * i + 8] for i in range(count)]
    for p in range(first, last):
        columns = [[wide(tiles[i][:, 8 * p + j : 8 * p + j + 1]) for j in range(8)] for i in range(p, count)]
        panel, own, pivots, scales = tiles[p], columns[0], jnp.ones((8, 2 * RANK), f32), []
        for s in range(8):
            pivot = own[s][s : s + 1]
            scales.append(1.0 / pivot)
            pivots = jnp.where(sub == s, pivot, pivots)
            factor = jnp.where(sub > s, own[s] * scales[s], 0.0)
            panel = panel - factor * panel[s : s + 1]
            for j in range(s + 1, 8):
                own[j] = own[j] - factor * own[j][s : s + 1]
        for i in range(p + 1, count):
            below, tile = columns[i - p], tiles[i]
            for s in range(8):
                factor = below[s] * scales[s]
                tile = tile - factor * panel[s : s + 1]
                for j in range(s + 1, 8):
                    below[j] = below[j] - factor * own[j][s : s + 1]
            tiles[i] = tile
        tiles[p] = panel * lax.rsqrt(pivots)
    return jnp.concatenate(tiles, axis=0)


def inverse_factor(gram):
    return eliminate(with_identity(gram), 0, RANK // 8)[:, RANK:]


def near_inverse_factor(off):
    rows = lax.broadcasted_iota(jnp.int32, (RANK, RANK), 0)
    cols = lax.broadcasted_iota(jnp.int32, (RANK, RANK), 1)
    lower = jnp.where(rows > cols, 1.0, jnp.where(rows == cols, 0.5, 0.0)).astype(f32)
    first = off * lower
    second = -lower * lax.dot_general(first, first, NT, precision=HIGHEST, preferred_element_type=f32)
    square = jnp.dot(first, first, precision=HIGHEST, preferred_element_type=f32)
    eye = jnp.where(rows == cols, 1.0, 0.0).astype(f32)
    return eye - first + (square - second)


def dot6(a, b3):
    hi = a.astype(bf16).astype(f32)
    mid = (a - hi).astype(bf16).astype(f32)
    low = a - hi - mid
    one = jnp.concatenate([hi, hi, hi, mid], axis=1).astype(bf16)
    two = jnp.concatenate([mid, low], axis=1).astype(bf16)
    high, middle = b3[:RANK], b3[RANK : 2 * RANK]
    out = jnp.dot(one, jnp.concatenate([b3, high], axis=0), preferred_element_type=f32)
    return out + jnp.dot(two, jnp.concatenate([middle, high], axis=0), preferred_element_type=f32)


def pack(square):
    return jnp.concatenate([square[: RANK // 2], square[RANK // 2 :]], axis=1)


def unpack(packed):
    return jnp.concatenate([packed[:, :RANK], packed[:, RANK:]], axis=0)


def call(kernel, out_shape, *args, scratch=(), hbm=(), unread=(), out_hbm=False, aliases=None):
    vmem, far, anywhere = (pl.BlockSpec(memory_space=m) for m in (pltpu.VMEM, pltpu.HBM, pl.ANY))
    many = isinstance(out_shape, list)
    shapes = [jax.ShapeDtypeStruct(*s) for s in (out_shape if many else [out_shape])]
    return pl.pallas_call(
        kernel,
        out_shape=shapes if many else shapes[0],
        in_specs=[far if i in hbm else anywhere if i in unread else vmem for i in range(len(args))],
        out_specs=[vmem] * len(shapes) if many else far if out_hbm else vmem,
        scratch_shapes=list(scratch),
        input_output_aliases=aliases or {},
        compiler_params=pltpu.CompilerParams(vmem_limit_bytes=32 * 1024 * 1024),
    )(*args)


DEALT = (0, 2, 1, 3)


def rows_at(index, size):
    return pl.ds(pl.multiple_of(index * size, size), size)


def in_order(index, refs, ks=(0, 1, 3, 2)):
    for k, ref in zip(ks, refs, strict=True):
        yield lax.rem(index + 4 - k, 4), ref


def sum_in_order(slots_ref, index, refs, ks=(0, 1, 3, 2)):
    for place, ref in in_order(index, refs, ks):
        slots_ref[place] = ref[...]
    return (slots_ref[0] + slots_ref[1]) + (slots_ref[2] + slots_ref[3])


def scatter(whole_ref, index, refs):
    size = whole_ref.shape[0] // 4
    for k, ref in zip(DEALT, refs, strict=True):
        ref[...] = whole_ref[rows_at(lax.rem(index + k, 4), size), :]


def project_kernel(cot_ref, qt_ref, out_ref, c_ref, own_ref, qt, sems):
    at, cut, parts = lax.axis_index("y") * NZ + lax.axis_index("z"), 1024, []
    pairs = [(cot_ref, c_ref)]
    pairs += [(qt_ref.at[:, i : i + cut], qt.at[:, i : i + cut]) for i in range(0, D, cut)]
    pairs += [(qt_ref.at[:, rows_at(at, EB)], own_ref)]
    copies = [pltpu.make_async_copy(a, b, sems.at[i]) for i, (a, b) in enumerate(pairs)]
    for copy in copies:
        copy.start()
    copies[0].wait()
    for i in range(D // cut):
        copies[1 + i].wait()
        cols = slice(i * cut, (i + 1) * cut)
        parts.append(lax.dot_general(c_ref[:, cols], split3(qt[:, cols]), NT, preferred_element_type=f32))
    got = (parts[0] + parts[1]) + (parts[2] + parts[3])
    own = got[:, :RANK] + (got[:, RANK : 2 * RANK] + got[:, 2 * RANK :])
    out_ref[...] = jnp.concatenate([own[: TB // 2], own[TB // 2 :]], axis=1)
    copies[1 + D // cut].wait()


def fetch_kernel(hidden_ref, err_ref, after_ref, h_ref, e_ref, sems):
    copies = [pltpu.make_async_copy(a, b, sems.at[i]) for i, (a, b) in enumerate(((hidden_ref, h_ref), (err_ref, e_ref)))]
    for copy in copies:
        copy.start()
    for copy in copies:
        copy.wait()


def join_c_kernel(own_ref, other_ref, out_ref):
    c, half = lax.axis_index("c"), own_ref.shape[0]
    out_ref[rows_at(c, half), :] = own_ref[...]
    out_ref[rows_at(1 - c, half), :] = other_ref[...]


def columns_kernel(own_ref, other_ref, after_ref, *out_refs):
    x, c = lax.axis_index("x"), lax.axis_index("c")
    for k, ref in zip(DEALT, out_refs, strict=True):
        cols = rows_at(lax.rem(x + k, NX), CB)
        ref[rows_at(c, TB), :] = own_ref[:, cols]
        ref[rows_at(1 - c, TB), :] = other_ref[:, cols]


def left_kernel(
    got_ref, a_got_ref, b_got_ref, c_got_ref, hidden_ref, err_ref, q_ref, cot_ref,
    own_ref, a_ref, b_ref, c_ref, pass_ref, slots_ref, whole_ref,
):
    for place, ref in in_order(lax.axis_index("x"), (got_ref, a_got_ref, b_got_ref, c_got_ref)):
        slots_ref[place] = ref[...]
    pass_ref[...] = cot_ref[...]
    packed = slots_ref[...].reshape(TOK // 2, 2 * RANK).T
    proj = jnp.concatenate([packed[:RANK], packed[RANK:]], axis=1)
    h = hidden_ref[...].reshape(NX * NC, 2, TB // 2, FB)
    h = jnp.concatenate([h[:, 0].reshape(TOK // 2, FB), h[:, 1].reshape(TOK // 2, FB)], axis=0)
    whole_ref[...] = dot3(split3(proj), h, NN) + dot3(split3(q_ref[...]), err_ref[...], NT)
    scatter(whole_ref, lax.axis_index("y"), (own_ref, a_ref, b_ref, c_ref))


def halve_kernel(own_ref, a_ref, b_ref, c_ref, after_ref, keep_ref, send_ref, slots_ref, both_ref):
    both_ref[...] = sum_in_order(slots_ref, lax.axis_index("y"), (own_ref, a_ref, b_ref, c_ref), DEALT)
    bit, half = lax.rem(lax.axis_index("z"), 2), keep_ref.shape[0]
    keep_ref[...] = both_ref[rows_at(bit, half), :]
    send_ref[...] = both_ref[rows_at(1 - bit, half), :]


def add_kernel(a_ref, b_ref, out_ref):
    out_ref[...] = a_ref[...] + b_ref[...]


def sum_z_kernel(own_ref, a_ref, b_ref, c_ref, out_ref, slots_ref):
    out_ref[...] = sum_in_order(slots_ref, lax.axis_index("z") // 2, (own_ref, a_ref, b_ref, c_ref))


def sum_z_after_kernel(own_ref, a_ref, b_ref, c_ref, *rest):
    sum_z_kernel(own_ref, a_ref, b_ref, c_ref, *rest[-2:])


def sum_class_kernel(own_ref, a_ref, b_ref, c_ref, after_ref, out_ref, slots_ref):
    out_ref[...] = sum_in_order(slots_ref, lax.rem(lax.axis_index("z"), 4), (own_ref, a_ref, b_ref, c_ref))


def sum_x_kernel(own_ref, a_ref, b_ref, c_ref, out_ref, slots_ref):
    out_ref[...] = sum_in_order(slots_ref, lax.axis_index("x"), (own_ref, a_ref, b_ref, c_ref))


def join_z_kernel(own_ref, other_ref, out_ref):
    bit, half = lax.rem(lax.axis_index("z"), 2), own_ref.shape[0]
    out_ref[rows_at(bit, half), :] = own_ref[...]
    out_ref[rows_at(1 - bit, half), :] = other_ref[...]


def mixed_kernel(own_ref, a_ref, b_ref, c_ref, hidden_ref, err_ref, after_ref, p3_ref, keep_ref, send_ref, p_ref, all_ref):
    for place, ref in in_order(lax.axis_index("y"), (own_ref, a_ref, b_ref, c_ref)):
        p_ref[rows_at(place, RANK // NY), :] = ref[...]
    p3 = split3(p_ref[...])
    p3_ref[...] = p3
    all_ref[:, :TOK] = dot3(p3, hidden_ref[...], NT)
    all_ref[:, TOK:] = dot3(p3, err_ref[...], NN)
    gram = pack(gram3(p3))
    c, half = lax.axis_index("c"), RANK // 2
    for ref, core in ((keep_ref, c), (send_ref, 1 - c)):
        ref[:, : TOK + EB] = all_ref[rows_at(core, half), :]
        ref[:, TOK + EB :] = gram


def right_kernel(mixed_ref, cot_ref, a_cot_ref, b_cot_ref, c_cot_ref, own_ref, a_ref, b_ref, c_ref, slots_ref, whole_ref):
    x, at = lax.axis_index("x"), lax.axis_index("y") * NZ + lax.axis_index("z")
    for place, ref in in_order(x, (cot_ref, a_cot_ref, b_cot_ref, c_cot_ref), DEALT):
        slots_ref[place] = ref[...]
    part = dot3(split3(mixed_ref[:, :TOK]), slots_ref[...].reshape(TOK, CB), NN)
    err_q = mixed_ref[:, TOK : TOK + EB]
    here = [jnp.where(at == x * (CB // EB) + i, err_q, 0.0) for i in range(CB // EB)]
    whole_ref[...] = part + jnp.concatenate(here, axis=1)
    scatter(whole_ref, lax.axis_index("y"), (own_ref, a_ref, b_ref, c_ref))


def first_kernel(mixed_ref, after_ref, half_ref):
    half_ref[...] = eliminate(with_identity(unpack(mixed_ref[:, TOK + EB :])), 0, RANK // 16)


def rest_kernel(half_ref, after_ref, inv_ref):
    inv_ref[...] = eliminate(half_ref[...], RANK // 16, RANK // 8)[:, RANK:]


def basis_kernel(inv_ref, p3_ref, b3_ref, gram_ref):
    b3 = split3(dot6(inv_ref[...], p3_ref[...]))
    b3_ref[...] = b3
    gram_ref[...] = pack(gram3(b3))


def sum_y_kernel(own_ref, a_ref, b_ref, c_ref, after_ref, out_ref, slots_ref):
    out_ref[...] = sum_in_order(slots_ref, lax.axis_index("y"), (own_ref, a_ref, b_ref, c_ref), DEALT)


def add_after_kernel(a_ref, b_ref, after_ref, out_ref):
    out_ref[...] = a_ref[...] + b_ref[...]


def block_kernel(own_ref, a_ref, b_ref, c_ref, after_ref, out_ref):
    for place, ref in in_order(lax.axis_index("y"), (own_ref, a_ref, b_ref, c_ref)):
        out_ref[rows_at(place, RANK // 2 // NY), :] = ref[...]


def second_kernel(gram_ref, b3_ref, inv_ref, block_ref, out_ref, total_ref, pass_ref, inverse_ref):
    pass_ref[...] = block_ref[...]
    gram = unpack(gram_ref[...])
    rows = lax.broadcasted_iota(jnp.int32, (RANK, RANK), 0)
    cols = lax.broadcasted_iota(jnp.int32, (RANK, RANK), 1)
    off = gram - jnp.where(rows == cols, 1.0, 0.0).astype(f32)
    near = jnp.max(jnp.abs(off)) < 1e-3

    @pl.when(near)
    def _():
        inverse_ref[...] = near_inverse_factor(off)

    @pl.when(jnp.logical_not(near))
    def _():
        inverse_ref[...] = inverse_factor(gram)

    inverse = inverse_ref[...]
    total_ref[...] = jnp.dot(inverse, inv_ref[...], precision=HIGHEST, preferred_element_type=f32) * (1.0 / N_DP)
    out_ref[...] = dot6(inverse * math.sqrt(FF), b3_ref[...])


def new_kernel(ks, *refs):
    count = len(ks)
    total_ref, (out_ref, s_ref, whole_ref, sems) = refs[2 * count], refs[-4:]
    x, c, half, total, copies = lax.axis_index("x"), lax.axis_index("c"), RANK // 2, total_ref[...], []
    for i, k in enumerate(ks):
        s_ref[i, rows_at(c, half), :] = refs[i][...]
        s_ref[i, rows_at(1 - c, half), :] = refs[count + i][...]
        whole_ref[i] = dot6(total, split3(s_ref[i]))
        cols = rows_at(lax.rem(x + NX - k, NX), CB)
        copies.append(pltpu.make_async_copy(whole_ref.at[i], out_ref.at[:, cols], sems.at[i]))
        copies[i].start()
    for copy in copies:
        copy.wait()


def swap(a):
    return lax.ppermute(a, "c", [(0, 1), (1, 0)])


def swap_z(a):
    return lax.ppermute(a, "z", [(i, i ^ 1) for i in range(NZ)])


def swap_pairs(a, axis, size, partner):
    return lax.ppermute(a, axis, [(i, partner(i)) for i in range(size)])


def shift(a, axis, k):
    size, step = {"y": (NY, 1), "z": (NZ, 2), "x": (NX, 1)}[axis]
    return lax.ppermute(a, axis, [(i, (i + k * step) % size) for i in range(size)])


def share_z(block):
    return [block] + [lax.ppermute(block, "z", [(i, (i + k) % NZ) for i in range(NZ)]) for k in (1, -1, 2)]


def deal(blocks, axis):
    return [blocks[0]] + [shift(block, axis, k) for k, block in zip(DEALT[1:], blocks[1:], strict=True)]


def share(block, axis):
    return [block] + [shift(block, axis, k) for k in (1, 3, 2)]


def shards(hidden, cotangent, error_buf, q_start):
    qt = q_start.T
    dma, half = pltpu.SemaphoreType.DMA, RANK // 2
    cot, qt, hid, err = (pltpu.with_memory_space_constraint(a, pltpu.HBM) for a in (cotangent, q_start.T, hidden, error_buf))
    proj, cot, q_own = call(
        project_kernel, [((TB // 2, 2 * RANK), f32), ((TB, D), bf16), ((RANK, EB), f32)], cot, qt,
        scratch=[pltpu.VMEM((RANK, D), f32), dma((6,))], hbm=(0, 1),
    )
    hid, err = call(
        fetch_kernel, [((TOK, FB), bf16), ((FB, EB), bf16)], hid, err, proj, scratch=[dma((2,))], hbm=(0, 1), unread=(2,)
    )
    proj = call(join_c_kernel, ((TB, 2 * RANK), f32), proj, swap(proj))
    quarter, eighth = ((RANK // NY, FB), f32), ((RANK // NY // 2, FB), f32)
    *parts, cot = call(
        left_kernel, [quarter] * 4 + [((TB, D), bf16)], *share(proj, "x"), hid, err, q_own, cot,
        scratch=[pltpu.VMEM((4, TB, 2 * RANK), f32), pltpu.VMEM((RANK, FB), f32)],
    )

    parts = deal(parts, "y")
    blocks = call(columns_kernel, [((2 * TB, CB), bf16)] * NX, cot, swap(cot), parts[2], unread=(2,))
    cot = deal(blocks, "x")
    keep, send = call(
        halve_kernel, [eighth, eighth], *parts, cot[0], scratch=[pltpu.VMEM((4, *quarter[0]), f32), pltpu.VMEM(*quarter)], unread=(4,)
    )
    p = call(add_kernel, eighth, keep, swap_z(send))
    p = call(
        sum_z_after_kernel, eighth, *share(p, "z"), cot[2], cot[3], scratch=[pltpu.VMEM((4, *eighth[0]), f32)], unread=(4, 5)
    )
    p = call(join_z_kernel, quarter, p, swap_z(p))

    halves = ((half, TOK + EB + 2 * RANK), f32)
    p3, keep, send = call(
        mixed_kernel, [((3 * RANK, FB), bf16), halves, halves], *share(p, "y"), hid, err, cot[1],
        scratch=[pltpu.VMEM((RANK, FB), f32), pltpu.VMEM((RANK, TOK + EB), f32)], unread=(6,),
    )
    mixed = call(add_kernel, halves, keep, swap(send))
    mixed = call(sum_x_kernel, halves, *share(mixed, "x"), scratch=[pltpu.VMEM((4, *halves[0]), f32)])

    piece = ((half // NY, CB), f32)
    parts = call(
        right_kernel, [piece] * 4, mixed, *cot, scratch=[pltpu.VMEM((4, 2 * TB, CB), bf16), pltpu.VMEM((half, CB), f32)]
    )
    small = ((half, 2 * RANK), f32)
    state = call(first_kernel, ((RANK, 2 * RANK), f32), mixed, parts[0], unread=(1,))
    s = call(sum_y_kernel, piece, *deal(parts, "y"), state, scratch=[pltpu.VMEM((4, *piece[0]), f32)], unread=(4,))
    inverse = call(rest_kernel, ((RANK, RANK), f32), state, s, unread=(1,))
    b3, gram = call(basis_kernel, [((3 * RANK, FB), bf16), small], inverse, p3)
    s = call(add_after_kernel, piece, s, swap_pairs(s, "z", NZ, lambda i: (i + 4) % NZ), gram, unread=(2,))
    gram = call(add_after_kernel, small, gram, swap(gram), s, unread=(2,))
    other = swap_pairs(gram, "x", NX, lambda i: i ^ 1)
    s = call(sum_class_kernel, piece, *share_z(s), other, scratch=[pltpu.VMEM((4, *piece[0]), f32)], unread=(4,))
    gram = call(add_after_kernel, small, gram, other, s, unread=(2,))
    other = swap_pairs(gram, "x", NX, lambda i: 3 - i)
    s = call(block_kernel, ((half, CB), f32), *share(s, "y"), other, unread=(4,))
    gram = call(add_after_kernel, small, gram, other, s, unread=(2,))
    scaled, total, own = call(
        second_kernel, [((RANK, FB), f32), ((RANK, RANK), f32), ((half, CB), f32)], gram, b3, inverse, s,
        scratch=[pltpu.VMEM((RANK, RANK), f32)],
    )
    _, one, three, two = share(s, "x")
    some = (own, two, three)

    def scratch(count):
        return [pltpu.VMEM((count, RANK, CB), f32), pltpu.VMEM((count, RANK, CB), f32), dma((count,))]

    q_new = call(
        functools.partial(new_kernel, (0, 2, 3)), ((RANK, D), f32), *some, *[swap(b) for b in some], total,
        scratch=scratch(3), out_hbm=True,
    )
    q_new = call(
        functools.partial(new_kernel, (1,)), ((RANK, D), f32), one, swap(one), total, q_new,
        scratch=scratch(1), hbm=(3,), out_hbm=True, aliases={3: 0},
    )
    return scaled.T, q_new.T


def solution(mesh):
    fine = Mesh(mesh.devices.reshape(NY, NZ, NX, NC), ("y", "z", "x", "c"))
    dp, tensor = ("y", "z"), ("x", "c")
    placed = (P(dp, tensor), P(dp + tensor, None), P(tensor, dp), P())
    return jax.shard_map(
        shards, mesh=fine, in_specs=placed, out_specs=(P(tensor, None), P()), check_vma=False
    )
```

```python
import functools
import math

import jax
import jax.numpy as jnp
from jax import lax
from jax.experimental import pallas as pl
from jax.experimental.pallas import tpu as pltpu
from jax.sharding import Mesh
from jax.sharding import PartitionSpec as P

FF = 14336
D = 4096
RANK = 64
N_DP = 32
TOK = 256
NY, NZ, NX, NC = 4, 8, 4, 2
FB = FF // (NX * NC)
CB = D // NX
EB = D // N_DP
TB = TOK // (NX * NC)
f32, bf16 = jnp.float32, jnp.bfloat16
HIGHEST = lax.Precision.HIGHEST
NN = (((1,), (0,)), ((), ()))
NT = (((1,), (1,)), ((), ()))


def split3(a):
    hi = a.astype(bf16)
    rest = a - hi.astype(f32)
    mid = rest.astype(bf16)
    low = (rest - mid.astype(f32)).astype(bf16)
    return jnp.concatenate([hi, mid, low], axis=0)


def add3(a):
    n = a.shape[0] // 3
    return a[:n] + (a[n : 2 * n] + a[2 * n :])


def dot3(a, b, dims):
    return add3(lax.dot_general(a, b, dims, preferred_element_type=f32))


def gram3(a3):
    g = lax.dot_general(a3, a3, NT, preferred_element_type=f32)
    r = RANK
    g00, g01, g02 = g[:r, :r], g[:r, r : 2 * r], g[:r, 2 * r :]
    g10, g11, g20 = g[r : 2 * r, :r], g[r : 2 * r, r : 2 * r], g[2 * r :, :r]
    return g00 + ((g01 + g10) + (g11 + (g02 + g20)))


def wide(column):
    return jnp.broadcast_to(column, (8, 2 * RANK))


def inverse_factor(gram):
    rows = lax.broadcasted_iota(jnp.int32, (RANK, RANK), 0)
    cols = lax.broadcasted_iota(jnp.int32, (RANK, RANK), 1)
    both = jnp.concatenate([gram, jnp.where(rows == cols, 1.0, 0.0).astype(f32)], axis=1)
    sub = lax.broadcasted_iota(jnp.int32, (8, 2 * RANK), 0)
    count = RANK // 8
    tiles = [both[8 * i : 8 * i + 8] for i in range(count)]
    for p in range(count):
        columns = [[wide(tiles[i][:, 8 * p + j : 8 * p + j + 1]) for j in range(8)] for i in range(p, count)]
        panel, own, pivots, scales = tiles[p], columns[0], jnp.ones((8, 2 * RANK), f32), []
        for s in range(8):
            pivot = own[s][s : s + 1]
            scales.append(1.0 / pivot)
            pivots = jnp.where(sub == s, pivot, pivots)
            factor = jnp.where(sub > s, own[s] * scales[s], 0.0)
            panel = panel - factor * panel[s : s + 1]
            for j in range(s + 1, 8):
                own[j] = own[j] - factor * own[j][s : s + 1]
        for i in range(p + 1, count):
            below, tile = columns[i - p], tiles[i]
            for s in range(8):
                factor = below[s] * scales[s]
                tile = tile - factor * panel[s : s + 1]
                for j in range(s + 1, 8):
                    below[j] = below[j] - factor * own[j][s : s + 1]
            tiles[i] = tile
        tiles[p] = panel * lax.rsqrt(pivots)
    return jnp.concatenate(tiles, axis=0)[:, RANK:]


def near_inverse_factor(off):
    rows = lax.broadcasted_iota(jnp.int32, (RANK, RANK), 0)
    cols = lax.broadcasted_iota(jnp.int32, (RANK, RANK), 1)
    lower = jnp.where(rows > cols, 1.0, jnp.where(rows == cols, 0.5, 0.0)).astype(f32)
    first = off * lower
    second = -lower * lax.dot_general(first, first, NT, precision=HIGHEST, preferred_element_type=f32)
    square = jnp.dot(first, first, precision=HIGHEST, preferred_element_type=f32)
    eye = jnp.where(rows == cols, 1.0, 0.0).astype(f32)
    return eye - first + (square - second)


def dot6(a, b3):
    hi = a.astype(bf16).astype(f32)
    mid = (a - hi).astype(bf16).astype(f32)
    low = a - hi - mid
    one = jnp.concatenate([hi, hi, hi, mid], axis=1).astype(bf16)
    two = jnp.concatenate([mid, low], axis=1).astype(bf16)
    high, middle = b3[:RANK], b3[RANK : 2 * RANK]
    out = jnp.dot(one, jnp.concatenate([b3, high], axis=0), preferred_element_type=f32)
    return out + jnp.dot(two, jnp.concatenate([middle, high], axis=0), preferred_element_type=f32)


def pack(square):
    return jnp.concatenate([square[: RANK // 2], square[RANK // 2 :]], axis=1)


def unpack(packed):
    return jnp.concatenate([packed[:, :RANK], packed[:, RANK:]], axis=0)


def call(kernel, out_shape, *args, scratch=(), hbm=(), unread=(), out_hbm=False):
    vmem, far, anywhere = (pl.BlockSpec(memory_space=m) for m in (pltpu.VMEM, pltpu.HBM, pl.ANY))
    many = isinstance(out_shape, list)
    shapes = [jax.ShapeDtypeStruct(*s) for s in (out_shape if many else [out_shape])]
    return pl.pallas_call(
        kernel,
        out_shape=shapes if many else shapes[0],
        in_specs=[far if i in hbm else anywhere if i in unread else vmem for i in range(len(args))],
        out_specs=[far if out_hbm else vmem] * len(shapes) if many else vmem,
        scratch_shapes=list(scratch),
        compiler_params=pltpu.CompilerParams(vmem_limit_bytes=32 * 1024 * 1024),
    )(*args)


DEALT = (0, 2, 1, 3)


def rows_at(index, size):
    return pl.ds(pl.multiple_of(index * size, size), size)


def in_order(index, refs, ks=(0, 1, 3, 2)):
    for k, ref in zip(ks, refs, strict=True):
        yield lax.rem(index + 4 - k, 4), ref


def sum_in_order(slots_ref, index, refs, ks=(0, 1, 3, 2)):
    for place, ref in in_order(index, refs, ks):
        slots_ref[place] = ref[...]
    return (slots_ref[0] + slots_ref[1]) + (slots_ref[2] + slots_ref[3])


def scatter(whole_ref, index, refs):
    size = whole_ref.shape[0] // 4
    for k, ref in zip(DEALT, refs, strict=True):
        ref[...] = whole_ref[rows_at(lax.rem(index + k, 4), size), :]


def factor_kernel(qt_ref, q3_ref, own_ref, qt, sems):
    at, cut = lax.axis_index("y") * NZ + lax.axis_index("z"), 1024
    pairs = [(qt_ref.at[:, i : i + cut], qt.at[:, i : i + cut]) for i in range(0, D, cut)]
    pairs += [(qt_ref.at[:, rows_at(at, EB)], own_ref)]
    copies = [pltpu.make_async_copy(a, b, sems.at[i]) for i, (a, b) in enumerate(pairs)]
    for copy in copies:
        copy.start()
    for i in range(D // cut):
        copies[i].wait()
        q3_ref[:, i * cut : (i + 1) * cut] = split3(qt[:, i * cut : (i + 1) * cut])
    copies[-1].wait()


def project_kernel(cot_ref, other_ref, q3_ref, out_ref, both_ref):
    c = lax.axis_index("c")
    both_ref[rows_at(c, TB), :] = cot_ref[...]
    both_ref[rows_at(1 - c, TB), :] = other_ref[...]
    got = lax.dot_general(both_ref[...], q3_ref[...], NT, preferred_element_type=f32)
    got = got[:, :RANK] + (got[:, RANK : 2 * RANK] + got[:, 2 * RANK :])
    part = TB // 2
    for i in range(NC):
        own = got[i * TB : (i + 1) * TB]
        out_ref[i * part : (i + 1) * part, :] = jnp.concatenate([own[:part], own[part:]], axis=1)


def fetch_kernel(hidden_ref, err_ref, after_ref, h_ref, e_ref, sems):
    copies = [pltpu.make_async_copy(a, b, sems.at[i]) for i, (a, b) in enumerate(((hidden_ref, h_ref), (err_ref, e_ref)))]
    for copy in copies:
        copy.start()
    for copy in copies:
        copy.wait()


def columns_kernel(both_ref, after_ref, *out_refs):
    x = lax.axis_index("x")
    for k, ref in zip(DEALT, out_refs, strict=True):
        ref[...] = both_ref[:, rows_at(lax.rem(x + k, NX), CB)]


def left_kernel(
    got_ref, a_got_ref, b_got_ref, c_got_ref, hidden_ref, err_ref, q_ref,
    own_ref, a_ref, b_ref, c_ref, slots_ref, whole_ref,
):
    for place, ref in in_order(lax.axis_index("x"), (got_ref, a_got_ref, b_got_ref, c_got_ref)):
        slots_ref[place] = ref[...]
    packed = slots_ref[...].reshape(TOK // 2, 2 * RANK).T
    proj = jnp.concatenate([packed[:RANK], packed[RANK:]], axis=1)
    h = hidden_ref[...].reshape(NX * NC, 2, TB // 2, FB)
    h = jnp.concatenate([h[:, 0].reshape(TOK // 2, FB), h[:, 1].reshape(TOK // 2, FB)], axis=0)
    whole_ref[...] = dot3(split3(proj), h, NN) + dot3(split3(q_ref[...]), err_ref[...], NT)
    scatter(whole_ref, lax.axis_index("y"), (own_ref, a_ref, b_ref, c_ref))


def halve_kernel(own_ref, a_ref, b_ref, c_ref, after_ref, keep_ref, send_ref, slots_ref, both_ref):
    both_ref[...] = sum_in_order(slots_ref, lax.axis_index("y"), (own_ref, a_ref, b_ref, c_ref), DEALT)
    bit, half = lax.rem(lax.axis_index("z"), 2), keep_ref.shape[0]
    keep_ref[...] = both_ref[rows_at(bit, half), :]
    send_ref[...] = both_ref[rows_at(1 - bit, half), :]


def add_kernel(a_ref, b_ref, out_ref):
    out_ref[...] = a_ref[...] + b_ref[...]


def sum_z_kernel(own_ref, a_ref, b_ref, c_ref, out_ref, slots_ref):
    out_ref[...] = sum_in_order(slots_ref, lax.axis_index("z") // 2, (own_ref, a_ref, b_ref, c_ref))


def sum_z_after_kernel(own_ref, a_ref, b_ref, c_ref, *rest):
    sum_z_kernel(own_ref, a_ref, b_ref, c_ref, *rest[-2:])


def sum_x_kernel(own_ref, a_ref, b_ref, c_ref, out_ref, slots_ref):
    out_ref[...] = sum_in_order(slots_ref, lax.axis_index("x"), (own_ref, a_ref, b_ref, c_ref))


def join_z_kernel(own_ref, other_ref, out_ref):
    bit, half = lax.rem(lax.axis_index("z"), 2), own_ref.shape[0]
    out_ref[rows_at(bit, half), :] = own_ref[...]
    out_ref[rows_at(1 - bit, half), :] = other_ref[...]


def mixed_kernel(own_ref, a_ref, b_ref, c_ref, hidden_ref, err_ref, after_ref, p3_ref, keep_ref, send_ref, p_ref, all_ref):
    for place, ref in in_order(lax.axis_index("y"), (own_ref, a_ref, b_ref, c_ref)):
        p_ref[rows_at(place, RANK // NY), :] = ref[...]
    p3 = split3(p_ref[...])
    p3_ref[...] = p3
    all_ref[:, :TOK] = dot3(p3, hidden_ref[...], NT)
    all_ref[:, TOK:] = dot3(p3, err_ref[...], NN)
    gram = pack(gram3(p3))
    c, half = lax.axis_index("c"), RANK // 2
    for ref, core in ((keep_ref, c), (send_ref, 1 - c)):
        ref[:, : TOK + EB] = all_ref[rows_at(core, half), :]
        ref[:, TOK + EB :] = gram


def right_kernel(mixed_ref, cot_ref, a_cot_ref, b_cot_ref, c_cot_ref, own_ref, a_ref, b_ref, c_ref, slots_ref, whole_ref):
    x, at = lax.axis_index("x"), lax.axis_index("y") * NZ + lax.axis_index("z")
    for place, ref in in_order(x, (cot_ref, a_cot_ref, b_cot_ref, c_cot_ref), DEALT):
        slots_ref[place] = ref[...]
    part = dot3(split3(mixed_ref[:, :TOK]), slots_ref[...].reshape(TOK, CB), NN)
    err_q = mixed_ref[:, TOK : TOK + EB]
    here = [jnp.where(at == x * (CB // EB) + i, err_q, 0.0) for i in range(CB // EB)]
    whole_ref[...] = part + jnp.concatenate(here, axis=1)
    scatter(whole_ref, lax.axis_index("y"), (own_ref, a_ref, b_ref, c_ref))


def first_kernel(mixed_ref, after_ref, inv_ref):
    inv_ref[...] = inverse_factor(unpack(mixed_ref[:, TOK + EB :]))


def basis_kernel(inv_ref, p3_ref, b3_ref, gram_ref):
    b3 = split3(dot6(inv_ref[...], p3_ref[...]))
    b3_ref[...] = b3
    gram_ref[...] = pack(gram3(b3))


def sum_y_kernel(own_ref, a_ref, b_ref, c_ref, after_ref, out_ref, slots_ref):
    out_ref[...] = sum_in_order(slots_ref, lax.axis_index("y"), (own_ref, a_ref, b_ref, c_ref), DEALT)


def add_after_kernel(a_ref, b_ref, after_ref, out_ref):
    out_ref[...] = a_ref[...] + b_ref[...]


def block_kernel(own_ref, a_ref, b_ref, c_ref, gram_ref, other_ref, out_ref):
    for place, ref in in_order(lax.axis_index("y"), (own_ref, a_ref, b_ref, c_ref)):
        out_ref[rows_at(place, RANK // 2 // NY), :CB] = ref[...]
    out_ref[:, CB:] = gram_ref[...] + other_ref[...]


def second_kernel(own_ref, a_ref, b_ref, c_ref, inv_ref, total_ref, inverse_ref, slots_ref):
    for place, ref in in_order(lax.axis_index("x"), (own_ref, a_ref, b_ref, c_ref)):
        slots_ref[place] = ref[:, CB:]
    gram = unpack((slots_ref[0] + slots_ref[1]) + (slots_ref[2] + slots_ref[3]))
    rows = lax.broadcasted_iota(jnp.int32, (RANK, RANK), 0)
    cols = lax.broadcasted_iota(jnp.int32, (RANK, RANK), 1)
    off = gram - jnp.where(rows == cols, 1.0, 0.0).astype(f32)
    near = jnp.max(jnp.abs(off)) < 1e-3

    @pl.when(near)
    def _():
        inverse_ref[...] = near_inverse_factor(off)

    @pl.when(jnp.logical_not(near))
    def _():
        inverse_ref[...] = inverse_factor(gram)

    inverse = inverse_ref[...]
    total_ref[...] = jnp.dot(inverse, inv_ref[...], precision=HIGHEST, preferred_element_type=f32) * (1.0 / N_DP)


def new_kernel(*refs):
    total_ref, inverse_ref, b3_ref, out_ref, basis_ref, s_ref, whole_ref, scaled_ref, sems = refs[2 * NX :]
    x, c, half, total, copies = lax.axis_index("x"), lax.axis_index("c"), RANK // 2, total_ref[...], []
    for k, (place, ref) in enumerate(in_order(x, refs[:NX])):
        s_ref[k, rows_at(c, half), :] = ref[:, :CB]
        s_ref[k, rows_at(1 - c, half), :] = refs[NX + k][:, :CB]
        whole_ref[k] = dot6(total, split3(s_ref[k]))
        cols = rows_at(place, CB)
        copies.append(pltpu.make_async_copy(whole_ref.at[k], out_ref.at[:, cols], sems.at[k]))
        copies[-1].start()
        if k == 0:
            scaled_ref[...] = dot6(inverse_ref[...] * math.sqrt(FF), b3_ref[...])
            copies.append(pltpu.make_async_copy(scaled_ref, basis_ref, sems.at[NX]))
            copies[-1].start()
    for copy in copies:
        copy.wait()


def swap(a):
    return lax.ppermute(a, "c", [(0, 1), (1, 0)])


def swap_z(a):
    return lax.ppermute(a, "z", [(i, i ^ 1) for i in range(NZ)])


def shift(a, axis, k):
    size, step = {"y": (NY, 1), "z": (NZ, 2), "x": (NX, 1)}[axis]
    return lax.ppermute(a, axis, [(i, (i + k * step) % size) for i in range(size)])


def deal(blocks, axis):
    return [blocks[0]] + [shift(block, axis, k) for k, block in zip(DEALT[1:], blocks[1:], strict=True)]


def share(block, axis):
    return [block] + [shift(block, axis, k) for k in (1, 3, 2)]


def shards(hidden, cotangent, error_buf, q_start):
    qt = q_start.T
    dma, half = pltpu.SemaphoreType.DMA, RANK // 2
    qt, hid, err = (pltpu.with_memory_space_constraint(a, pltpu.HBM) for a in (q_start.T, hidden, error_buf))
    other = swap(cotangent)
    q3, q_own = call(
        factor_kernel, [((3 * RANK, D), bf16), ((RANK, EB), f32)], qt, scratch=[pltpu.VMEM((RANK, D), f32), dma((5,))], hbm=(0,)
    )
    proj, both = call(project_kernel, [((TB, 2 * RANK), f32), ((2 * TB, D), bf16)], cotangent, other, q3)
    hid, err = call(
        fetch_kernel, [((TOK, FB), bf16), ((FB, EB), bf16)], hid, err, proj, scratch=[dma((2,))], hbm=(0, 1), unread=(2,)
    )
    quarter, eighth = ((RANK // NY, FB), f32), ((RANK // NY // 2, FB), f32)
    parts = call(
        left_kernel, [quarter] * 4, *share(proj, "x"), hid, err, q_own,
        scratch=[pltpu.VMEM((4, TB, 2 * RANK), f32), pltpu.VMEM((RANK, FB), f32)],
    )

    parts = deal(parts, "y")
    blocks = call(columns_kernel, [((2 * TB, CB), bf16)] * NX, both, parts[2], unread=(1,))
    cot = deal(blocks, "x")
    keep, send = call(
        halve_kernel, [eighth, eighth], *parts, cot[0], scratch=[pltpu.VMEM((4, *quarter[0]), f32), pltpu.VMEM(*quarter)], unread=(4,)
    )
    p = call(add_kernel, eighth, keep, swap_z(send))
    p = call(
        sum_z_after_kernel, eighth, *share(p, "z"), cot[2], cot[3], scratch=[pltpu.VMEM((4, *eighth[0]), f32)], unread=(4, 5)
    )
    p = call(join_z_kernel, quarter, p, swap_z(p))

    halves = ((half, TOK + EB + 2 * RANK), f32)
    p3, keep, send = call(
        mixed_kernel, [((3 * RANK, FB), bf16), halves, halves], *share(p, "y"), hid, err, cot[1],
        scratch=[pltpu.VMEM((RANK, FB), f32), pltpu.VMEM((RANK, TOK + EB), f32)], unread=(6,),
    )
    mixed = call(add_kernel, halves, keep, swap(send))
    mixed = call(sum_x_kernel, halves, *share(mixed, "x"), scratch=[pltpu.VMEM((4, *halves[0]), f32)])

    piece = ((half // NY, CB), f32)
    parts = call(
        right_kernel, [piece] * 4, mixed, *cot, scratch=[pltpu.VMEM((4, 2 * TB, CB), bf16), pltpu.VMEM((half, CB), f32)]
    )
    inverse = call(first_kernel, ((RANK, RANK), f32), mixed, parts[0], unread=(1,))
    s = call(sum_y_kernel, piece, *deal(parts, "y"), inverse, scratch=[pltpu.VMEM((4, *piece[0]), f32)], unread=(4,))
    b3, gram = call(basis_kernel, [((3 * RANK, FB), bf16), ((half, 2 * RANK), f32)], inverse, p3)
    s = call(add_after_kernel, piece, s, swap_z(s), gram, unread=(2,))
    s = call(sum_z_kernel, piece, *share(s, "z"), scratch=[pltpu.VMEM((4, *piece[0]), f32)])
    s = call(block_kernel, ((half, CB + 2 * RANK), f32), *share(s, "y"), gram, swap(gram))
    blocks = share(s, "x")
    square = ((RANK, RANK), f32)
    total, second = call(second_kernel, [square, square], *blocks, inverse, scratch=[pltpu.VMEM((4, half, 2 * RANK), f32)])
    wide_block = pltpu.VMEM((NX, RANK, CB), f32)
    q_new, scaled = call(
        new_kernel, [((RANK, D), f32), ((RANK, FB), f32)], *blocks, *[swap(b) for b in blocks], total, second, b3,
        scratch=[wide_block, wide_block, pltpu.VMEM((RANK, FB), f32), dma((NX + 1,))], out_hbm=True,
    )
    return scaled.T, q_new.T


def solution(mesh):
    fine = Mesh(mesh.devices.reshape(NY, NZ, NX, NC), ("y", "z", "x", "c"))
    dp, tensor = ("y", "z"), ("x", "c")
    placed = (P(dp, tensor), P(dp + tensor, None), P(tensor, dp), P())
    return jax.shard_map(
        shards, mesh=fine, in_specs=placed, out_specs=(P(tensor, None), P()), check_vma=False
    )
```

```python
import functools
import math

import jax
import jax.numpy as jnp
from jax import lax
from jax.experimental import pallas as pl
from jax.experimental.pallas import tpu as pltpu
from jax.sharding import Mesh
from jax.sharding import PartitionSpec as P

FF = 14336
D = 4096
RANK = 64
N_DP = 32
TOK = 256
NY, NZ, NX, NC = 4, 8, 4, 2
FB = FF // (NX * NC)
CB = D // NX
EB = D // N_DP
TB = TOK // (NX * NC)
f32, bf16 = jnp.float32, jnp.bfloat16
HIGHEST = lax.Precision.HIGHEST
NN = (((1,), (0,)), ((), ()))
NT = (((1,), (1,)), ((), ()))


def split3(a):
    hi = a.astype(bf16)
    rest = a - hi.astype(f32)
    mid = rest.astype(bf16)
    low = (rest - mid.astype(f32)).astype(bf16)
    return jnp.concatenate([hi, mid, low], axis=0)


def add3(a):
    n = a.shape[0] // 3
    return a[:n] + (a[n : 2 * n] + a[2 * n :])


def dot3(a, b, dims):
    return add3(lax.dot_general(a, b, dims, preferred_element_type=f32))


def gram3(a3):
    g = lax.dot_general(a3, a3, NT, preferred_element_type=f32)
    r = RANK
    g00, g01, g02 = g[:r, :r], g[:r, r : 2 * r], g[:r, 2 * r :]
    g10, g11, g20 = g[r : 2 * r, :r], g[r : 2 * r, r : 2 * r], g[2 * r :, :r]
    return g00 + ((g01 + g10) + (g11 + (g02 + g20)))


def wide(column):
    return jnp.broadcast_to(column, (8, 2 * RANK))


def inverse_factor(gram):
    rows = lax.broadcasted_iota(jnp.int32, (RANK, RANK), 0)
    cols = lax.broadcasted_iota(jnp.int32, (RANK, RANK), 1)
    both = jnp.concatenate([gram, jnp.where(rows == cols, 1.0, 0.0).astype(f32)], axis=1)
    sub = lax.broadcasted_iota(jnp.int32, (8, 2 * RANK), 0)
    count = RANK // 8
    tiles = [both[8 * i : 8 * i + 8] for i in range(count)]
    for p in range(count):
        columns = [[wide(tiles[i][:, 8 * p + j : 8 * p + j + 1]) for j in range(8)] for i in range(p, count)]
        panel, own, pivots, scales = tiles[p], columns[0], jnp.ones((8, 2 * RANK), f32), []
        for s in range(8):
            pivot = own[s][s : s + 1]
            scales.append(1.0 / pivot)
            pivots = jnp.where(sub == s, pivot, pivots)
            factor = jnp.where(sub > s, own[s] * scales[s], 0.0)
            panel = panel - factor * panel[s : s + 1]
            for j in range(s + 1, 8):
                own[j] = own[j] - factor * own[j][s : s + 1]
        for i in range(p + 1, count):
            below, tile = columns[i - p], tiles[i]
            for s in range(8):
                factor = below[s] * scales[s]
                tile = tile - factor * panel[s : s + 1]
                for j in range(s + 1, 8):
                    below[j] = below[j] - factor * own[j][s : s + 1]
            tiles[i] = tile
        tiles[p] = panel * lax.rsqrt(pivots)
    return jnp.concatenate(tiles, axis=0)[:, RANK:]


def near_inverse_factor(off):
    rows = lax.broadcasted_iota(jnp.int32, (RANK, RANK), 0)
    cols = lax.broadcasted_iota(jnp.int32, (RANK, RANK), 1)
    lower = jnp.where(rows > cols, 1.0, jnp.where(rows == cols, 0.5, 0.0)).astype(f32)
    first = off * lower
    second = -lower * lax.dot_general(first, first, NT, precision=HIGHEST, preferred_element_type=f32)
    square = jnp.dot(first, first, precision=HIGHEST, preferred_element_type=f32)
    eye = jnp.where(rows == cols, 1.0, 0.0).astype(f32)
    return eye - first + (square - second)


def dot6(a, b3):
    hi = a.astype(bf16).astype(f32)
    mid = (a - hi).astype(bf16).astype(f32)
    low = a - hi - mid
    one = jnp.concatenate([hi, hi, hi, mid], axis=1).astype(bf16)
    two = jnp.concatenate([mid, low], axis=1).astype(bf16)
    high, middle = b3[:RANK], b3[RANK : 2 * RANK]
    out = jnp.dot(one, jnp.concatenate([b3, high], axis=0), preferred_element_type=f32)
    return out + jnp.dot(two, jnp.concatenate([middle, high], axis=0), preferred_element_type=f32)


def pack(square):
    return jnp.concatenate([square[: RANK // 2], square[RANK // 2 :]], axis=1)


def unpack(packed):
    return jnp.concatenate([packed[:, :RANK], packed[:, RANK:]], axis=0)


def call(kernel, out_shape, *args, scratch=(), hbm=(), unread=(), out_hbm=False):
    vmem, far, anywhere = (pl.BlockSpec(memory_space=m) for m in (pltpu.VMEM, pltpu.HBM, pl.ANY))
    many = isinstance(out_shape, list)
    shapes = [jax.ShapeDtypeStruct(*s) for s in (out_shape if many else [out_shape])]
    return pl.pallas_call(
        kernel,
        out_shape=shapes if many else shapes[0],
        in_specs=[far if i in hbm else anywhere if i in unread else vmem for i in range(len(args))],
        out_specs=[far if out_hbm else vmem] * len(shapes) if many else vmem,
        scratch_shapes=list(scratch),
        compiler_params=pltpu.CompilerParams(vmem_limit_bytes=32 * 1024 * 1024),
    )(*args)


DEALT = (0, 2, 1, 3)


def rows_at(index, size):
    return pl.ds(pl.multiple_of(index * size, size), size)


def in_order(index, refs, ks=(0, 1, 3, 2)):
    for k, ref in zip(ks, refs, strict=True):
        yield lax.rem(index + 4 - k, 4), ref


def sum_in_order(slots_ref, index, refs, ks=(0, 1, 3, 2)):
    for place, ref in in_order(index, refs, ks):
        slots_ref[place] = ref[...]
    return (slots_ref[0] + slots_ref[1]) + (slots_ref[2] + slots_ref[3])


def scatter(whole_ref, index, refs):
    size = whole_ref.shape[0] // 4
    for k, ref in zip(DEALT, refs, strict=True):
        ref[...] = whole_ref[rows_at(lax.rem(index + k, 4), size), :]


def factor_kernel(qt_ref, cot_ref, q3_ref, own_ref, cot_out_ref, qt, sems):
    at, cut = lax.axis_index("y") * NZ + lax.axis_index("z"), 1024
    pairs = [(qt_ref.at[:, i : i + cut], qt.at[:, i : i + cut]) for i in range(0, D, cut)]
    pairs += [(qt_ref.at[:, rows_at(at, EB)], own_ref), (cot_ref, cot_out_ref)]
    copies = [pltpu.make_async_copy(a, b, sems.at[i]) for i, (a, b) in enumerate(pairs)]
    for copy in copies:
        copy.start()
    for i in range(D // cut):
        copies[i].wait()
        q3_ref[:, i * cut : (i + 1) * cut] = split3(qt[:, i * cut : (i + 1) * cut])
    copies[-2].wait()
    copies[-1].wait()


def project_kernel(cot_ref, other_ref, q3_ref, out_ref, both_ref):
    c = lax.axis_index("c")
    both_ref[rows_at(c, TB), :] = cot_ref[...]
    both_ref[rows_at(1 - c, TB), :] = other_ref[...]
    got = lax.dot_general(both_ref[...], q3_ref[...], NT, preferred_element_type=f32)
    got = got[:, :RANK] + (got[:, RANK : 2 * RANK] + got[:, 2 * RANK :])
    part = TB // 2
    for i in range(NC):
        own = got[i * TB : (i + 1) * TB]
        out_ref[i * part : (i + 1) * part, :] = jnp.concatenate([own[:part], own[part:]], axis=1)


def fetch_kernel(hidden_ref, err_ref, after_ref, h_ref, e_ref, sems):
    copies = [pltpu.make_async_copy(a, b, sems.at[i]) for i, (a, b) in enumerate(((hidden_ref, h_ref), (err_ref, e_ref)))]
    for copy in copies:
        copy.start()
    for copy in copies:
        copy.wait()


def columns_kernel(both_ref, after_ref, *out_refs):
    x = lax.axis_index("x")
    for k, ref in zip(DEALT, out_refs, strict=True):
        ref[...] = both_ref[:, rows_at(lax.rem(x + k, NX), CB)]


def join_x_kernel(own_ref, other_ref, out_ref):
    bit = lax.rem(lax.axis_index("x"), 2)
    out_ref[bit] = own_ref[...]
    out_ref[1 - bit] = other_ref[...]


def left_kernel(pair_ref, far_ref, hidden_ref, err_ref, q_ref, own_ref, a_ref, b_ref, c_ref, slots_ref, whole_ref):
    at = lax.axis_index("x") // 2
    slots_ref[at] = pair_ref[...]
    slots_ref[1 - at] = far_ref[...]
    packed = slots_ref[...].reshape(TOK // 2, 2 * RANK).T
    proj = jnp.concatenate([packed[:RANK], packed[RANK:]], axis=1)
    h = hidden_ref[...].reshape(NX * NC, 2, TB // 2, FB)
    h = jnp.concatenate([h[:, 0].reshape(TOK // 2, FB), h[:, 1].reshape(TOK // 2, FB)], axis=0)
    whole_ref[...] = dot3(split3(proj), h, NN) + dot3(split3(q_ref[...]), err_ref[...], NT)
    scatter(whole_ref, lax.axis_index("y"), (own_ref, a_ref, b_ref, c_ref))


def halve_kernel(own_ref, a_ref, b_ref, c_ref, after_ref, keep_ref, send_ref, slots_ref, both_ref):
    both_ref[...] = sum_in_order(slots_ref, lax.axis_index("y"), (own_ref, a_ref, b_ref, c_ref), DEALT)
    bit, half = lax.rem(lax.axis_index("z"), 2), keep_ref.shape[0]
    keep_ref[...] = both_ref[rows_at(bit, half), :]
    send_ref[...] = both_ref[rows_at(1 - bit, half), :]


def add_kernel(a_ref, b_ref, out_ref):
    out_ref[...] = a_ref[...] + b_ref[...]


def sum_z_kernel(own_ref, a_ref, b_ref, c_ref, out_ref, slots_ref):
    out_ref[...] = sum_in_order(slots_ref, lax.axis_index("z") // 2, (own_ref, a_ref, b_ref, c_ref))


def sum_z_after_kernel(own_ref, a_ref, b_ref, c_ref, *rest):
    sum_z_kernel(own_ref, a_ref, b_ref, c_ref, *rest[-2:])


def sum_x_kernel(own_ref, a_ref, b_ref, c_ref, out_ref, slots_ref):
    out_ref[...] = sum_in_order(slots_ref, lax.axis_index("x"), (own_ref, a_ref, b_ref, c_ref))


def join_z_kernel(own_ref, other_ref, out_ref):
    bit, half = lax.rem(lax.axis_index("z"), 2), own_ref.shape[0]
    out_ref[rows_at(bit, half), :] = own_ref[...]
    out_ref[rows_at(1 - bit, half), :] = other_ref[...]


def mixed_kernel(own_ref, a_ref, b_ref, c_ref, hidden_ref, err_ref, after_ref, p3_ref, keep_ref, send_ref, p_ref, all_ref):
    for place, ref in in_order(lax.axis_index("y"), (own_ref, a_ref, b_ref, c_ref)):
        p_ref[rows_at(place, RANK // NY), :] = ref[...]
    p3 = split3(p_ref[...])
    p3_ref[...] = p3
    all_ref[:, :TOK] = dot3(p3, hidden_ref[...], NT)
    all_ref[:, TOK:] = dot3(p3, err_ref[...], NN)
    gram = pack(gram3(p3))
    c, half = lax.axis_index("c"), RANK // 2
    for ref, core in ((keep_ref, c), (send_ref, 1 - c)):
        ref[:, : TOK + EB] = all_ref[rows_at(core, half), :]
        ref[:, TOK + EB :] = gram


def right_kernel(mixed_ref, cot_ref, a_cot_ref, b_cot_ref, c_cot_ref, own_ref, a_ref, b_ref, c_ref, slots_ref, whole_ref):
    x, at = lax.axis_index("x"), lax.axis_index("y") * NZ + lax.axis_index("z")
    for place, ref in in_order(x, (cot_ref, a_cot_ref, b_cot_ref, c_cot_ref), DEALT):
        slots_ref[place] = ref[...]
    part = dot3(split3(mixed_ref[:, :TOK]), slots_ref[...].reshape(TOK, CB), NN)
    err_q = mixed_ref[:, TOK : TOK + EB]
    here = [jnp.where(at == x * (CB // EB) + i, err_q, 0.0) for i in range(CB // EB)]
    whole_ref[...] = part + jnp.concatenate(here, axis=1)
    scatter(whole_ref, lax.axis_index("y"), (own_ref, a_ref, b_ref, c_ref))


def first_kernel(mixed_ref, after_ref, inv_ref):
    inv_ref[...] = inverse_factor(unpack(mixed_ref[:, TOK + EB :]))


def basis_kernel(inv_ref, p3_ref, b3_ref, gram_ref):
    b3 = split3(dot6(inv_ref[...], p3_ref[...]))
    b3_ref[...] = b3
    gram_ref[...] = pack(gram3(b3))


def sum_y_kernel(own_ref, a_ref, b_ref, c_ref, after_ref, out_ref, slots_ref):
    out_ref[...] = sum_in_order(slots_ref, lax.axis_index("y"), (own_ref, a_ref, b_ref, c_ref), DEALT)


def add_after_kernel(a_ref, b_ref, after_ref, out_ref):
    out_ref[...] = a_ref[...] + b_ref[...]


def block_kernel(own_ref, a_ref, b_ref, c_ref, gram_ref, other_ref, out_ref):
    for place, ref in in_order(lax.axis_index("y"), (own_ref, a_ref, b_ref, c_ref)):
        out_ref[rows_at(place, RANK // 2 // NY), :CB] = ref[...]
    out_ref[:, CB:] = gram_ref[...] + other_ref[...]


def second_kernel(own_ref, a_ref, b_ref, c_ref, inv_ref, total_ref, inverse_ref, slots_ref):
    for place, ref in in_order(lax.axis_index("x"), (own_ref, a_ref, b_ref, c_ref)):
        slots_ref[place] = ref[:, CB:]
    gram = unpack((slots_ref[0] + slots_ref[1]) + (slots_ref[2] + slots_ref[3]))
    rows = lax.broadcasted_iota(jnp.int32, (RANK, RANK), 0)
    cols = lax.broadcasted_iota(jnp.int32, (RANK, RANK), 1)
    off = gram - jnp.where(rows == cols, 1.0, 0.0).astype(f32)
    near = jnp.max(jnp.abs(off)) < 1e-3

    @pl.when(near)
    def _():
        inverse_ref[...] = near_inverse_factor(off)

    @pl.when(jnp.logical_not(near))
    def _():
        inverse_ref[...] = inverse_factor(gram)

    inverse = inverse_ref[...]
    total_ref[...] = jnp.dot(inverse, inv_ref[...], precision=HIGHEST, preferred_element_type=f32) * (1.0 / N_DP)


def new_kernel(*refs):
    total_ref, inverse_ref, b3_ref, out_ref, basis_ref, s_ref, whole_ref, scaled_ref, sems = refs[2 * NX :]
    x, c, half, total, copies = lax.axis_index("x"), lax.axis_index("c"), RANK // 2, total_ref[...], []
    for k, (place, ref) in enumerate(in_order(x, refs[:NX])):
        s_ref[k, rows_at(c, half), :] = ref[:, :CB]
        s_ref[k, rows_at(1 - c, half), :] = refs[NX + k][:, :CB]
        whole_ref[k] = dot6(total, split3(s_ref[k]))
        cols = rows_at(place, CB)
        copies.append(pltpu.make_async_copy(whole_ref.at[k], out_ref.at[:, cols], sems.at[k]))
        copies[-1].start()
        if k == 0:
            scaled_ref[...] = dot6(inverse_ref[...] * math.sqrt(FF), b3_ref[...])
            copies.append(pltpu.make_async_copy(scaled_ref, basis_ref, sems.at[NX]))
            copies[-1].start()
    for copy in copies:
        copy.wait()


def swap(a):
    return lax.ppermute(a, "c", [(0, 1), (1, 0)])


def pair_x(a, partner):
    return lax.ppermute(a, "x", [(x, partner(x)) for x in range(NX)])


def swap_z(a):
    return lax.ppermute(a, "z", [(i, i ^ 1) for i in range(NZ)])


def shift(a, axis, k):
    size, step = {"y": (NY, 1), "z": (NZ, 2), "x": (NX, 1)}[axis]
    return lax.ppermute(a, axis, [(i, (i + k * step) % size) for i in range(size)])


def deal(blocks, axis):
    return [blocks[0]] + [shift(block, axis, k) for k, block in zip(DEALT[1:], blocks[1:], strict=True)]


def share(block, axis):
    return [block] + [shift(block, axis, k) for k in (1, 3, 2)]


def shards(hidden, cotangent, error_buf, q_start):
    qt = q_start.T
    dma, half = pltpu.SemaphoreType.DMA, RANK // 2
    pinned = [pltpu.with_memory_space_constraint(a, pltpu.HBM) for a in (q_start.T, cotangent, hidden, error_buf)]
    other = swap(cotangent)
    q3, q_own, cot = call(
        factor_kernel, [((3 * RANK, D), bf16), ((RANK, EB), f32), ((TB, D), bf16)], *pinned[:2],
        scratch=[pltpu.VMEM((RANK, D), f32), dma((6,))], hbm=(0, 1),
    )
    proj, both = call(project_kernel, [((TB, 2 * RANK), f32), ((2 * TB, D), bf16)], cot, other, q3)
    hid, err = call(
        fetch_kernel, [((TOK, FB), bf16), ((FB, EB), bf16)], *pinned[2:], proj, scratch=[dma((2,))], hbm=(0, 1), unread=(2,)
    )
    pair = call(join_x_kernel, ((2, TB, 2 * RANK), f32), proj, pair_x(proj, lambda x: x ^ 1))
    quarter, eighth = ((RANK // NY, FB), f32), ((RANK // NY // 2, FB), f32)
    parts = call(
        left_kernel, [quarter] * 4, pair, pair_x(pair, lambda x: NX - 1 - x), hid, err, q_own,
        scratch=[pltpu.VMEM((2, 2, TB, 2 * RANK), f32), pltpu.VMEM((RANK, FB), f32)],
    )

    parts = deal(parts, "y")
    blocks = call(columns_kernel, [((2 * TB, CB), bf16)] * NX, both, parts[2], unread=(1,))
    cot = deal(blocks, "x")
    keep, send = call(
        halve_kernel, [eighth, eighth], *parts, cot[0], scratch=[pltpu.VMEM((4, *quarter[0]), f32), pltpu.VMEM(*quarter)], unread=(4,)
    )
    p = call(add_kernel, eighth, keep, swap_z(send))
    p = call(
        sum_z_after_kernel, eighth, *share(p, "z"), cot[2], cot[3], scratch=[pltpu.VMEM((4, *eighth[0]), f32)], unread=(4, 5)
    )
    p = call(join_z_kernel, quarter, p, swap_z(p))

    halves = ((half, TOK + EB + 2 * RANK), f32)
    p3, keep, send = call(
        mixed_kernel, [((3 * RANK, FB), bf16), halves, halves], *share(p, "y"), hid, err, cot[1],
        scratch=[pltpu.VMEM((RANK, FB), f32), pltpu.VMEM((RANK, TOK + EB), f32)], unread=(6,),
    )
    mixed = call(add_kernel, halves, keep, swap(send))
    mixed = call(sum_x_kernel, halves, *share(mixed, "x"), scratch=[pltpu.VMEM((4, *halves[0]), f32)])

    piece = ((half // NY, CB), f32)
    parts = call(
        right_kernel, [piece] * 4, mixed, *cot, scratch=[pltpu.VMEM((4, 2 * TB, CB), bf16), pltpu.VMEM((half, CB), f32)]
    )
    inverse = call(first_kernel, ((RANK, RANK), f32), mixed, parts[0], unread=(1,))
    s = call(sum_y_kernel, piece, *deal(parts, "y"), inverse, scratch=[pltpu.VMEM((4, *piece[0]), f32)], unread=(4,))
    b3, gram = call(basis_kernel, [((3 * RANK, FB), bf16), ((half, 2 * RANK), f32)], inverse, p3)
    s = call(add_after_kernel, piece, s, swap_z(s), gram, unread=(2,))
    s = call(sum_z_kernel, piece, *share(s, "z"), scratch=[pltpu.VMEM((4, *piece[0]), f32)])
    s = call(block_kernel, ((half, CB + 2 * RANK), f32), *share(s, "y"), gram, swap(gram))
    blocks = share(s, "x")
    square = ((RANK, RANK), f32)
    total, second = call(second_kernel, [square, square], *blocks, inverse, scratch=[pltpu.VMEM((4, half, 2 * RANK), f32)])
    wide_block = pltpu.VMEM((NX, RANK, CB), f32)
    q_new, scaled = call(
        new_kernel, [((RANK, D), f32), ((RANK, FB), f32)], *blocks, *[swap(b) for b in blocks], total, second, b3,
        scratch=[wide_block, wide_block, pltpu.VMEM((RANK, FB), f32), dma((NX + 1,))], out_hbm=True,
    )
    return scaled.T, q_new.T


def solution(mesh):
    fine = Mesh(mesh.devices.reshape(NY, NZ, NX, NC), ("y", "z", "x", "c"))
    dp, tensor = ("y", "z"), ("x", "c")
    placed = (P(dp, tensor), P(dp + tensor, None), P(tensor, dp), P())
    return jax.shard_map(
        shards, mesh=fine, in_specs=placed, out_specs=(P(tensor, None), P()), check_vma=False
    )
```

```python
import functools
import math

import jax
import jax.numpy as jnp
from jax import lax
from jax.experimental import pallas as pl
from jax.experimental.pallas import tpu as pltpu
from jax.sharding import Mesh
from jax.sharding import PartitionSpec as P

FF = 14336
D = 4096
RANK = 64
N_DP = 32
TOK = 256
NY, NZ, NX, NC = 4, 8, 4, 2
FB = FF // (NX * NC)
CB = D // NX
EB = D // N_DP
TB = TOK // (NX * NC)
f32, bf16 = jnp.float32, jnp.bfloat16
HIGHEST = lax.Precision.HIGHEST
NN = (((1,), (0,)), ((), ()))
NT = (((1,), (1,)), ((), ()))


def split3(a):
    hi = a.astype(bf16)
    rest = a - hi.astype(f32)
    mid = rest.astype(bf16)
    low = (rest - mid.astype(f32)).astype(bf16)
    return jnp.concatenate([hi, mid, low], axis=0)


def add3(a):
    n = a.shape[0] // 3
    return a[:n] + (a[n : 2 * n] + a[2 * n :])


def dot3(a, b, dims):
    return add3(lax.dot_general(a, b, dims, preferred_element_type=f32))


def gram3(a3):
    g = lax.dot_general(a3, a3, NT, preferred_element_type=f32)
    r = RANK
    g00, g01, g02 = g[:r, :r], g[:r, r : 2 * r], g[:r, 2 * r :]
    g10, g11, g20 = g[r : 2 * r, :r], g[r : 2 * r, r : 2 * r], g[2 * r :, :r]
    return g00 + ((g01 + g10) + (g11 + (g02 + g20)))


def wide(column):
    return jnp.broadcast_to(column, (8, 2 * RANK))


def inverse_factor(gram):
    rows = lax.broadcasted_iota(jnp.int32, (RANK, RANK), 0)
    cols = lax.broadcasted_iota(jnp.int32, (RANK, RANK), 1)
    both = jnp.concatenate([gram, jnp.where(rows == cols, 1.0, 0.0).astype(f32)], axis=1)
    sub = lax.broadcasted_iota(jnp.int32, (8, 2 * RANK), 0)
    count = RANK // 8
    tiles = [both[8 * i : 8 * i + 8] for i in range(count)]
    for p in range(count):
        columns = [[wide(tiles[i][:, 8 * p + j : 8 * p + j + 1]) for j in range(8)] for i in range(p, count)]
        panel, own, pivots, scales = tiles[p], columns[0], jnp.ones((8, 2 * RANK), f32), []
        for s in range(8):
            pivot = own[s][s : s + 1]
            scales.append(1.0 / pivot)
            pivots = jnp.where(sub == s, pivot, pivots)
            factor = jnp.where(sub > s, own[s] * scales[s], 0.0)
            panel = panel - factor * panel[s : s + 1]
            for j in range(s + 1, 8):
                own[j] = own[j] - factor * own[j][s : s + 1]
        for i in range(p + 1, count):
            below, tile = columns[i - p], tiles[i]
            for s in range(8):
                factor = below[s] * scales[s]
                tile = tile - factor * panel[s : s + 1]
                for j in range(s + 1, 8):
                    below[j] = below[j] - factor * own[j][s : s + 1]
            tiles[i] = tile
        tiles[p] = panel * lax.rsqrt(pivots)
    return jnp.concatenate(tiles, axis=0)[:, RANK:]


def near_inverse_factor(off):
    rows = lax.broadcasted_iota(jnp.int32, (RANK, RANK), 0)
    cols = lax.broadcasted_iota(jnp.int32, (RANK, RANK), 1)
    lower = jnp.where(rows > cols, 1.0, jnp.where(rows == cols, 0.5, 0.0)).astype(f32)
    first = off * lower
    second = -lower * lax.dot_general(first, first, NT, precision=HIGHEST, preferred_element_type=f32)
    square = jnp.dot(first, first, precision=HIGHEST, preferred_element_type=f32)
    eye = jnp.where(rows == cols, 1.0, 0.0).astype(f32)
    return eye - first + (square - second)


def dot6(a, b3):
    hi = a.astype(bf16).astype(f32)
    mid = (a - hi).astype(bf16).astype(f32)
    low = a - hi - mid
    one = jnp.concatenate([hi, hi, hi, mid], axis=1).astype(bf16)
    two = jnp.concatenate([mid, low], axis=1).astype(bf16)
    high, middle = b3[:RANK], b3[RANK : 2 * RANK]
    out = jnp.dot(one, jnp.concatenate([b3, high], axis=0), preferred_element_type=f32)
    return out + jnp.dot(two, jnp.concatenate([middle, high], axis=0), preferred_element_type=f32)


def pack(square):
    return jnp.concatenate([square[: RANK // 2], square[RANK // 2 :]], axis=1)


def unpack(packed):
    return jnp.concatenate([packed[:, :RANK], packed[:, RANK:]], axis=0)


def call(kernel, out_shape, *args, scratch=(), hbm=(), unread=(), out_hbm=False):
    vmem, far, anywhere = (pl.BlockSpec(memory_space=m) for m in (pltpu.VMEM, pltpu.HBM, pl.ANY))
    many = isinstance(out_shape, list)
    shapes = [jax.ShapeDtypeStruct(*s) for s in (out_shape if many else [out_shape])]
    return pl.pallas_call(
        kernel,
        out_shape=shapes if many else shapes[0],
        in_specs=[far if i in hbm else anywhere if i in unread else vmem for i in range(len(args))],
        out_specs=[far if out_hbm else vmem] * len(shapes) if many else vmem,
        scratch_shapes=list(scratch),
        compiler_params=pltpu.CompilerParams(vmem_limit_bytes=32 * 1024 * 1024),
    )(*args)


DEALT = (0, 2, 1, 3)


def rows_at(index, size):
    return pl.ds(pl.multiple_of(index * size, size), size)


def in_order(index, refs, ks=(0, 1, 3, 2)):
    for k, ref in zip(ks, refs, strict=True):
        yield lax.rem(index + 4 - k, 4), ref


def sum_in_order(slots_ref, index, refs, ks=(0, 1, 3, 2)):
    for place, ref in in_order(index, refs, ks):
        slots_ref[place] = ref[...]
    return (slots_ref[0] + slots_ref[1]) + (slots_ref[2] + slots_ref[3])


def scatter(whole_ref, index, refs):
    size = whole_ref.shape[0] // 4
    for k, ref in zip(DEALT, refs, strict=True):
        ref[...] = whole_ref[rows_at(lax.rem(index + k, 4), size), :]


def factor_kernel(qt_ref, cot_ref, q3_ref, own_ref, cot_out_ref, qt, sems):
    at, cut = lax.axis_index("y") * NZ + lax.axis_index("z"), 1024
    pairs = [(qt_ref.at[:, i : i + cut], qt.at[:, i : i + cut]) for i in range(0, D, cut)]
    pairs += [(qt_ref.at[:, rows_at(at, EB)], own_ref), (cot_ref, cot_out_ref)]
    copies = [pltpu.make_async_copy(a, b, sems.at[i]) for i, (a, b) in enumerate(pairs)]
    for copy in copies:
        copy.start()
    for i in range(D // cut):
        copies[i].wait()
        q3_ref[:, i * cut : (i + 1) * cut] = split3(qt[:, i * cut : (i + 1) * cut])
    copies[-2].wait()
    copies[-1].wait()


def project_kernel(cot_ref, other_ref, q3_ref, out_ref, both_ref):
    c = lax.axis_index("c")
    both_ref[rows_at(c, TB), :] = cot_ref[...]
    both_ref[rows_at(1 - c, TB), :] = other_ref[...]
    got = lax.dot_general(both_ref[...], q3_ref[...], NT, preferred_element_type=f32)
    got = got[:, :RANK] + (got[:, RANK : 2 * RANK] + got[:, 2 * RANK :])
    part = TB // 2
    for i in range(NC):
        own = got[i * TB : (i + 1) * TB]
        out_ref[i * part : (i + 1) * part, :] = jnp.concatenate([own[:part], own[part:]], axis=1)


def fetch_kernel(hidden_ref, err_ref, after_ref, h_ref, e_ref, sems):
    copies = [pltpu.make_async_copy(a, b, sems.at[i]) for i, (a, b) in enumerate(((hidden_ref, h_ref), (err_ref, e_ref)))]
    for copy in copies:
        copy.start()
    for copy in copies:
        copy.wait()


def columns_kernel(both_ref, after_ref, *out_refs):
    x = lax.axis_index("x")
    for k, ref in zip(DEALT, out_refs, strict=True):
        ref[...] = both_ref[:, rows_at(lax.rem(x + k, NX), CB)]


def join_x_kernel(own_ref, other_ref, out_ref):
    bit = lax.rem(lax.axis_index("x"), 2)
    out_ref[bit] = own_ref[...]
    out_ref[1 - bit] = other_ref[...]


def left_kernel(pair_ref, far_ref, hidden_ref, err_ref, q_ref, own_ref, a_ref, b_ref, c_ref, slots_ref, whole_ref):
    at = lax.axis_index("x") // 2
    slots_ref[at] = pair_ref[...]
    slots_ref[1 - at] = far_ref[...]
    packed = slots_ref[...].reshape(TOK // 2, 2 * RANK).T
    proj = jnp.concatenate([packed[:RANK], packed[RANK:]], axis=1)
    h = hidden_ref[...].reshape(NX * NC, 2, TB // 2, FB)
    h = jnp.concatenate([h[:, 0].reshape(TOK // 2, FB), h[:, 1].reshape(TOK // 2, FB)], axis=0)
    whole_ref[...] = dot3(split3(proj), h, NN) + dot3(split3(q_ref[...]), err_ref[...], NT)
    scatter(whole_ref, lax.axis_index("y"), (own_ref, a_ref, b_ref, c_ref))


def halve_kernel(own_ref, a_ref, b_ref, c_ref, after_ref, keep_ref, send_ref, slots_ref, both_ref):
    both_ref[...] = sum_in_order(slots_ref, lax.axis_index("y"), (own_ref, a_ref, b_ref, c_ref), DEALT)
    bit, half = lax.rem(lax.axis_index("z"), 2), keep_ref.shape[0]
    keep_ref[...] = both_ref[rows_at(bit, half), :]
    send_ref[...] = both_ref[rows_at(1 - bit, half), :]


def add_kernel(a_ref, b_ref, out_ref):
    out_ref[...] = a_ref[...] + b_ref[...]


def sum_z_kernel(own_ref, a_ref, b_ref, c_ref, out_ref, slots_ref):
    out_ref[...] = sum_in_order(slots_ref, lax.axis_index("z") // 2, (own_ref, a_ref, b_ref, c_ref))


def sum_z_after_kernel(own_ref, a_ref, b_ref, c_ref, *rest):
    sum_z_kernel(own_ref, a_ref, b_ref, c_ref, *rest[-2:])


def sum_x_kernel(own_ref, a_ref, b_ref, c_ref, out_ref, gram_ref, slots_ref):
    out_ref[...] = sum_in_order(slots_ref, lax.axis_index("x"), (own_ref, a_ref, b_ref, c_ref))
    gram_ref[...] = out_ref[3 * RANK :, :]


def join_z_kernel(own_ref, other_ref, out_ref):
    bit, half = lax.rem(lax.axis_index("z"), 2), own_ref.shape[0]
    out_ref[rows_at(bit, half), :] = own_ref[...]
    out_ref[rows_at(1 - bit, half), :] = other_ref[...]


def mixed_kernel(own_ref, a_ref, b_ref, c_ref, hidden_ref, err_ref, after_ref, p3_ref, all_ref, p_ref):
    for place, ref in in_order(lax.axis_index("y"), (own_ref, a_ref, b_ref, c_ref)):
        p_ref[rows_at(place, RANK // NY), :] = ref[...]
    p3 = split3(p_ref[...])
    p3_ref[...] = p3
    mixed = dot3(p3, hidden_ref[...], NT)
    all_ref[:RANK, :] = mixed[:, :EB]
    all_ref[RANK : 2 * RANK, :] = mixed[:, EB:]
    all_ref[2 * RANK : 3 * RANK, :] = dot3(p3, err_ref[...], NN)
    all_ref[3 * RANK :, :] = pack(gram3(p3))


def right_kernel(mixed_ref, cot_ref, a_cot_ref, b_cot_ref, c_cot_ref, own_ref, a_ref, b_ref, c_ref, slots_ref, whole_ref):
    x, at = lax.axis_index("x"), lax.axis_index("y") * NZ + lax.axis_index("z")
    for place, ref in in_order(x, (cot_ref, a_cot_ref, b_cot_ref, c_cot_ref), DEALT):
        slots_ref[place] = ref[...]
    mixed = jnp.concatenate([mixed_ref[:RANK, :], mixed_ref[RANK : 2 * RANK, :]], axis=1)
    part = dot3(split3(mixed), slots_ref[...].reshape(TOK, CB), NN)
    err_q = mixed_ref[2 * RANK : 3 * RANK, :]
    here = [jnp.where(at == x * (CB // EB) + i, err_q, 0.0) for i in range(CB // EB)]
    whole_ref[...] = part + jnp.concatenate(here, axis=1)
    scatter(whole_ref, lax.axis_index("y"), (own_ref, a_ref, b_ref, c_ref))


def first_kernel(own_ref, other_ref, after_ref, inv_ref):
    inv_ref[...] = inverse_factor(unpack(jnp.where(lax.axis_index("c") == 1, own_ref[...], other_ref[...])))


def basis_kernel(inv_ref, p3_ref, b3_ref, gram_ref):
    b3 = split3(dot6(inv_ref[...], p3_ref[...]))
    b3_ref[...] = b3
    gram_ref[...] = pack(gram3(b3))


def sum_y_kernel(own_ref, a_ref, b_ref, c_ref, after_ref, out_ref, slots_ref):
    out_ref[...] = sum_in_order(slots_ref, lax.axis_index("y"), (own_ref, a_ref, b_ref, c_ref), DEALT)


def add_after_kernel(a_ref, b_ref, after_ref, out_ref):
    out_ref[...] = a_ref[...] + b_ref[...]


def block_kernel(own_ref, a_ref, b_ref, c_ref, gram_ref, other_ref, out_ref):
    for place, ref in in_order(lax.axis_index("y"), (own_ref, a_ref, b_ref, c_ref)):
        out_ref[rows_at(place, RANK // NY), :CB] = ref[...]
    out_ref[: RANK // 2, CB:] = gram_ref[...] + other_ref[...]
    out_ref[RANK // 2 :, CB:] = jnp.zeros((RANK // 2, 2 * RANK), f32)


def second_kernel(*refs):
    inv_ref, total_ref, inverse_ref, slots_ref = refs[2 * NX :]
    core = lax.axis_index("c") == 1
    for k, (place, ref) in enumerate(in_order(lax.axis_index("x"), refs[:NX])):
        slots_ref[place] = jnp.where(core, ref[: RANK // 2, CB:], refs[NX + k][: RANK // 2, CB:])
    gram = unpack((slots_ref[0] + slots_ref[1]) + (slots_ref[2] + slots_ref[3]))
    rows = lax.broadcasted_iota(jnp.int32, (RANK, RANK), 0)
    cols = lax.broadcasted_iota(jnp.int32, (RANK, RANK), 1)
    off = gram - jnp.where(rows == cols, 1.0, 0.0).astype(f32)
    near = jnp.max(jnp.abs(off)) < 1e-3

    @pl.when(near)
    def _():
        inverse_ref[...] = near_inverse_factor(off)

    @pl.when(jnp.logical_not(near))
    def _():
        inverse_ref[...] = inverse_factor(gram)

    inverse = inverse_ref[...]
    total_ref[...] = jnp.dot(inverse, inv_ref[...], precision=HIGHEST, preferred_element_type=f32) * (1.0 / N_DP)


def new_kernel(*refs):
    total_ref, inverse_ref, b3_ref, out_ref, basis_ref, whole_ref, scaled_ref, sems = refs[2 * NX :]
    x, core, total, copies = lax.axis_index("x"), lax.axis_index("c") == 1, total_ref[...], []
    for k, (place, ref) in enumerate(in_order(x, refs[:NX])):
        block = jnp.where(core, ref[:, :CB], refs[NX + k][:, :CB])
        whole_ref[k] = dot6(total, split3(block))
        cols = rows_at(place, CB)
        copies.append(pltpu.make_async_copy(whole_ref.at[k], out_ref.at[:, cols], sems.at[k]))
        copies[-1].start()
        if k == 0:
            scaled_ref[...] = dot6(inverse_ref[...] * math.sqrt(FF), b3_ref[...])
            copies.append(pltpu.make_async_copy(scaled_ref, basis_ref, sems.at[NX]))
            copies[-1].start()
    for copy in copies:
        copy.wait()


def swap(a):
    return lax.ppermute(a, "c", [(0, 1), (1, 0)])


def pair_x(a, partner):
    return lax.ppermute(a, "x", [(x, partner(x)) for x in range(NX)])


def lead(a, step, idle):
    places = [(y, z, x) for y in range(NY) for z in range(NZ) for x in range(NX)]
    number = {place: i * NC for i, place in enumerate(places)}
    pairs = [(number[p] + c, number[move(*p)] + c) for p in places for c, move in ((0, idle), (1, step))]
    return lax.ppermute(a, ("y", "z", "x", "c"), pairs)


def lead_shift(a, axis, k):
    hop = 1 if k == 3 else -1
    if axis == "x":
        return lead(a, lambda y, z, x: (y, z, (x + k) % NX), lambda y, z, x: ((y + hop) % NY, z, x))

    def step(y, z, x):
        return ((y + k) % NY, z, x) if axis == "y" else (y, (z + 2 * k) % NZ, x)

    return lead(a, step, lambda y, z, x: (y, z, (x + hop) % NX))


def lead_swap_z(a):
    return lead(a, lambda y, z, x: (y, z ^ 1, x), lambda y, z, x: (y, z, x ^ 1))


def swap_z(a):
    return lax.ppermute(a, "z", [(i, i ^ 1) for i in range(NZ)])


def shift(a, axis, k):
    size, step = {"y": (NY, 1), "z": (NZ, 2), "x": (NX, 1)}[axis]
    return lax.ppermute(a, axis, [(i, (i + k * step) % size) for i in range(size)])


def deal(blocks, axis, shift=shift):
    return [blocks[0]] + [shift(block, axis, k) for k, block in zip(DEALT[1:], blocks[1:], strict=True)]


def share(block, axis, shift=shift):
    return [block] + [shift(block, axis, k) for k in (1, 3, 2)]


def shards(hidden, cotangent, error_buf, q_start):
    qt = q_start.T
    dma, half = pltpu.SemaphoreType.DMA, RANK // 2
    pinned = [pltpu.with_memory_space_constraint(a, pltpu.HBM) for a in (q_start.T, cotangent, hidden, error_buf)]
    other = swap(cotangent)
    q3, q_own, cot = call(
        factor_kernel, [((3 * RANK, D), bf16), ((RANK, EB), f32), ((TB, D), bf16)], *pinned[:2],
        scratch=[pltpu.VMEM((RANK, D), f32), dma((6,))], hbm=(0, 1),
    )
    proj, both = call(project_kernel, [((TB, 2 * RANK), f32), ((2 * TB, D), bf16)], cot, other, q3)
    hid, err = call(
        fetch_kernel, [((TOK, FB), bf16), ((FB, EB), bf16)], *pinned[2:], proj, scratch=[dma((2,))], hbm=(0, 1), unread=(2,)
    )
    pair = call(join_x_kernel, ((2, TB, 2 * RANK), f32), proj, pair_x(proj, lambda x: x ^ 1))
    quarter, eighth = ((RANK // NY, FB), f32), ((RANK // NY // 2, FB), f32)
    parts = call(
        left_kernel, [quarter] * 4, pair, pair_x(pair, lambda x: NX - 1 - x), hid, err, q_own,
        scratch=[pltpu.VMEM((2, 2, TB, 2 * RANK), f32), pltpu.VMEM((RANK, FB), f32)],
    )

    parts = deal(parts, "y")
    blocks = call(columns_kernel, [((2 * TB, CB), bf16)] * NX, both, parts[2], unread=(1,))
    cot = deal(blocks, "x")
    keep, send = call(
        halve_kernel, [eighth, eighth], *parts, cot[0], scratch=[pltpu.VMEM((4, *quarter[0]), f32), pltpu.VMEM(*quarter)], unread=(4,)
    )
    p = call(add_kernel, eighth, keep, swap_z(send))
    p = call(
        sum_z_after_kernel, eighth, *share(p, "z"), cot[2], cot[3], scratch=[pltpu.VMEM((4, *eighth[0]), f32)], unread=(4, 5)
    )
    p = call(join_z_kernel, quarter, p, swap_z(p))

    mix, small = ((3 * RANK + half, EB), f32), ((half, 2 * RANK), f32)
    p3, mixed = call(
        mixed_kernel, [((3 * RANK, FB), bf16), mix], *share(p, "y"), hid, err, cot[1], scratch=[pltpu.VMEM((RANK, FB), f32)], unread=(6,)
    )
    mixed = call(add_kernel, mix, mixed, swap(mixed))
    mixed, gram = call(sum_x_kernel, [mix, small], *share(mixed, "x", lead_shift), scratch=[pltpu.VMEM((4, *mix[0]), f32)])

    piece, slots = ((RANK // NY, CB), f32), pltpu.VMEM((4, RANK // NY, CB), f32)
    parts = call(
        right_kernel, [piece] * 4, mixed, *cot, scratch=[pltpu.VMEM((4, 2 * TB, CB), bf16), pltpu.VMEM((RANK, CB), f32)]
    )
    inverse = call(first_kernel, ((RANK, RANK), f32), gram, swap(gram), parts[0], unread=(2,))
    s = call(sum_y_kernel, piece, *deal(parts, "y", lead_shift), inverse, scratch=[slots], unread=(4,))
    b3, gram = call(basis_kernel, [((3 * RANK, FB), bf16), small], inverse, p3)
    s = call(add_after_kernel, piece, s, lead_swap_z(s), gram, unread=(2,))
    s = call(sum_z_kernel, piece, *share(s, "z", lead_shift), scratch=[slots])
    s = call(block_kernel, ((RANK, CB + 2 * RANK), f32), *share(s, "y", lead_shift), gram, swap(gram))
    blocks = share(s, "x", lead_shift)
    blocks += [swap(b) for b in blocks]
    square = ((RANK, RANK), f32)
    total, second = call(second_kernel, [square, square], *blocks, inverse, scratch=[pltpu.VMEM((4, *small[0]), f32)])
    q_new, scaled = call(
        new_kernel, [((RANK, D), f32), ((RANK, FB), f32)], *blocks, total, second, b3,
        scratch=[pltpu.VMEM((NX, RANK, CB), f32), pltpu.VMEM((RANK, FB), f32), dma((NX + 1,))], out_hbm=True,
    )
    return scaled.T, q_new.T


def solution(mesh):
    fine = Mesh(mesh.devices.reshape(NY, NZ, NX, NC), ("y", "z", "x", "c"))
    dp, tensor = ("y", "z"), ("x", "c")
    placed = (P(dp, tensor), P(dp + tensor, None), P(tensor, dp), P())
    return jax.shard_map(
        shards, mesh=fine, in_specs=placed, out_specs=(P(tensor, None), P()), check_vma=False
    )
```

```python
import functools
import math

import jax
import jax.numpy as jnp
from jax import lax
from jax.experimental import pallas as pl
from jax.experimental.pallas import tpu as pltpu
from jax.sharding import Mesh
from jax.sharding import PartitionSpec as P

FF = 14336
D = 4096
RANK = 64
N_DP = 32
TOK = 256
NY, NZ, NX, NC = 4, 8, 4, 2
FB = FF // (NX * NC)
CB = D // NX
EB = D // N_DP
TB = TOK // (NX * NC)
f32, bf16 = jnp.float32, jnp.bfloat16
HIGHEST = lax.Precision.HIGHEST
NN = (((1,), (0,)), ((), ()))
NT = (((1,), (1,)), ((), ()))


def split3(a):
    hi = a.astype(bf16)
    rest = a - hi.astype(f32)
    mid = rest.astype(bf16)
    low = (rest - mid.astype(f32)).astype(bf16)
    return jnp.concatenate([hi, mid, low], axis=0)


def add3(a):
    n = a.shape[0] // 3
    return a[:n] + (a[n : 2 * n] + a[2 * n :])


def dot3(a, b, dims):
    return add3(lax.dot_general(a, b, dims, preferred_element_type=f32))


def gram3(a3):
    g = lax.dot_general(a3, a3, NT, preferred_element_type=f32)
    r = RANK
    g00, g01, g02 = g[:r, :r], g[:r, r : 2 * r], g[:r, 2 * r :]
    g10, g11, g20 = g[r : 2 * r, :r], g[r : 2 * r, r : 2 * r], g[2 * r :, :r]
    return g00 + ((g01 + g10) + (g11 + (g02 + g20)))


def wide(column):
    return jnp.broadcast_to(column, (8, 2 * RANK))


def inverse_factor(gram):
    rows = lax.broadcasted_iota(jnp.int32, (RANK, RANK), 0)
    cols = lax.broadcasted_iota(jnp.int32, (RANK, RANK), 1)
    both = jnp.concatenate([gram, jnp.where(rows == cols, 1.0, 0.0).astype(f32)], axis=1)
    sub = lax.broadcasted_iota(jnp.int32, (8, 2 * RANK), 0)
    count = RANK // 8
    tiles = [both[8 * i : 8 * i + 8] for i in range(count)]
    for p in range(count):
        columns = [[wide(tiles[i][:, 8 * p + j : 8 * p + j + 1]) for j in range(8)] for i in range(p, count)]
        panel, own, pivots, scales = tiles[p], columns[0], jnp.ones((8, 2 * RANK), f32), []
        for s in range(8):
            pivot = own[s][s : s + 1]
            scales.append(1.0 / pivot)
            pivots = jnp.where(sub == s, pivot, pivots)
            factor = jnp.where(sub > s, own[s] * scales[s], 0.0)
            panel = panel - factor * panel[s : s + 1]
            for j in range(s + 1, 8):
                own[j] = own[j] - factor * own[j][s : s + 1]
        for i in range(p + 1, count):
            below, tile = columns[i - p], tiles[i]
            for s in range(8):
                factor = below[s] * scales[s]
                tile = tile - factor * panel[s : s + 1]
                for j in range(s + 1, 8):
                    below[j] = below[j] - factor * own[j][s : s + 1]
            tiles[i] = tile
        tiles[p] = panel * lax.rsqrt(pivots)
    return jnp.concatenate(tiles, axis=0)[:, RANK:]


def near_inverse_factor(off):
    rows = lax.broadcasted_iota(jnp.int32, (RANK, RANK), 0)
    cols = lax.broadcasted_iota(jnp.int32, (RANK, RANK), 1)
    lower = jnp.where(rows > cols, 1.0, jnp.where(rows == cols, 0.5, 0.0)).astype(f32)
    first = off * lower
    second = -lower * lax.dot_general(first, first, NT, precision=HIGHEST, preferred_element_type=f32)
    square = jnp.dot(first, first, precision=HIGHEST, preferred_element_type=f32)
    eye = jnp.where(rows == cols, 1.0, 0.0).astype(f32)
    return eye - first + (square - second)


def dot6(a, b3):
    hi = a.astype(bf16).astype(f32)
    mid = (a - hi).astype(bf16).astype(f32)
    low = a - hi - mid
    one = jnp.concatenate([hi, hi, hi, mid], axis=1).astype(bf16)
    two = jnp.concatenate([mid, low], axis=1).astype(bf16)
    high, middle = b3[:RANK], b3[RANK : 2 * RANK]
    out = jnp.dot(one, jnp.concatenate([b3, high], axis=0), preferred_element_type=f32)
    return out + jnp.dot(two, jnp.concatenate([middle, high], axis=0), preferred_element_type=f32)


def pack(square):
    return jnp.concatenate([square[: RANK // 2], square[RANK // 2 :]], axis=1)


def unpack(packed):
    return jnp.concatenate([packed[:, :RANK], packed[:, RANK:]], axis=0)


def call(kernel, out_shape, *args, scratch=(), hbm=(), unread=(), out_hbm=False):
    vmem, far, anywhere = (pl.BlockSpec(memory_space=m) for m in (pltpu.VMEM, pltpu.HBM, pl.ANY))
    many = isinstance(out_shape, list)
    shapes = [jax.ShapeDtypeStruct(*s) for s in (out_shape if many else [out_shape])]
    return pl.pallas_call(
        kernel,
        out_shape=shapes if many else shapes[0],
        in_specs=[far if i in hbm else anywhere if i in unread else vmem for i in range(len(args))],
        out_specs=[far if out_hbm else vmem] * len(shapes) if many else vmem,
        scratch_shapes=list(scratch),
        compiler_params=pltpu.CompilerParams(vmem_limit_bytes=32 * 1024 * 1024),
    )(*args)


DEALT = (0, 2, 1, 3)


def rows_at(index, size):
    return pl.ds(pl.multiple_of(index * size, size), size)


def in_order(index, refs, ks=(0, 1, 3, 2)):
    for k, ref in zip(ks, refs, strict=True):
        yield lax.rem(index + 4 - k, 4), ref


def sum_in_order(slots_ref, index, refs, ks=(0, 1, 3, 2)):
    for place, ref in in_order(index, refs, ks):
        slots_ref[place] = ref[...]
    return (slots_ref[0] + slots_ref[1]) + (slots_ref[2] + slots_ref[3])


def scatter(whole_ref, index, refs):
    size = whole_ref.shape[0] // 4
    for k, ref in zip(DEALT, refs, strict=True):
        ref[...] = whole_ref[rows_at(lax.rem(index + k, 4), size), :]


def factor_kernel(qt_ref, cot_ref, q3_ref, own_ref, cot_out_ref, qt, sems):
    at, cut = lax.axis_index("y") * NZ + lax.axis_index("z"), 1024
    pairs = [(qt_ref.at[:, i : i + cut], qt.at[:, i : i + cut]) for i in range(0, D, cut)]
    pairs += [(qt_ref.at[:, rows_at(at, EB)], own_ref), (cot_ref, cot_out_ref)]
    copies = [pltpu.make_async_copy(a, b, sems.at[i]) for i, (a, b) in enumerate(pairs)]
    for copy in copies:
        copy.start()
    for i in range(D // cut):
        copies[i].wait()
        q3_ref[:, i * cut : (i + 1) * cut] = split3(qt[:, i * cut : (i + 1) * cut])
    copies[-2].wait()
    copies[-1].wait()


def project_kernel(cot_ref, other_ref, q3_ref, out_ref, both_ref):
    c = lax.axis_index("c")
    both_ref[rows_at(c, TB), :] = cot_ref[...]
    both_ref[rows_at(1 - c, TB), :] = other_ref[...]
    got = lax.dot_general(both_ref[...], q3_ref[...], NT, preferred_element_type=f32)
    got = got[:, :RANK] + (got[:, RANK : 2 * RANK] + got[:, 2 * RANK :])
    part = TB // 2
    for i in range(NC):
        own = got[i * TB : (i + 1) * TB]
        out_ref[i * part : (i + 1) * part, :] = jnp.concatenate([own[:part], own[part:]], axis=1)


def fetch_kernel(hidden_ref, err_ref, after_ref, h_ref, e_ref, sems):
    copies = [pltpu.make_async_copy(a, b, sems.at[i]) for i, (a, b) in enumerate(((hidden_ref, h_ref), (err_ref, e_ref)))]
    for copy in copies:
        copy.start()
    for copy in copies:
        copy.wait()


def columns_kernel(both_ref, after_ref, *out_refs):
    x = lax.axis_index("x")
    for k, ref in zip(DEALT, out_refs, strict=True):
        ref[...] = both_ref[:, rows_at(lax.rem(x + k, NX), CB)]


def join_x_kernel(own_ref, other_ref, out_ref):
    bit = lax.rem(lax.axis_index("x"), 2)
    out_ref[bit] = own_ref[...]
    out_ref[1 - bit] = other_ref[...]


def left_kernel(pair_ref, far_ref, hidden_ref, err_ref, q_ref, own_ref, a_ref, b_ref, c_ref, slots_ref, whole_ref):
    at = lax.axis_index("x") // 2
    slots_ref[at] = pair_ref[...]
    slots_ref[1 - at] = far_ref[...]
    packed = slots_ref[...].reshape(TOK // 2, 2 * RANK).T
    proj = jnp.concatenate([packed[:RANK], packed[RANK:]], axis=1)
    h = hidden_ref[...].reshape(NX * NC, 2, TB // 2, FB)
    h = jnp.concatenate([h[:, 0].reshape(TOK // 2, FB), h[:, 1].reshape(TOK // 2, FB)], axis=0)
    whole_ref[...] = dot3(split3(proj), h, NN) + dot3(split3(q_ref[...]), err_ref[...], NT)
    scatter(whole_ref, lax.axis_index("y"), (own_ref, a_ref, b_ref, c_ref))


def halve_kernel(own_ref, a_ref, b_ref, c_ref, after_ref, keep_ref, send_ref, slots_ref, both_ref):
    both_ref[...] = sum_in_order(slots_ref, lax.axis_index("y"), (own_ref, a_ref, b_ref, c_ref), DEALT)
    bit, half = lax.rem(lax.axis_index("z"), 2), keep_ref.shape[0]
    keep_ref[...] = both_ref[rows_at(bit, half), :]
    send_ref[...] = both_ref[rows_at(1 - bit, half), :]


def add_kernel(a_ref, b_ref, out_ref):
    out_ref[...] = a_ref[...] + b_ref[...]


def sum_z_kernel(own_ref, a_ref, b_ref, c_ref, out_ref, slots_ref):
    out_ref[...] = sum_in_order(slots_ref, lax.axis_index("z") // 2, (own_ref, a_ref, b_ref, c_ref))


def sum_z_after_kernel(own_ref, a_ref, b_ref, c_ref, *rest):
    sum_z_kernel(own_ref, a_ref, b_ref, c_ref, *rest[-2:])


def sum_x_kernel(own_ref, a_ref, b_ref, c_ref, out_ref, gram_ref, slots_ref):
    out_ref[...] = sum_in_order(slots_ref, lax.axis_index("x"), (own_ref, a_ref, b_ref, c_ref))
    gram_ref[...] = out_ref[3 * RANK :, :]


def join_z_kernel(own_ref, other_ref, out_ref):
    bit, half = lax.rem(lax.axis_index("z"), 2), own_ref.shape[0]
    out_ref[rows_at(bit, half), :] = own_ref[...]
    out_ref[rows_at(1 - bit, half), :] = other_ref[...]


def mixed_kernel(own_ref, a_ref, b_ref, c_ref, hidden_ref, err_ref, after_ref, p3_ref, all_ref, p_ref):
    for place, ref in in_order(lax.axis_index("y"), (own_ref, a_ref, b_ref, c_ref)):
        p_ref[rows_at(place, RANK // NY), :] = ref[...]
    p3 = split3(p_ref[...])
    p3_ref[...] = p3
    mixed = dot3(p3, hidden_ref[...], NT)
    all_ref[:RANK, :] = mixed[:, :EB]
    all_ref[RANK : 2 * RANK, :] = mixed[:, EB:]
    all_ref[2 * RANK : 3 * RANK, :] = dot3(p3, err_ref[...], NN)
    all_ref[3 * RANK :, :] = pack(gram3(p3))


def right_kernel(mixed_ref, cot_ref, a_cot_ref, b_cot_ref, c_cot_ref, own_ref, a_ref, b_ref, c_ref, slots_ref, whole_ref):
    x, at = lax.axis_index("x"), lax.axis_index("y") * NZ + lax.axis_index("z")
    for place, ref in in_order(x, (cot_ref, a_cot_ref, b_cot_ref, c_cot_ref), DEALT):
        slots_ref[place] = ref[...]
    mixed = jnp.concatenate([mixed_ref[:RANK, :], mixed_ref[RANK : 2 * RANK, :]], axis=1)
    part = dot3(split3(mixed), slots_ref[...].reshape(TOK, CB), NN)
    err_q = mixed_ref[2 * RANK : 3 * RANK, :]
    here = [jnp.where(at == x * (CB // EB) + i, err_q, 0.0) for i in range(CB // EB)]
    whole_ref[...] = part + jnp.concatenate(here, axis=1)
    scatter(whole_ref, lax.axis_index("y"), (own_ref, a_ref, b_ref, c_ref))


def first_kernel(own_ref, other_ref, after_ref, inv_ref):
    inv_ref[...] = inverse_factor(unpack(jnp.where(lax.axis_index("c") == 1, own_ref[...], other_ref[...])))


def basis_kernel(inv_ref, p3_ref, after_ref, b3_ref, gram_ref):
    b3 = split3(dot6(inv_ref[...], p3_ref[...]))
    b3_ref[...] = b3
    gram_ref[...] = pack(gram3(b3))


def sum_y_kernel(own_ref, a_ref, b_ref, c_ref, after_ref, out_ref, slots_ref):
    out_ref[...] = sum_in_order(slots_ref, lax.axis_index("y"), (own_ref, a_ref, b_ref, c_ref), DEALT)


def add_after_kernel(a_ref, b_ref, after_ref, out_ref):
    out_ref[...] = a_ref[...] + b_ref[...]


def block_kernel(own_ref, a_ref, b_ref, c_ref, after_ref, keep_ref, send_ref, whole_ref):
    for place, ref in in_order(lax.axis_index("y"), (own_ref, a_ref, b_ref, c_ref)):
        whole_ref[rows_at(place, RANK // NY), :] = ref[...]
    c, half = lax.axis_index("c"), RANK // 2
    keep_ref[...] = whole_ref[rows_at(c, half), :]
    send_ref[...] = whole_ref[rows_at(1 - c, half), :]


def hand_kernel(keep_ref, got_ref, gram_ref, other_ref, out_ref):
    out_ref[:, :CB] = jnp.where(lax.axis_index("c") == 1, keep_ref[...], got_ref[...])
    out_ref[:, CB:] = gram_ref[...] + other_ref[...]


def second_kernel(own_ref, a_ref, b_ref, c_ref, inv_ref, total_ref, inverse_ref, slots_ref):
    for place, ref in in_order(lax.axis_index("x"), (own_ref, a_ref, b_ref, c_ref)):
        slots_ref[place] = ref[:, CB:]
    gram = unpack((slots_ref[0] + slots_ref[1]) + (slots_ref[2] + slots_ref[3]))
    rows = lax.broadcasted_iota(jnp.int32, (RANK, RANK), 0)
    cols = lax.broadcasted_iota(jnp.int32, (RANK, RANK), 1)
    off = gram - jnp.where(rows == cols, 1.0, 0.0).astype(f32)
    near = jnp.max(jnp.abs(off)) < 1e-3

    @pl.when(near)
    def _():
        inverse_ref[...] = near_inverse_factor(off)

    @pl.when(jnp.logical_not(near))
    def _():
        inverse_ref[...] = inverse_factor(gram)

    inverse = inverse_ref[...]
    total_ref[...] = jnp.dot(inverse, inv_ref[...], precision=HIGHEST, preferred_element_type=f32) * (1.0 / N_DP)


def new_kernel(*refs):
    total_ref, inverse_ref, b3_ref, out_ref, basis_ref, s_ref, whole_ref, scaled_ref, sems = refs[2 * NX :]
    x, c, half, total, copies = lax.axis_index("x"), lax.axis_index("c"), RANK // 2, total_ref[...], []
    for k, (place, ref) in enumerate(in_order(x, refs[:NX])):
        s_ref[k, rows_at(c, half), :] = ref[:, :CB]
        s_ref[k, rows_at(1 - c, half), :] = refs[NX + k][:, :CB]
        whole_ref[k] = dot6(total, split3(s_ref[k]))
        cols = rows_at(place, CB)
        copies.append(pltpu.make_async_copy(whole_ref.at[k], out_ref.at[:, cols], sems.at[k]))
        copies[-1].start()
        if k == 0:
            scaled_ref[...] = dot6(inverse_ref[...] * math.sqrt(FF), b3_ref[...])
            copies.append(pltpu.make_async_copy(scaled_ref, basis_ref, sems.at[NX]))
            copies[-1].start()
    for copy in copies:
        copy.wait()


def swap(a):
    return lax.ppermute(a, "c", [(0, 1), (1, 0)])


def pair_x(a, partner):
    return lax.ppermute(a, "x", [(x, partner(x)) for x in range(NX)])


def lead(a, step, idle):
    places = [(y, z, x) for y in range(NY) for z in range(NZ) for x in range(NX)]
    number = {place: i * NC for i, place in enumerate(places)}
    pairs = [(number[p] + c, number[move(*p)] + c) for p in places for c, move in ((0, idle), (1, step))]
    return lax.ppermute(a, ("y", "z", "x", "c"), pairs)


def lead_shift(a, axis, k):
    hop = 1 if k == 3 else -1
    if axis == "x":
        return lead(a, lambda y, z, x: (y, z, (x + k) % NX), lambda y, z, x: ((y + hop) % NY, z, x))

    def step(y, z, x):
        return ((y + k) % NY, z, x) if axis == "y" else (y, (z + 2 * k) % NZ, x)

    return lead(a, step, lambda y, z, x: (y, z, (x + hop) % NX))


def lead_swap_z(a):
    return lead(a, lambda y, z, x: (y, z ^ 1, x), lambda y, z, x: (y, z, x ^ 1))


def swap_z(a):
    return lax.ppermute(a, "z", [(i, i ^ 1) for i in range(NZ)])


def shift(a, axis, k):
    size, step = {"y": (NY, 1), "z": (NZ, 2), "x": (NX, 1)}[axis]
    return lax.ppermute(a, axis, [(i, (i + k * step) % size) for i in range(size)])


def deal(blocks, axis, shift=shift):
    return [blocks[0]] + [shift(block, axis, k) for k, block in zip(DEALT[1:], blocks[1:], strict=True)]


def share(block, axis, shift=shift):
    return [block] + [shift(block, axis, k) for k in (1, 3, 2)]


def shards(hidden, cotangent, error_buf, q_start):
    qt = q_start.T
    dma, half = pltpu.SemaphoreType.DMA, RANK // 2
    pinned = [pltpu.with_memory_space_constraint(a, pltpu.HBM) for a in (q_start.T, cotangent, hidden, error_buf)]
    other = swap(cotangent)
    q3, q_own, cot = call(
        factor_kernel, [((3 * RANK, D), bf16), ((RANK, EB), f32), ((TB, D), bf16)], *pinned[:2],
        scratch=[pltpu.VMEM((RANK, D), f32), dma((6,))], hbm=(0, 1),
    )
    proj, both = call(project_kernel, [((TB, 2 * RANK), f32), ((2 * TB, D), bf16)], cot, other, q3)
    hid, err = call(
        fetch_kernel, [((TOK, FB), bf16), ((FB, EB), bf16)], *pinned[2:], proj, scratch=[dma((2,))], hbm=(0, 1), unread=(2,)
    )
    pair = call(join_x_kernel, ((2, TB, 2 * RANK), f32), proj, pair_x(proj, lambda x: x ^ 1))
    quarter, eighth = ((RANK // NY, FB), f32), ((RANK // NY // 2, FB), f32)
    parts = call(
        left_kernel, [quarter] * 4, pair, pair_x(pair, lambda x: NX - 1 - x), hid, err, q_own,
        scratch=[pltpu.VMEM((2, 2, TB, 2 * RANK), f32), pltpu.VMEM((RANK, FB), f32)],
    )

    parts = deal(parts, "y")
    blocks = call(columns_kernel, [((2 * TB, CB), bf16)] * NX, both, parts[2], unread=(1,))
    cot = deal(blocks, "x")
    keep, send = call(
        halve_kernel, [eighth, eighth], *parts, cot[0], scratch=[pltpu.VMEM((4, *quarter[0]), f32), pltpu.VMEM(*quarter)], unread=(4,)
    )
    p = call(add_kernel, eighth, keep, swap_z(send))
    p = call(
        sum_z_after_kernel, eighth, *share(p, "z"), cot[2], cot[3], scratch=[pltpu.VMEM((4, *eighth[0]), f32)], unread=(4, 5)
    )
    p = call(join_z_kernel, quarter, p, swap_z(p))

    mix, small = ((3 * RANK + half, EB), f32), ((half, 2 * RANK), f32)
    p3, mixed = call(
        mixed_kernel, [((3 * RANK, FB), bf16), mix], *share(p, "y"), hid, err, cot[1], scratch=[pltpu.VMEM((RANK, FB), f32)], unread=(6,)
    )
    mixed = call(add_kernel, mix, mixed, swap(mixed))
    mixed, gram = call(sum_x_kernel, [mix, small], *share(mixed, "x", lead_shift), scratch=[pltpu.VMEM((4, *mix[0]), f32)])

    piece, slots = ((RANK // NY, CB), f32), pltpu.VMEM((4, RANK // NY, CB), f32)
    parts = call(
        right_kernel, [piece] * 4, mixed, *cot, scratch=[pltpu.VMEM((4, 2 * TB, CB), bf16), pltpu.VMEM((RANK, CB), f32)]
    )
    gram_other = swap(gram)
    s = call(sum_y_kernel, piece, *deal(parts, "y", lead_shift), gram_other, scratch=[slots], unread=(4,))
    inverse = call(first_kernel, ((RANK, RANK), f32), gram, gram_other, s, unread=(2,))
    s = call(add_after_kernel, piece, s, lead_swap_z(s), inverse, unread=(2,))
    b3, gram = call(basis_kernel, [((3 * RANK, FB), bf16), small], inverse, p3, s, unread=(2,))
    s = call(sum_z_after_kernel, piece, *share(s, "z", lead_shift), gram, scratch=[slots], unread=(4,))
    rows = ((half, CB), f32)
    gram_other = swap(gram)
    keep, send = call(
        block_kernel, [rows, rows], *share(s, "y", lead_shift), gram_other, scratch=[pltpu.VMEM((RANK, CB), f32)], unread=(4,)
    )
    s = call(hand_kernel, ((half, CB + 2 * RANK), f32), keep, swap(send), gram, gram_other)
    blocks = share(s, "x")
    blocks += [swap(b) for b in blocks]
    square = ((RANK, RANK), f32)
    total, second = call(second_kernel, [square, square], *blocks[:NX], inverse, scratch=[pltpu.VMEM((4, *small[0]), f32)])
    wide_block = pltpu.VMEM((NX, RANK, CB), f32)
    q_new, scaled = call(
        new_kernel, [((RANK, D), f32), ((RANK, FB), f32)], *blocks, total, second, b3,
        scratch=[wide_block, wide_block, pltpu.VMEM((RANK, FB), f32), dma((NX + 1,))], out_hbm=True,
    )
    return scaled.T, q_new.T


def solution(mesh):
    fine = Mesh(mesh.devices.reshape(NY, NZ, NX, NC), ("y", "z", "x", "c"))
    dp, tensor = ("y", "z"), ("x", "c")
    placed = (P(dp, tensor), P(dp + tensor, None), P(tensor, dp), P())
    return jax.shard_map(
        shards, mesh=fine, in_specs=placed, out_specs=(P(tensor, None), P()), check_vma=False
    )
```

```python
import functools
import math

import jax
import jax.numpy as jnp
from jax import lax
from jax.experimental import pallas as pl
from jax.experimental.pallas import tpu as pltpu
from jax.sharding import Mesh
from jax.sharding import PartitionSpec as P

FF = 14336
D = 4096
RANK = 64
N_DP = 32
TOK = 256
NY, NZ, NX, NC = 4, 8, 4, 2
FB = FF // (NX * NC)
CB = D // NX
EB = D // N_DP
TB = TOK // (NX * NC)
f32, bf16 = jnp.float32, jnp.bfloat16
HIGHEST = lax.Precision.HIGHEST
NN = (((1,), (0,)), ((), ()))
NT = (((1,), (1,)), ((), ()))


def split3(a):
    hi = a.astype(bf16)
    rest = a - hi.astype(f32)
    mid = rest.astype(bf16)
    low = (rest - mid.astype(f32)).astype(bf16)
    return jnp.concatenate([hi, mid, low], axis=0)


def add3(a):
    n = a.shape[0] // 3
    return a[:n] + (a[n : 2 * n] + a[2 * n :])


def dot3(a, b, dims):
    return add3(lax.dot_general(a, b, dims, preferred_element_type=f32))


def gram3(a3):
    g = lax.dot_general(a3, a3, NT, preferred_element_type=f32)
    r = RANK
    g00, g01, g02 = g[:r, :r], g[:r, r : 2 * r], g[:r, 2 * r :]
    g10, g11, g20 = g[r : 2 * r, :r], g[r : 2 * r, r : 2 * r], g[2 * r :, :r]
    return g00 + ((g01 + g10) + (g11 + (g02 + g20)))


def wide(column):
    return jnp.broadcast_to(column, (8, 2 * RANK))


def inverse_factor(gram):
    rows = lax.broadcasted_iota(jnp.int32, (RANK, RANK), 0)
    cols = lax.broadcasted_iota(jnp.int32, (RANK, RANK), 1)
    both = jnp.concatenate([gram, jnp.where(rows == cols, 1.0, 0.0).astype(f32)], axis=1)
    sub = lax.broadcasted_iota(jnp.int32, (8, 2 * RANK), 0)
    count = RANK // 8
    tiles = [both[8 * i : 8 * i + 8] for i in range(count)]
    for p in range(count):
        columns = [[wide(tiles[i][:, 8 * p + j : 8 * p + j + 1]) for j in range(8)] for i in range(p, count)]
        panel, own, pivots, scales = tiles[p], columns[0], jnp.ones((8, 2 * RANK), f32), []
        for s in range(8):
            pivot = own[s][s : s + 1]
            scales.append(1.0 / pivot)
            pivots = jnp.where(sub == s, pivot, pivots)
            factor = jnp.where(sub > s, own[s] * scales[s], 0.0)
            panel = panel - factor * panel[s : s + 1]
            for j in range(s + 1, 8):
                own[j] = own[j] - factor * own[j][s : s + 1]
        for i in range(p + 1, count):
            below, tile = columns[i - p], tiles[i]
            for s in range(8):
                factor = below[s] * scales[s]
                tile = tile - factor * panel[s : s + 1]
                for j in range(s + 1, 8):
                    below[j] = below[j] - factor * own[j][s : s + 1]
            tiles[i] = tile
        tiles[p] = panel * lax.rsqrt(pivots)
    return jnp.concatenate(tiles, axis=0)[:, RANK:]


def near_inverse_factor(off):
    rows = lax.broadcasted_iota(jnp.int32, (RANK, RANK), 0)
    cols = lax.broadcasted_iota(jnp.int32, (RANK, RANK), 1)
    lower = jnp.where(rows > cols, 1.0, jnp.where(rows == cols, 0.5, 0.0)).astype(f32)
    first = off * lower
    second = -lower * lax.dot_general(first, first, NT, precision=HIGHEST, preferred_element_type=f32)
    square = jnp.dot(first, first, precision=HIGHEST, preferred_element_type=f32)
    eye = jnp.where(rows == cols, 1.0, 0.0).astype(f32)
    return eye - first + (square - second)


def dot6(a, b3):
    hi = a.astype(bf16).astype(f32)
    mid = (a - hi).astype(bf16).astype(f32)
    low = a - hi - mid
    one = jnp.concatenate([hi, hi, hi, mid], axis=1).astype(bf16)
    two = jnp.concatenate([mid, low], axis=1).astype(bf16)
    high, middle = b3[:RANK], b3[RANK : 2 * RANK]
    out = jnp.dot(one, jnp.concatenate([b3, high], axis=0), preferred_element_type=f32)
    return out + jnp.dot(two, jnp.concatenate([middle, high], axis=0), preferred_element_type=f32)


def pack(square):
    return jnp.concatenate([square[: RANK // 2], square[RANK // 2 :]], axis=1)


def unpack(packed):
    return jnp.concatenate([packed[:, :RANK], packed[:, RANK:]], axis=0)


def call(kernel, out_shape, *args, scratch=(), hbm=(), unread=(), out_hbm=False):
    vmem, far, anywhere = (pl.BlockSpec(memory_space=m) for m in (pltpu.VMEM, pltpu.HBM, pl.ANY))
    many = isinstance(out_shape, list)
    shapes = [jax.ShapeDtypeStruct(*s) for s in (out_shape if many else [out_shape])]
    return pl.pallas_call(
        kernel,
        out_shape=shapes if many else shapes[0],
        in_specs=[far if i in hbm else anywhere if i in unread else vmem for i in range(len(args))],
        out_specs=[far if out_hbm else vmem] * len(shapes) if many else vmem,
        scratch_shapes=list(scratch),
        compiler_params=pltpu.CompilerParams(vmem_limit_bytes=32 * 1024 * 1024),
    )(*args)


DEALT = (0, 2, 1, 3)


def rows_at(index, size):
    return pl.ds(pl.multiple_of(index * size, size), size)


def in_order(index, refs, ks=(0, 1, 3, 2)):
    for k, ref in zip(ks, refs, strict=True):
        yield lax.rem(index + 4 - k, 4), ref


def sum_in_order(slots_ref, index, refs, ks=(0, 1, 3, 2)):
    for place, ref in in_order(index, refs, ks):
        slots_ref[place] = ref[...]
    return (slots_ref[0] + slots_ref[1]) + (slots_ref[2] + slots_ref[3])


def scatter(whole_ref, index, refs):
    size = whole_ref.shape[0] // 4
    for k, ref in zip(DEALT, refs, strict=True):
        ref[...] = whole_ref[rows_at(lax.rem(index + k, 4), size), :]


def factor_kernel(qt_ref, cot_ref, q3_ref, own_ref, cot_out_ref, qt, sems):
    at, cut = lax.axis_index("y") * NZ + lax.axis_index("z"), 1024
    pairs = [(qt_ref.at[:, i : i + cut], qt.at[:, i : i + cut]) for i in range(0, D, cut)]
    pairs += [(qt_ref.at[:, rows_at(at, EB)], own_ref), (cot_ref, cot_out_ref)]
    copies = [pltpu.make_async_copy(a, b, sems.at[i]) for i, (a, b) in enumerate(pairs)]
    for copy in copies:
        copy.start()
    for i in range(D // cut):
        copies[i].wait()
        q3_ref[:, i * cut : (i + 1) * cut] = split3(qt[:, i * cut : (i + 1) * cut])
    copies[-2].wait()
    copies[-1].wait()


def project_kernel(cot_ref, other_ref, q3_ref, out_ref, both_ref):
    c = lax.axis_index("c")
    both_ref[rows_at(c, TB), :] = cot_ref[...]
    both_ref[rows_at(1 - c, TB), :] = other_ref[...]
    got = lax.dot_general(both_ref[...], q3_ref[...], NT, preferred_element_type=f32)
    got = got[:, :RANK] + (got[:, RANK : 2 * RANK] + got[:, 2 * RANK :])
    part = TB // 2
    for i in range(NC):
        own = got[i * TB : (i + 1) * TB]
        out_ref[i * part : (i + 1) * part, :] = jnp.concatenate([own[:part], own[part:]], axis=1)


def fetch_kernel(hidden_ref, err_ref, after_ref, h_ref, e_ref, sems):
    copies = [pltpu.make_async_copy(a, b, sems.at[i]) for i, (a, b) in enumerate(((hidden_ref, h_ref), (err_ref, e_ref)))]
    for copy in copies:
        copy.start()
    for copy in copies:
        copy.wait()


def columns_kernel(both_ref, after_ref, *out_refs):
    x = lax.axis_index("x")
    for k, ref in zip(DEALT, out_refs, strict=True):
        ref[...] = both_ref[:, rows_at(lax.rem(x + k, NX), CB)]


def join_x_kernel(own_ref, other_ref, out_ref):
    bit = lax.rem(lax.axis_index("x"), 2)
    out_ref[bit] = own_ref[...]
    out_ref[1 - bit] = other_ref[...]


def left_kernel(pair_ref, far_ref, hidden_ref, err_ref, q_ref, own_ref, a_ref, b_ref, c_ref, slots_ref, whole_ref):
    at = lax.axis_index("x") // 2
    slots_ref[at] = pair_ref[...]
    slots_ref[1 - at] = far_ref[...]
    packed = slots_ref[...].reshape(TOK // 2, 2 * RANK).T
    proj = jnp.concatenate([packed[:RANK], packed[RANK:]], axis=1)
    h = hidden_ref[...].reshape(NX * NC, 2, TB // 2, FB)
    h = jnp.concatenate([h[:, 0].reshape(TOK // 2, FB), h[:, 1].reshape(TOK // 2, FB)], axis=0)
    whole_ref[...] = dot3(split3(proj), h, NN) + dot3(split3(q_ref[...]), err_ref[...], NT)
    scatter(whole_ref, lax.axis_index("y"), (own_ref, a_ref, b_ref, c_ref))


def halve_kernel(own_ref, a_ref, b_ref, c_ref, after_ref, keep_ref, send_ref, slots_ref, both_ref):
    both_ref[...] = sum_in_order(slots_ref, lax.axis_index("y"), (own_ref, a_ref, b_ref, c_ref), DEALT)
    bit, half = lax.rem(lax.axis_index("z"), 2), keep_ref.shape[0]
    keep_ref[...] = both_ref[rows_at(bit, half), :]
    send_ref[...] = both_ref[rows_at(1 - bit, half), :]


def add_kernel(a_ref, b_ref, out_ref):
    out_ref[...] = a_ref[...] + b_ref[...]


def sum_z_kernel(own_ref, a_ref, b_ref, c_ref, out_ref, slots_ref):
    out_ref[...] = sum_in_order(slots_ref, lax.axis_index("z") // 2, (own_ref, a_ref, b_ref, c_ref))


def sum_z_after_kernel(own_ref, a_ref, b_ref, c_ref, *rest):
    sum_z_kernel(own_ref, a_ref, b_ref, c_ref, *rest[-2:])


def sum_x_kernel(own_ref, a_ref, b_ref, c_ref, out_ref, gram_ref, slots_ref):
    out_ref[...] = sum_in_order(slots_ref, lax.axis_index("x"), (own_ref, a_ref, b_ref, c_ref))
    gram_ref[...] = out_ref[3 * RANK :, :]


def join_z_kernel(own_ref, other_ref, out_ref):
    bit, half = lax.rem(lax.axis_index("z"), 2), own_ref.shape[0]
    out_ref[rows_at(bit, half), :] = own_ref[...]
    out_ref[rows_at(1 - bit, half), :] = other_ref[...]


def mixed_kernel(own_ref, a_ref, b_ref, c_ref, hidden_ref, err_ref, after_ref, p3_ref, all_ref, p_ref):
    for place, ref in in_order(lax.axis_index("y"), (own_ref, a_ref, b_ref, c_ref)):
        p_ref[rows_at(place, RANK // NY), :] = ref[...]
    p3 = split3(p_ref[...])
    p3_ref[...] = p3
    mixed = dot3(p3, hidden_ref[...], NT)
    all_ref[:RANK, :] = mixed[:, :EB]
    all_ref[RANK : 2 * RANK, :] = mixed[:, EB:]
    all_ref[2 * RANK : 3 * RANK, :] = dot3(p3, err_ref[...], NN)
    all_ref[3 * RANK :, :] = pack(gram3(p3))


def right_kernel(mixed_ref, cot_ref, a_cot_ref, b_cot_ref, c_cot_ref, own_ref, a_ref, b_ref, c_ref, slots_ref, whole_ref):
    x, at = lax.axis_index("x"), lax.axis_index("y") * NZ + lax.axis_index("z")
    for place, ref in in_order(x, (cot_ref, a_cot_ref, b_cot_ref, c_cot_ref), DEALT):
        slots_ref[place] = ref[...]
    mixed = jnp.concatenate([mixed_ref[:RANK, :], mixed_ref[RANK : 2 * RANK, :]], axis=1)
    part = dot3(split3(mixed), slots_ref[...].reshape(TOK, CB), NN)
    err_q = mixed_ref[2 * RANK : 3 * RANK, :]
    here = [jnp.where(at == x * (CB // EB) + i, err_q, 0.0) for i in range(CB // EB)]
    whole_ref[...] = part + jnp.concatenate(here, axis=1)
    scatter(whole_ref, lax.axis_index("y"), (own_ref, a_ref, b_ref, c_ref))


def first_kernel(own_ref, other_ref, after_ref, inv_ref):
    inv_ref[...] = inverse_factor(unpack(jnp.where(lax.axis_index("c") == 1, own_ref[...], other_ref[...])))


def basis_kernel(inv_ref, p3_ref, after_ref, b3_ref, gram_ref):
    b3 = split3(dot6(inv_ref[...], p3_ref[...]))
    b3_ref[...] = b3
    gram_ref[...] = pack(gram3(b3))


def sum_y_kernel(own_ref, a_ref, b_ref, c_ref, after_ref, out_ref, slots_ref):
    out_ref[...] = sum_in_order(slots_ref, lax.axis_index("y"), (own_ref, a_ref, b_ref, c_ref), DEALT)


def add_after_kernel(a_ref, b_ref, after_ref, out_ref):
    out_ref[...] = a_ref[...] + b_ref[...]


def sum_z_gram_kernel(own_ref, a_ref, b_ref, c_ref, gram_ref, other_ref, out_ref, slots_ref):
    total = sum_in_order(slots_ref, lax.axis_index("z") // 2, (own_ref, a_ref, b_ref, c_ref))
    gram, rows = gram_ref[...] + other_ref[...], RANK // NY
    gram = jnp.concatenate([gram[:rows], gram[rows:]], axis=1)
    core, size = lax.axis_index("c") == 1, 4 * RANK
    out_ref[:, :size] = jnp.where(core, total[:, :size], gram)
    out_ref[:, size:] = total[:, size:]


def block_kernel(own_ref, a_ref, b_ref, c_ref, out_ref):
    for place, ref in in_order(lax.axis_index("y"), (own_ref, a_ref, b_ref, c_ref)):
        out_ref[rows_at(place, RANK // NY), :] = ref[...]


def second_kernel(own_ref, a_ref, b_ref, c_ref, inverse_ref, slots_ref):
    for place, ref in in_order(lax.axis_index("x"), (own_ref, a_ref, b_ref, c_ref)):
        slots_ref[place] = ref[:, : 4 * RANK]
    gram = (slots_ref[0] + slots_ref[1]) + (slots_ref[2] + slots_ref[3])
    gram = unpack(jnp.concatenate([gram[:, : 2 * RANK], gram[:, 2 * RANK :]], axis=0))
    rows = lax.broadcasted_iota(jnp.int32, (RANK, RANK), 0)
    cols = lax.broadcasted_iota(jnp.int32, (RANK, RANK), 1)
    off = gram - jnp.where(rows == cols, 1.0, 0.0).astype(f32)
    here, near = lax.axis_index("c") == 0, jnp.max(jnp.abs(off)) < 1e-3

    @pl.when(jnp.logical_and(here, near))
    def _():
        inverse_ref[...] = near_inverse_factor(off)

    @pl.when(jnp.logical_and(here, jnp.logical_not(near)))
    def _():
        inverse_ref[...] = inverse_factor(gram)

    @pl.when(jnp.logical_not(here))
    def _():
        inverse_ref[...] = jnp.zeros((RANK, RANK), f32)


def total_kernel(own_ref, other_ref, inv_ref, block_ref, total_ref, inverse_ref, pass_ref):
    pass_ref[...] = block_ref[...]
    inverse = jnp.where(lax.axis_index("c") == 0, own_ref[...], other_ref[...])
    inverse_ref[...] = inverse
    total_ref[...] = jnp.dot(inverse, inv_ref[...], precision=HIGHEST, preferred_element_type=f32) * (1.0 / N_DP)


def new_kernel(*refs):
    total_ref, inverse_ref, b3_ref, out_ref, basis_ref, whole_ref, scaled_ref, sems = refs[2 * NX :]
    x, core, total, copies = lax.axis_index("x"), lax.axis_index("c") == 1, total_ref[...], []
    for k, (place, ref) in enumerate(in_order(x, refs[:NX])):
        block = jnp.where(core, ref[...], refs[NX + k][...])
        whole_ref[k] = dot6(total, split3(block))
        cols = rows_at(place, CB)
        copies.append(pltpu.make_async_copy(whole_ref.at[k], out_ref.at[:, cols], sems.at[k]))
        copies[-1].start()
        if k == 0:
            scaled_ref[...] = dot6(inverse_ref[...] * math.sqrt(FF), b3_ref[...])
            copies.append(pltpu.make_async_copy(scaled_ref, basis_ref, sems.at[NX]))
            copies[-1].start()
    for copy in copies:
        copy.wait()


def swap(a):
    return lax.ppermute(a, "c", [(0, 1), (1, 0)])


def pair_x(a, partner):
    return lax.ppermute(a, "x", [(x, partner(x)) for x in range(NX)])


def lead(a, step, idle):
    places = [(y, z, x) for y in range(NY) for z in range(NZ) for x in range(NX)]
    number = {place: i * NC for i, place in enumerate(places)}
    pairs = [(number[p] + c, number[move(*p)] + c) for p in places for c, move in ((0, idle), (1, step))]
    return lax.ppermute(a, ("y", "z", "x", "c"), pairs)


def lead_shift(a, axis, k):
    hop = 1 if k == 3 else -1
    if axis == "x":
        return lead(a, lambda y, z, x: (y, z, (x + k) % NX), lambda y, z, x: ((y + hop) % NY, z, x))
    if axis == "y":
        return lead(a, lambda y, z, x: ((y + k) % NY, z, x), lambda y, z, x: (y, z, (x + k) % NX))
    return lead(a, lambda y, z, x: (y, (z + 2 * k) % NZ, x), lambda y, z, x: (y, z, (x + hop) % NX))


def lead_swap_z(a):
    return lead(a, lambda y, z, x: (y, z ^ 1, x), lambda y, z, x: (y, z, x ^ 1))


def swap_z(a):
    return lax.ppermute(a, "z", [(i, i ^ 1) for i in range(NZ)])


def shift(a, axis, k):
    size, step = {"y": (NY, 1), "z": (NZ, 2), "x": (NX, 1)}[axis]
    return lax.ppermute(a, axis, [(i, (i + k * step) % size) for i in range(size)])


def deal(blocks, axis, shift=shift):
    return [blocks[0]] + [shift(block, axis, k) for k, block in zip(DEALT[1:], blocks[1:], strict=True)]


def share(block, axis, shift=shift):
    return [block] + [shift(block, axis, k) for k in (1, 3, 2)]


def shards(hidden, cotangent, error_buf, q_start):
    qt = q_start.T
    dma, half = pltpu.SemaphoreType.DMA, RANK // 2
    pinned = [pltpu.with_memory_space_constraint(a, pltpu.HBM) for a in (q_start.T, cotangent, hidden, error_buf)]
    other = swap(cotangent)
    q3, q_own, cot = call(
        factor_kernel, [((3 * RANK, D), bf16), ((RANK, EB), f32), ((TB, D), bf16)], *pinned[:2],
        scratch=[pltpu.VMEM((RANK, D), f32), dma((6,))], hbm=(0, 1),
    )
    proj, both = call(project_kernel, [((TB, 2 * RANK), f32), ((2 * TB, D), bf16)], cot, other, q3)
    hid, err = call(
        fetch_kernel, [((TOK, FB), bf16), ((FB, EB), bf16)], *pinned[2:], proj, scratch=[dma((2,))], hbm=(0, 1), unread=(2,)
    )
    pair = call(join_x_kernel, ((2, TB, 2 * RANK), f32), proj, pair_x(proj, lambda x: x ^ 1))
    quarter, eighth = ((RANK // NY, FB), f32), ((RANK // NY // 2, FB), f32)
    parts = call(
        left_kernel, [quarter] * 4, pair, pair_x(pair, lambda x: NX - 1 - x), hid, err, q_own,
        scratch=[pltpu.VMEM((2, 2, TB, 2 * RANK), f32), pltpu.VMEM((RANK, FB), f32)],
    )

    parts = deal(parts, "y")
    blocks = call(columns_kernel, [((2 * TB, CB), bf16)] * NX, both, parts[2], unread=(1,))
    cot = deal(blocks, "x")
    keep, send = call(
        halve_kernel, [eighth, eighth], *parts, cot[0], scratch=[pltpu.VMEM((4, *quarter[0]), f32), pltpu.VMEM(*quarter)], unread=(4,)
    )
    p = call(add_kernel, eighth, keep, swap_z(send))
    p = call(
        sum_z_after_kernel, eighth, *share(p, "z"), cot[2], cot[3], scratch=[pltpu.VMEM((4, *eighth[0]), f32)], unread=(4, 5)
    )
    p = call(join_z_kernel, quarter, p, swap_z(p))

    mix, small = ((3 * RANK + half, EB), f32), ((half, 2 * RANK), f32)
    p3, mixed = call(
        mixed_kernel, [((3 * RANK, FB), bf16), mix], *share(p, "y"), hid, err, cot[1], scratch=[pltpu.VMEM((RANK, FB), f32)], unread=(6,)
    )
    mixed = call(add_kernel, mix, mixed, swap(mixed))
    mixed, gram = call(sum_x_kernel, [mix, small], *share(mixed, "x", lead_shift), scratch=[pltpu.VMEM((4, *mix[0]), f32)])

    piece, slots = ((RANK // NY, CB), f32), pltpu.VMEM((4, RANK // NY, CB), f32)
    parts = call(
        right_kernel, [piece] * 4, mixed, *cot, scratch=[pltpu.VMEM((4, 2 * TB, CB), bf16), pltpu.VMEM((RANK, CB), f32)]
    )
    gram_other = swap(gram)
    s = call(sum_y_kernel, piece, *deal(parts, "y", lead_shift), gram_other, scratch=[slots], unread=(4,))
    inverse = call(first_kernel, ((RANK, RANK), f32), gram, gram_other, s, unread=(2,))
    s = call(add_after_kernel, piece, s, lead_swap_z(s), inverse, unread=(2,))
    b3, gram = call(basis_kernel, [((3 * RANK, FB), bf16), small], inverse, p3, s, unread=(2,))
    s = call(sum_z_gram_kernel, piece, *share(s, "z", lead_shift), gram, swap(gram), scratch=[slots])
    quarters, square, whole = share(s, "y", lead_shift), ((RANK, RANK), f32), ((RANK, CB), f32)
    s = call(block_kernel, whole, *quarters)
    second = call(second_kernel, square, *quarters, scratch=[pltpu.VMEM((4, RANK // NY, 4 * RANK), f32)])
    total, second, own = call(total_kernel, [square, square, whole], second, swap(second), inverse, s)
    blocks = [own] + share(s, "x", lead_shift)[1:]
    blocks += [swap(b) for b in blocks]
    q_new, scaled = call(
        new_kernel, [((RANK, D), f32), ((RANK, FB), f32)], *blocks, total, second, b3,
        scratch=[pltpu.VMEM((NX, RANK, CB), f32), pltpu.VMEM((RANK, FB), f32), dma((NX + 1,))], out_hbm=True,
    )
    return scaled.T, q_new.T


def solution(mesh):
    fine = Mesh(mesh.devices.reshape(NY, NZ, NX, NC), ("y", "z", "x", "c"))
    dp, tensor = ("y", "z"), ("x", "c")
    placed = (P(dp, tensor), P(dp + tensor, None), P(tensor, dp), P())
    return jax.shard_map(
        shards, mesh=fine, in_specs=placed, out_specs=(P(tensor, None), P()), check_vma=False
    )
```

```python
import functools
import math

import jax
import jax.numpy as jnp
from jax import lax
from jax.experimental import pallas as pl
from jax.experimental.pallas import tpu as pltpu
from jax.sharding import Mesh
from jax.sharding import PartitionSpec as P

FF = 14336
D = 4096
RANK = 64
N_DP = 32
TOK = 256
NY, NZ, NX, NC = 4, 8, 4, 2
FB = FF // (NX * NC)
CB = D // NX
EB = D // N_DP
TB = TOK // (NX * NC)
f32, bf16 = jnp.float32, jnp.bfloat16
HIGHEST = lax.Precision.HIGHEST
NN = (((1,), (0,)), ((), ()))
NT = (((1,), (1,)), ((), ()))


def split3(a):
    hi = a.astype(bf16)
    rest = a - hi.astype(f32)
    mid = rest.astype(bf16)
    low = (rest - mid.astype(f32)).astype(bf16)
    return jnp.concatenate([hi, mid, low], axis=0)


def add3(a):
    n = a.shape[0] // 3
    return a[:n] + (a[n : 2 * n] + a[2 * n :])


def dot3(a, b, dims):
    return add3(lax.dot_general(a, b, dims, preferred_element_type=f32))


def gram3(a3):
    g = lax.dot_general(a3, a3, NT, preferred_element_type=f32)
    r = RANK
    g00, g01, g02 = g[:r, :r], g[:r, r : 2 * r], g[:r, 2 * r :]
    g10, g11, g20 = g[r : 2 * r, :r], g[r : 2 * r, r : 2 * r], g[2 * r :, :r]
    return g00 + ((g01 + g10) + (g11 + (g02 + g20)))


def wide(column):
    return jnp.broadcast_to(column, (8, 2 * RANK))


def inverse_factor(gram):
    rows = lax.broadcasted_iota(jnp.int32, (RANK, RANK), 0)
    cols = lax.broadcasted_iota(jnp.int32, (RANK, RANK), 1)
    both = jnp.concatenate([gram, jnp.where(rows == cols, 1.0, 0.0).astype(f32)], axis=1)
    sub = lax.broadcasted_iota(jnp.int32, (8, 2 * RANK), 0)
    count = RANK // 8
    tiles = [both[8 * i : 8 * i + 8] for i in range(count)]
    for p in range(count):
        columns = [[wide(tiles[i][:, 8 * p + j : 8 * p + j + 1]) for j in range(8)] for i in range(p, count)]
        panel, own, pivots, scales = tiles[p], columns[0], jnp.ones((8, 2 * RANK), f32), []
        for s in range(8):
            pivot = own[s][s : s + 1]
            scales.append(1.0 / pivot)
            pivots = jnp.where(sub == s, pivot, pivots)
            factor = jnp.where(sub > s, own[s] * scales[s], 0.0)
            panel = panel - factor * panel[s : s + 1]
            for j in range(s + 1, 8):
                own[j] = own[j] - factor * own[j][s : s + 1]
        for i in range(p + 1, count):
            below, tile = columns[i - p], tiles[i]
            for s in range(8):
                factor = below[s] * scales[s]
                tile = tile - factor * panel[s : s + 1]
                for j in range(s + 1, 8):
                    below[j] = below[j] - factor * own[j][s : s + 1]
            tiles[i] = tile
        tiles[p] = panel * lax.rsqrt(pivots)
    return jnp.concatenate(tiles, axis=0)[:, RANK:]


def near_inverse_factor(off):
    rows = lax.broadcasted_iota(jnp.int32, (RANK, RANK), 0)
    cols = lax.broadcasted_iota(jnp.int32, (RANK, RANK), 1)
    lower = jnp.where(rows > cols, 1.0, jnp.where(rows == cols, 0.5, 0.0)).astype(f32)
    first = off * lower
    second = -lower * lax.dot_general(first, first, NT, precision=HIGHEST, preferred_element_type=f32)
    square = jnp.dot(first, first, precision=HIGHEST, preferred_element_type=f32)
    eye = jnp.where(rows == cols, 1.0, 0.0).astype(f32)
    return eye - first + (square - second)


def dot6(a, b3):
    hi = a.astype(bf16).astype(f32)
    mid = (a - hi).astype(bf16).astype(f32)
    low = a - hi - mid
    one = jnp.concatenate([hi, hi, hi, mid], axis=1).astype(bf16)
    two = jnp.concatenate([mid, low], axis=1).astype(bf16)
    high, middle = b3[:RANK], b3[RANK : 2 * RANK]
    out = jnp.dot(one, jnp.concatenate([b3, high], axis=0), preferred_element_type=f32)
    return out + jnp.dot(two, jnp.concatenate([middle, high], axis=0), preferred_element_type=f32)


def pack(square):
    return jnp.concatenate([square[: RANK // 2], square[RANK // 2 :]], axis=1)


def unpack(packed):
    return jnp.concatenate([packed[:, :RANK], packed[:, RANK:]], axis=0)


def call(kernel, out_shape, *args, scratch=(), hbm=(), unread=(), out_hbm=False):
    vmem, far, anywhere = (pl.BlockSpec(memory_space=m) for m in (pltpu.VMEM, pltpu.HBM, pl.ANY))
    many = isinstance(out_shape, list)
    shapes = [jax.ShapeDtypeStruct(*s) for s in (out_shape if many else [out_shape])]
    return pl.pallas_call(
        kernel,
        out_shape=shapes if many else shapes[0],
        in_specs=[far if i in hbm else anywhere if i in unread else vmem for i in range(len(args))],
        out_specs=[far if out_hbm else vmem] * len(shapes) if many else vmem,
        scratch_shapes=list(scratch),
        compiler_params=pltpu.CompilerParams(vmem_limit_bytes=32 * 1024 * 1024),
    )(*args)


DEALT = (0, 2, 1, 3)


def rows_at(index, size):
    return pl.ds(pl.multiple_of(index * size, size), size)


def in_order(index, refs, ks=(0, 1, 3, 2)):
    for k, ref in zip(ks, refs, strict=True):
        yield lax.rem(index + 4 - k, 4), ref


def sum_in_order(slots_ref, index, refs, ks=(0, 1, 3, 2)):
    for place, ref in in_order(index, refs, ks):
        slots_ref[place] = ref[...]
    return (slots_ref[0] + slots_ref[1]) + (slots_ref[2] + slots_ref[3])


def scatter(whole_ref, index, refs):
    size = whole_ref.shape[0] // 4
    for k, ref in zip(DEALT, refs, strict=True):
        ref[...] = whole_ref[rows_at(lax.rem(index + k, 4), size), :]


def factor_kernel(qt_ref, cot_ref, q3_ref, own_ref, cot_out_ref, qt, sems):
    at, cut = lax.axis_index("y") * NZ + lax.axis_index("z"), 1024
    pairs = [(qt_ref.at[:, i : i + cut], qt.at[:, i : i + cut]) for i in range(0, D, cut)]
    pairs += [(qt_ref.at[:, rows_at(at, EB)], own_ref), (cot_ref, cot_out_ref)]
    copies = [pltpu.make_async_copy(a, b, sems.at[i]) for i, (a, b) in enumerate(pairs)]
    for copy in copies:
        copy.start()
    for i in range(D // cut):
        copies[i].wait()
        q3_ref[:, i * cut : (i + 1) * cut] = split3(qt[:, i * cut : (i + 1) * cut])
    copies[-2].wait()
    copies[-1].wait()


def project_kernel(cot_ref, other_ref, q3_ref, out_ref, both_ref):
    c = lax.axis_index("c")
    both_ref[rows_at(c, TB), :] = cot_ref[...]
    both_ref[rows_at(1 - c, TB), :] = other_ref[...]
    got = lax.dot_general(both_ref[...], q3_ref[...], NT, preferred_element_type=f32)
    got = got[:, :RANK] + (got[:, RANK : 2 * RANK] + got[:, 2 * RANK :])
    part = TB // 2
    for i in range(NC):
        own = got[i * TB : (i + 1) * TB]
        out_ref[i * part : (i + 1) * part, :] = jnp.concatenate([own[:part], own[part:]], axis=1)


def fetch_kernel(hidden_ref, err_ref, after_ref, h_ref, e_ref, sems):
    copies = [pltpu.make_async_copy(a, b, sems.at[i]) for i, (a, b) in enumerate(((hidden_ref, h_ref), (err_ref, e_ref)))]
    for copy in copies:
        copy.start()
    for copy in copies:
        copy.wait()


def columns_kernel(both_ref, after_ref, *out_refs):
    x = lax.axis_index("x")
    for k, ref in zip(DEALT, out_refs, strict=True):
        ref[...] = both_ref[:, rows_at(lax.rem(x + k, NX), CB)]


def join_x_kernel(own_ref, other_ref, out_ref):
    bit = lax.rem(lax.axis_index("x"), 2)
    out_ref[bit] = own_ref[...]
    out_ref[1 - bit] = other_ref[...]


def left_kernel(pair_ref, far_ref, hidden_ref, err_ref, q_ref, own_ref, a_ref, b_ref, c_ref, slots_ref, whole_ref):
    at = lax.axis_index("x") // 2
    slots_ref[at] = pair_ref[...]
    slots_ref[1 - at] = far_ref[...]
    packed = slots_ref[...].reshape(TOK // 2, 2 * RANK).T
    proj = jnp.concatenate([packed[:RANK], packed[RANK:]], axis=1)
    h = hidden_ref[...].reshape(NX * NC, 2, TB // 2, FB)
    h = jnp.concatenate([h[:, 0].reshape(TOK // 2, FB), h[:, 1].reshape(TOK // 2, FB)], axis=0)
    whole_ref[...] = dot3(split3(proj), h, NN) + dot3(split3(q_ref[...]), err_ref[...], NT)
    scatter(whole_ref, lax.axis_index("y"), (own_ref, a_ref, b_ref, c_ref))


def halve_kernel(own_ref, a_ref, b_ref, c_ref, after_ref, keep_ref, send_ref, slots_ref, both_ref):
    both_ref[...] = sum_in_order(slots_ref, lax.axis_index("y"), (own_ref, a_ref, b_ref, c_ref), DEALT)
    bit, half = lax.rem(lax.axis_index("z"), 2), keep_ref.shape[0]
    keep_ref[...] = both_ref[rows_at(bit, half), :]
    send_ref[...] = both_ref[rows_at(1 - bit, half), :]


def add_kernel(a_ref, b_ref, out_ref):
    out_ref[...] = a_ref[...] + b_ref[...]


def sum_z_kernel(own_ref, a_ref, b_ref, c_ref, out_ref, slots_ref):
    out_ref[...] = sum_in_order(slots_ref, lax.axis_index("z") // 2, (own_ref, a_ref, b_ref, c_ref))


def sum_z_after_kernel(own_ref, a_ref, b_ref, c_ref, *rest):
    sum_z_kernel(own_ref, a_ref, b_ref, c_ref, *rest[-2:])


def sum_x_kernel(own_ref, a_ref, b_ref, c_ref, out_ref, gram_ref, slots_ref):
    out_ref[...] = sum_in_order(slots_ref, lax.axis_index("x"), (own_ref, a_ref, b_ref, c_ref))
    gram_ref[...] = out_ref[3 * RANK :, :]


def join_z_kernel(own_ref, other_ref, out_ref):
    bit, half = lax.rem(lax.axis_index("z"), 2), own_ref.shape[0]
    out_ref[rows_at(bit, half), :] = own_ref[...]
    out_ref[rows_at(1 - bit, half), :] = other_ref[...]


def mixed_kernel(own_ref, a_ref, b_ref, c_ref, hidden_ref, err_ref, after_ref, p3_ref, all_ref, p_ref):
    for place, ref in in_order(lax.axis_index("y"), (own_ref, a_ref, b_ref, c_ref)):
        p_ref[rows_at(place, RANK // NY), :] = ref[...]
    p3 = split3(p_ref[...])
    p3_ref[...] = p3
    mixed = dot3(p3, hidden_ref[...], NT)
    all_ref[:RANK, :] = mixed[:, :EB]
    all_ref[RANK : 2 * RANK, :] = mixed[:, EB:]
    all_ref[2 * RANK : 3 * RANK, :] = dot3(p3, err_ref[...], NN)
    all_ref[3 * RANK :, :] = pack(gram3(p3))


def right_kernel(mixed_ref, cot_ref, a_cot_ref, b_cot_ref, c_cot_ref, own_ref, a_ref, b_ref, c_ref, slots_ref, whole_ref):
    x, at = lax.axis_index("x"), lax.axis_index("y") * NZ + lax.axis_index("z")
    for place, ref in in_order(x, (cot_ref, a_cot_ref, b_cot_ref, c_cot_ref), DEALT):
        slots_ref[place] = ref[...]
    mixed = jnp.concatenate([mixed_ref[:RANK, :], mixed_ref[RANK : 2 * RANK, :]], axis=1)
    part = dot3(split3(mixed), slots_ref[...].reshape(TOK, CB), NN)
    err_q = mixed_ref[2 * RANK : 3 * RANK, :]
    here = [jnp.where(at == x * (CB // EB) + i, err_q, 0.0) for i in range(CB // EB)]
    whole_ref[...] = part + jnp.concatenate(here, axis=1)
    scatter(whole_ref, lax.axis_index("y"), (own_ref, a_ref, b_ref, c_ref))


def first_kernel(own_ref, other_ref, after_ref, inv_ref):
    inv_ref[...] = inverse_factor(unpack(jnp.where(lax.axis_index("c") == 1, own_ref[...], other_ref[...])))


def basis_kernel(inv_ref, p3_ref, after_ref, b3_ref, gram_ref):
    b3 = split3(dot6(inv_ref[...], p3_ref[...]))
    b3_ref[...] = b3
    gram_ref[...] = pack(gram3(b3))


def sum_y_kernel(own_ref, a_ref, b_ref, c_ref, after_ref, out_ref, slots_ref):
    out_ref[...] = sum_in_order(slots_ref, lax.axis_index("y"), (own_ref, a_ref, b_ref, c_ref), DEALT)


def add_after_kernel(a_ref, b_ref, after_ref, out_ref):
    out_ref[...] = a_ref[...] + b_ref[...]


def sum_z_gram_kernel(own_ref, a_ref, b_ref, c_ref, gram_ref, other_ref, out_ref, slots_ref):
    total = sum_in_order(slots_ref, lax.axis_index("z") // 2, (own_ref, a_ref, b_ref, c_ref))
    gram, rows = gram_ref[...] + other_ref[...], RANK // NY
    gram = jnp.concatenate([gram[:rows], gram[rows:]], axis=1)
    core, size = lax.axis_index("c") == 1, 4 * RANK
    out_ref[:, :size] = jnp.where(core, total[:, :size], gram)
    out_ref[:, size:] = total[:, size:]


def block_kernel(own_ref, a_ref, b_ref, c_ref, out_ref):
    for place, ref in in_order(lax.axis_index("y"), (own_ref, a_ref, b_ref, c_ref)):
        out_ref[rows_at(place, RANK // NY), :] = ref[...]


def second_kernel(own_ref, a_ref, b_ref, c_ref, inverse_ref, slots_ref):
    for place, ref in in_order(lax.axis_index("x"), (own_ref, a_ref, b_ref, c_ref)):
        slots_ref[place] = ref[:, : 4 * RANK]
    gram = (slots_ref[0] + slots_ref[1]) + (slots_ref[2] + slots_ref[3])
    gram = unpack(jnp.concatenate([gram[:, : 2 * RANK], gram[:, 2 * RANK :]], axis=0))
    rows = lax.broadcasted_iota(jnp.int32, (RANK, RANK), 0)
    cols = lax.broadcasted_iota(jnp.int32, (RANK, RANK), 1)
    off = gram - jnp.where(rows == cols, 1.0, 0.0).astype(f32)
    here, near = lax.axis_index("c") == 0, jnp.max(jnp.abs(off)) < 1e-3

    @pl.when(jnp.logical_and(here, near))
    def _():
        inverse_ref[...] = near_inverse_factor(off)

    @pl.when(jnp.logical_and(here, jnp.logical_not(near)))
    def _():
        inverse_ref[...] = inverse_factor(gram)

    @pl.when(jnp.logical_not(here))
    def _():
        inverse_ref[...] = jnp.zeros((RANK, RANK), f32)


def total_kernel(own_ref, other_ref, inv_ref, block_ref, total_ref, inverse_ref, pass_ref):
    pass_ref[...] = block_ref[...]
    inverse = jnp.where(lax.axis_index("c") == 0, own_ref[...], other_ref[...])
    inverse_ref[...] = inverse
    total_ref[...] = jnp.dot(inverse, inv_ref[...], precision=HIGHEST, preferred_element_type=f32) * (1.0 / N_DP)


def new_kernel(*refs):
    total_ref, inverse_ref, b3_ref, out_ref, basis_ref, whole_ref, scaled_ref, sems = refs[2 * NX :]
    x, core, total, copies = lax.axis_index("x"), lax.axis_index("c") == 1, total_ref[...], []
    for k, (place, ref) in enumerate(in_order(x, refs[:NX])):
        block = jnp.where(core, ref[...], refs[NX + k][...])
        whole_ref[k] = dot6(total, split3(block))
        cols = rows_at(place, CB)
        copies.append(pltpu.make_async_copy(whole_ref.at[k], out_ref.at[:, cols], sems.at[k]))
        copies[-1].start()
        if k == 0:
            scaled_ref[...] = dot6(inverse_ref[...] * math.sqrt(FF), b3_ref[...])
            copies.append(pltpu.make_async_copy(scaled_ref, basis_ref, sems.at[NX]))
            copies[-1].start()
    for copy in copies:
        copy.wait()


def swap(a):
    return lax.ppermute(a, "c", [(0, 1), (1, 0)])


def pair_x(a, partner):
    return lax.ppermute(a, "x", [(x, partner(x)) for x in range(NX)])


def lead(a, step, idle):
    places = [(y, z, x) for y in range(NY) for z in range(NZ) for x in range(NX)]
    number = {place: i * NC for i, place in enumerate(places)}
    pairs = [(number[p] + c, number[move(*p)] + c) for p in places for c, move in ((0, idle), (1, step))]
    return lax.ppermute(a, ("y", "z", "x", "c"), pairs)


def one_hop(first, second, k):
    axis, hop = {1: (first, 1), 3: (first, -1), 2: (second, 1)}[k]
    return lambda y, z, x: ((y + hop * (axis == "y")) % NY, (z + hop * (axis == "z")) % NZ, (x + hop * (axis == "x")) % NX)


def lead_shift(a, axis, k):
    if axis == "x":
        return lead(a, lambda y, z, x: (y, z, (x + k) % NX), one_hop("y", "z", k))
    if axis == "y":
        return lead(a, lambda y, z, x: ((y + k) % NY, z, x), one_hop("x", "z", k))
    return lead(a, lambda y, z, x: (y, (z + 2 * k) % NZ, x), one_hop("x", "y", k))


def both_shift(a, axis, k):
    return lead(a, lambda y, z, x: ((y + k) % NY, z, x), lambda y, z, x: (y, z, (x + k) % NX))


def lead_swap_z(a):
    return lead(a, lambda y, z, x: (y, z ^ 1, x), lambda y, z, x: (y, z, x ^ 1))


def swap_z(a):
    return lax.ppermute(a, "z", [(i, i ^ 1) for i in range(NZ)])


def shift(a, axis, k):
    size, step = {"y": (NY, 1), "z": (NZ, 2), "x": (NX, 1)}[axis]
    return lax.ppermute(a, axis, [(i, (i + k * step) % size) for i in range(size)])


def deal(blocks, axis, shift=shift):
    return [blocks[0]] + [shift(block, axis, k) for k, block in zip(DEALT[1:], blocks[1:], strict=True)]


def share(block, axis, shift=shift):
    return [block] + [shift(block, axis, k) for k in (1, 3, 2)]


def shards(hidden, cotangent, error_buf, q_start):
    qt = q_start.T
    dma, half = pltpu.SemaphoreType.DMA, RANK // 2
    pinned = [pltpu.with_memory_space_constraint(a, pltpu.HBM) for a in (q_start.T, cotangent, hidden, error_buf)]
    other = swap(cotangent)
    q3, q_own, cot = call(
        factor_kernel, [((3 * RANK, D), bf16), ((RANK, EB), f32), ((TB, D), bf16)], *pinned[:2],
        scratch=[pltpu.VMEM((RANK, D), f32), dma((6,))], hbm=(0, 1),
    )
    proj, both = call(project_kernel, [((TB, 2 * RANK), f32), ((2 * TB, D), bf16)], cot, other, q3)
    hid, err = call(
        fetch_kernel, [((TOK, FB), bf16), ((FB, EB), bf16)], *pinned[2:], proj, scratch=[dma((2,))], hbm=(0, 1), unread=(2,)
    )
    pair = call(join_x_kernel, ((2, TB, 2 * RANK), f32), proj, pair_x(proj, lambda x: x ^ 1))
    quarter, eighth = ((RANK // NY, FB), f32), ((RANK // NY // 2, FB), f32)
    parts = call(
        left_kernel, [quarter] * 4, pair, pair_x(pair, lambda x: NX - 1 - x), hid, err, q_own,
        scratch=[pltpu.VMEM((2, 2, TB, 2 * RANK), f32), pltpu.VMEM((RANK, FB), f32)],
    )

    parts = deal(parts, "y")
    blocks = call(columns_kernel, [((2 * TB, CB), bf16)] * NX, both, parts[2], unread=(1,))
    cot = deal(blocks, "x")
    keep, send = call(
        halve_kernel, [eighth, eighth], *parts, cot[0], scratch=[pltpu.VMEM((4, *quarter[0]), f32), pltpu.VMEM(*quarter)], unread=(4,)
    )
    p = call(add_kernel, eighth, keep, swap_z(send))
    p = call(
        sum_z_after_kernel, eighth, *share(p, "z"), cot[2], cot[3], scratch=[pltpu.VMEM((4, *eighth[0]), f32)], unread=(4, 5)
    )
    p = call(join_z_kernel, quarter, p, swap_z(p))

    mix, small = ((3 * RANK + half, EB), f32), ((half, 2 * RANK), f32)
    p3, mixed = call(
        mixed_kernel, [((3 * RANK, FB), bf16), mix], *share(p, "y"), hid, err, cot[1], scratch=[pltpu.VMEM((RANK, FB), f32)], unread=(6,)
    )
    mixed = call(add_kernel, mix, mixed, swap(mixed))
    mixed, gram = call(sum_x_kernel, [mix, small], *share(mixed, "x", lead_shift), scratch=[pltpu.VMEM((4, *mix[0]), f32)])

    piece, slots = ((RANK // NY, CB), f32), pltpu.VMEM((4, RANK // NY, CB), f32)
    parts = call(
        right_kernel, [piece] * 4, mixed, *cot, scratch=[pltpu.VMEM((4, 2 * TB, CB), bf16), pltpu.VMEM((RANK, CB), f32)]
    )
    gram_other = swap(gram)
    s = call(sum_y_kernel, piece, *deal(parts, "y", lead_shift), gram_other, scratch=[slots], unread=(4,))
    inverse = call(first_kernel, ((RANK, RANK), f32), gram, gram_other, s, unread=(2,))
    s = call(add_after_kernel, piece, s, lead_swap_z(s), inverse, unread=(2,))
    b3, gram = call(basis_kernel, [((3 * RANK, FB), bf16), small], inverse, p3, s, unread=(2,))
    s = call(sum_z_gram_kernel, piece, *share(s, "z", lead_shift), gram, swap(gram), scratch=[slots])
    quarters, square, whole = share(s, "y", both_shift), ((RANK, RANK), f32), ((RANK, CB), f32)
    s = call(block_kernel, whole, *quarters)
    second = call(second_kernel, square, *quarters, scratch=[pltpu.VMEM((4, RANK // NY, 4 * RANK), f32)])
    total, second, own = call(total_kernel, [square, square, whole], second, swap(second), inverse, s)
    blocks = [own] + share(s, "x", lead_shift)[1:]
    blocks += [swap(b) for b in blocks]
    q_new, scaled = call(
        new_kernel, [((RANK, D), f32), ((RANK, FB), f32)], *blocks, total, second, b3,
        scratch=[pltpu.VMEM((NX, RANK, CB), f32), pltpu.VMEM((RANK, FB), f32), dma((NX + 1,))], out_hbm=True,
    )
    return scaled.T, q_new.T


def solution(mesh):
    fine = Mesh(mesh.devices.reshape(NY, NZ, NX, NC), ("y", "z", "x", "c"))
    dp, tensor = ("y", "z"), ("x", "c")
    placed = (P(dp, tensor), P(dp + tensor, None), P(tensor, dp), P())
    return jax.shard_map(
        shards, mesh=fine, in_specs=placed, out_specs=(P(tensor, None), P()), check_vma=False
    )
```

```python
import functools
import math

import jax
import jax.numpy as jnp
from jax import lax
from jax.experimental import pallas as pl
from jax.experimental.pallas import tpu as pltpu
from jax.sharding import Mesh
from jax.sharding import PartitionSpec as P

FF = 14336
D = 4096
RANK = 64
N_DP = 32
TOK = 256
NY, NZ, NX, NC = 4, 8, 4, 2
FB = FF // (NX * NC)
CB = D // NX
EB = D // N_DP
TB = TOK // (NX * NC)
f32, bf16 = jnp.float32, jnp.bfloat16
HIGHEST = lax.Precision.HIGHEST
NN = (((1,), (0,)), ((), ()))
NT = (((1,), (1,)), ((), ()))


def split3(a):
    hi = a.astype(bf16)
    rest = a - hi.astype(f32)
    mid = rest.astype(bf16)
    low = (rest - mid.astype(f32)).astype(bf16)
    return jnp.concatenate([hi, mid, low], axis=0)


def add3(a):
    n = a.shape[0] // 3
    return a[:n] + (a[n : 2 * n] + a[2 * n :])


def dot3(a, b, dims):
    return add3(lax.dot_general(a, b, dims, preferred_element_type=f32))


def gram3(a3):
    g = lax.dot_general(a3, a3, NT, preferred_element_type=f32)
    r = RANK
    g00, g01, g02 = g[:r, :r], g[:r, r : 2 * r], g[:r, 2 * r :]
    g10, g11, g20 = g[r : 2 * r, :r], g[r : 2 * r, r : 2 * r], g[2 * r :, :r]
    return g00 + ((g01 + g10) + (g11 + (g02 + g20)))


def wide(column):
    return jnp.broadcast_to(column, (8, 2 * RANK))


def inverse_factor(gram):
    rows = lax.broadcasted_iota(jnp.int32, (RANK, RANK), 0)
    cols = lax.broadcasted_iota(jnp.int32, (RANK, RANK), 1)
    both = jnp.concatenate([gram, jnp.where(rows == cols, 1.0, 0.0).astype(f32)], axis=1)
    sub = lax.broadcasted_iota(jnp.int32, (8, 2 * RANK), 0)
    count = RANK // 8
    tiles = [both[8 * i : 8 * i + 8] for i in range(count)]
    for p in range(count):
        columns = [[wide(tiles[i][:, 8 * p + j : 8 * p + j + 1]) for j in range(8)] for i in range(p, count)]
        panel, own, pivots, scales = tiles[p], columns[0], jnp.ones((8, 2 * RANK), f32), []
        for s in range(8):
            pivot = own[s][s : s + 1]
            scales.append(1.0 / pivot)
            pivots = jnp.where(sub == s, pivot, pivots)
            factor = jnp.where(sub > s, own[s] * scales[s], 0.0)
            panel = panel - factor * panel[s : s + 1]
            for j in range(s + 1, 8):
                own[j] = own[j] - factor * own[j][s : s + 1]
        for i in range(p + 1, count):
            below, tile = columns[i - p], tiles[i]
            for s in range(8):
                factor = below[s] * scales[s]
                tile = tile - factor * panel[s : s + 1]
                for j in range(s + 1, 8):
                    below[j] = below[j] - factor * own[j][s : s + 1]
            tiles[i] = tile
        tiles[p] = panel * lax.rsqrt(pivots)
    return jnp.concatenate(tiles, axis=0)[:, RANK:]


def near_inverse_factor(off):
    rows = lax.broadcasted_iota(jnp.int32, (RANK, RANK), 0)
    cols = lax.broadcasted_iota(jnp.int32, (RANK, RANK), 1)
    lower = jnp.where(rows > cols, 1.0, jnp.where(rows == cols, 0.5, 0.0)).astype(f32)
    first = off * lower
    second = -lower * lax.dot_general(first, first, NT, precision=HIGHEST, preferred_element_type=f32)
    square = jnp.dot(first, first, precision=HIGHEST, preferred_element_type=f32)
    eye = jnp.where(rows == cols, 1.0, 0.0).astype(f32)
    return eye - first + (square - second)


def dot6(a, b3):
    hi = a.astype(bf16).astype(f32)
    mid = (a - hi).astype(bf16).astype(f32)
    low = a - hi - mid
    one = jnp.concatenate([hi, hi, hi, mid], axis=1).astype(bf16)
    two = jnp.concatenate([mid, low], axis=1).astype(bf16)
    high, middle = b3[:RANK], b3[RANK : 2 * RANK]
    out = jnp.dot(one, jnp.concatenate([b3, high], axis=0), preferred_element_type=f32)
    return out + jnp.dot(two, jnp.concatenate([middle, high], axis=0), preferred_element_type=f32)


def pack(square):
    return jnp.concatenate([square[: RANK // 2], square[RANK // 2 :]], axis=1)


def unpack(packed):
    return jnp.concatenate([packed[:, :RANK], packed[:, RANK:]], axis=0)


def call(kernel, out_shape, *args, scratch=(), hbm=(), unread=(), out_hbm=False):
    vmem, far, anywhere = (pl.BlockSpec(memory_space=m) for m in (pltpu.VMEM, pltpu.HBM, pl.ANY))
    many = isinstance(out_shape, list)
    shapes = [jax.ShapeDtypeStruct(*s) for s in (out_shape if many else [out_shape])]
    return pl.pallas_call(
        kernel,
        out_shape=shapes if many else shapes[0],
        in_specs=[far if i in hbm else anywhere if i in unread else vmem for i in range(len(args))],
        out_specs=[far if out_hbm else vmem] * len(shapes) if many else vmem,
        scratch_shapes=list(scratch),
        compiler_params=pltpu.CompilerParams(vmem_limit_bytes=32 * 1024 * 1024),
    )(*args)


DEALT = (0, 2, 1, 3)


def rows_at(index, size):
    return pl.ds(pl.multiple_of(index * size, size), size)


def in_order(index, refs, ks=(0, 1, 3, 2)):
    for k, ref in zip(ks, refs, strict=True):
        yield lax.rem(index + 4 - k, 4), ref


def sum_in_order(slots_ref, index, refs, ks=(0, 1, 3, 2)):
    for place, ref in in_order(index, refs, ks):
        slots_ref[place] = ref[...]
    return (slots_ref[0] + slots_ref[1]) + (slots_ref[2] + slots_ref[3])


def scatter(whole_ref, index, refs):
    size = whole_ref.shape[0] // 4
    for k, ref in zip(DEALT, refs, strict=True):
        ref[...] = whole_ref[rows_at(lax.rem(index + k, 4), size), :]


def factor_kernel(qt_ref, cot_ref, q3_ref, own_ref, cot_out_ref, qt, sems):
    at, cut = lax.axis_index("y") * NZ + lax.axis_index("z"), 1024
    pairs = [(qt_ref.at[:, i : i + cut], qt.at[:, i : i + cut]) for i in range(0, D, cut)]
    pairs += [(qt_ref.at[:, rows_at(at, EB)], own_ref), (cot_ref, cot_out_ref)]
    copies = [pltpu.make_async_copy(a, b, sems.at[i]) for i, (a, b) in enumerate(pairs)]
    for copy in copies:
        copy.start()
    for i in range(D // cut):
        copies[i].wait()
        q3_ref[:, i * cut : (i + 1) * cut] = split3(qt[:, i * cut : (i + 1) * cut])
    copies[-2].wait()
    copies[-1].wait()


def project_kernel(cot_ref, other_ref, q3_ref, out_ref, both_ref):
    c = lax.axis_index("c")
    both_ref[rows_at(c, TB), :] = cot_ref[...]
    both_ref[rows_at(1 - c, TB), :] = other_ref[...]
    got = lax.dot_general(both_ref[...], q3_ref[...], NT, preferred_element_type=f32)
    got = got[:, :RANK] + (got[:, RANK : 2 * RANK] + got[:, 2 * RANK :])
    part = TB // 2
    for i in range(NC):
        own = got[i * TB : (i + 1) * TB]
        out_ref[i * part : (i + 1) * part, :] = jnp.concatenate([own[:part], own[part:]], axis=1)


def fetch_kernel(hidden_ref, err_ref, after_ref, h_ref, e_ref, sems):
    copies = [pltpu.make_async_copy(a, b, sems.at[i]) for i, (a, b) in enumerate(((hidden_ref, h_ref), (err_ref, e_ref)))]
    for copy in copies:
        copy.start()
    for copy in copies:
        copy.wait()


def columns_kernel(both_ref, after_ref, *out_refs):
    x = lax.axis_index("x")
    for k, ref in zip(DEALT, out_refs, strict=True):
        ref[...] = both_ref[:, rows_at(lax.rem(x + k, NX), CB)]


def join_x_kernel(own_ref, other_ref, out_ref):
    bit = lax.rem(lax.axis_index("x"), 2)
    out_ref[bit] = own_ref[...]
    out_ref[1 - bit] = other_ref[...]


def left_kernel(pair_ref, far_ref, hidden_ref, err_ref, q_ref, own_ref, a_ref, b_ref, c_ref, slots_ref, whole_ref):
    at = lax.axis_index("x") // 2
    slots_ref[at] = pair_ref[...]
    slots_ref[1 - at] = far_ref[...]
    packed = slots_ref[...].reshape(TOK // 2, 2 * RANK).T
    proj = jnp.concatenate([packed[:RANK], packed[RANK:]], axis=1)
    h = hidden_ref[...].reshape(NX * NC, 2, TB // 2, FB)
    h = jnp.concatenate([h[:, 0].reshape(TOK // 2, FB), h[:, 1].reshape(TOK // 2, FB)], axis=0)
    whole_ref[...] = dot3(split3(proj), h, NN) + dot3(split3(q_ref[...]), err_ref[...], NT)
    scatter(whole_ref, lax.axis_index("y"), (own_ref, a_ref, b_ref, c_ref))


def halve_kernel(own_ref, a_ref, b_ref, c_ref, after_ref, keep_ref, send_ref, slots_ref, both_ref):
    both_ref[...] = sum_in_order(slots_ref, lax.axis_index("y"), (own_ref, a_ref, b_ref, c_ref), DEALT)
    bit, half = lax.rem(lax.axis_index("z"), 2), keep_ref.shape[0]
    keep_ref[...] = both_ref[rows_at(bit, half), :]
    send_ref[...] = both_ref[rows_at(1 - bit, half), :]


def add_kernel(a_ref, b_ref, out_ref):
    out_ref[...] = a_ref[...] + b_ref[...]


def sum_z_kernel(own_ref, a_ref, b_ref, c_ref, out_ref, slots_ref):
    out_ref[...] = sum_in_order(slots_ref, lax.axis_index("z") // 2, (own_ref, a_ref, b_ref, c_ref))


def sum_z_after_kernel(own_ref, a_ref, b_ref, c_ref, *rest):
    sum_z_kernel(own_ref, a_ref, b_ref, c_ref, *rest[-2:])


def sum_x_kernel(own_ref, a_ref, b_ref, c_ref, out_ref, gram_ref, slots_ref):
    out_ref[...] = sum_in_order(slots_ref, lax.axis_index("x"), (own_ref, a_ref, b_ref, c_ref))
    gram_ref[...] = out_ref[3 * RANK :, :]


def join_z_kernel(own_ref, other_ref, out_ref):
    bit, half = lax.rem(lax.axis_index("z"), 2), own_ref.shape[0]
    out_ref[rows_at(bit, half), :] = own_ref[...]
    out_ref[rows_at(1 - bit, half), :] = other_ref[...]


def mixed_kernel(own_ref, a_ref, b_ref, c_ref, hidden_ref, err_ref, after_ref, p3_ref, all_ref, p_ref):
    for place, ref in in_order(lax.axis_index("y"), (own_ref, a_ref, b_ref, c_ref)):
        p_ref[rows_at(place, RANK // NY), :] = ref[...]
    p3 = split3(p_ref[...])
    p3_ref[...] = p3
    mixed = dot3(p3, hidden_ref[...], NT)
    all_ref[:RANK, :] = mixed[:, :EB]
    all_ref[RANK : 2 * RANK, :] = mixed[:, EB:]
    all_ref[2 * RANK : 3 * RANK, :] = dot3(p3, err_ref[...], NN)
    all_ref[3 * RANK :, :] = pack(gram3(p3))


def right_kernel(mixed_ref, cot_ref, a_cot_ref, b_cot_ref, c_cot_ref, own_ref, a_ref, b_ref, c_ref, slots_ref, whole_ref):
    x, at = lax.axis_index("x"), lax.axis_index("y") * NZ + lax.axis_index("z")
    for place, ref in in_order(x, (cot_ref, a_cot_ref, b_cot_ref, c_cot_ref), DEALT):
        slots_ref[place] = ref[...]
    mixed = jnp.concatenate([mixed_ref[:RANK, :], mixed_ref[RANK : 2 * RANK, :]], axis=1)
    part = dot3(split3(mixed), slots_ref[...].reshape(TOK, CB), NN)
    err_q = mixed_ref[2 * RANK : 3 * RANK, :]
    here = [jnp.where(at == x * (CB // EB) + i, err_q, 0.0) for i in range(CB // EB)]
    whole_ref[...] = part + jnp.concatenate(here, axis=1)
    scatter(whole_ref, lax.axis_index("y"), (own_ref, a_ref, b_ref, c_ref))


def first_kernel(own_ref, other_ref, after_ref, inv_ref):
    inv_ref[...] = inverse_factor(unpack(jnp.where(lax.axis_index("c") == 1, own_ref[...], other_ref[...])))


def basis_kernel(inv_ref, p3_ref, after_ref, b3_ref, gram_ref):
    b3 = split3(dot6(inv_ref[...], p3_ref[...]))
    b3_ref[...] = b3
    gram_ref[...] = pack(gram3(b3))


def sum_y_kernel(own_ref, a_ref, b_ref, c_ref, after_ref, out_ref, slots_ref):
    out_ref[...] = sum_in_order(slots_ref, lax.axis_index("y"), (own_ref, a_ref, b_ref, c_ref), DEALT)


def add_after_kernel(a_ref, b_ref, after_ref, out_ref):
    out_ref[...] = a_ref[...] + b_ref[...]


def sum_z_gram_kernel(own_ref, a_ref, b_ref, c_ref, gram_ref, other_ref, out_ref, slots_ref):
    total = sum_in_order(slots_ref, lax.axis_index("z") // 2, (own_ref, a_ref, b_ref, c_ref))
    gram, rows = gram_ref[...] + other_ref[...], RANK // NY
    gram = jnp.concatenate([gram[:rows], gram[rows:]], axis=1)
    core, size = lax.axis_index("c") == 1, 4 * RANK
    out_ref[:, :size] = jnp.where(core, total[:, :size], gram)
    out_ref[:, size:] = total[:, size:]


def block_kernel(own_ref, a_ref, b_ref, c_ref, out_ref):
    for place, ref in in_order(lax.axis_index("y"), (own_ref, a_ref, b_ref, c_ref)):
        out_ref[rows_at(place, RANK // NY), :] = ref[...]


def second_kernel(own_ref, a_ref, b_ref, c_ref, inverse_ref, slots_ref):
    for place, ref in in_order(lax.axis_index("x"), (own_ref, a_ref, b_ref, c_ref)):
        slots_ref[place] = ref[:, : 4 * RANK]
    gram = (slots_ref[0] + slots_ref[1]) + (slots_ref[2] + slots_ref[3])
    gram = unpack(jnp.concatenate([gram[:, : 2 * RANK], gram[:, 2 * RANK :]], axis=0))
    rows = lax.broadcasted_iota(jnp.int32, (RANK, RANK), 0)
    cols = lax.broadcasted_iota(jnp.int32, (RANK, RANK), 1)
    off = gram - jnp.where(rows == cols, 1.0, 0.0).astype(f32)
    here, near = lax.axis_index("c") == 0, jnp.max(jnp.abs(off)) < 1e-3

    @pl.when(jnp.logical_and(here, near))
    def _():
        inverse_ref[...] = near_inverse_factor(off)

    @pl.when(jnp.logical_and(here, jnp.logical_not(near)))
    def _():
        inverse_ref[...] = inverse_factor(gram)

    @pl.when(jnp.logical_not(here))
    def _():
        inverse_ref[...] = jnp.zeros((RANK, RANK), f32)


def total_kernel(own_ref, other_ref, inv_ref, total_ref, inverse_ref):
    inverse = jnp.where(lax.axis_index("c") == 0, own_ref[...], other_ref[...])
    inverse_ref[...] = inverse
    total_ref[...] = jnp.dot(inverse, inv_ref[...], precision=HIGHEST, preferred_element_type=f32) * (1.0 / N_DP)


def new_kernel(*refs):
    total_ref, inverse_ref, b3_ref, out_ref, basis_ref, whole_ref, scaled_ref, sems = refs[2 * NX :]
    x, core, total, copies = lax.axis_index("x"), lax.axis_index("c") == 1, total_ref[...], []
    for k, (place, ref) in enumerate(in_order(x, refs[:NX])):
        block = jnp.where(core, ref[...], refs[NX + k][...])
        whole_ref[k] = dot6(total, split3(block))
        cols = rows_at(place, CB)
        copies.append(pltpu.make_async_copy(whole_ref.at[k], out_ref.at[:, cols], sems.at[k]))
        copies[-1].start()
        if k == 0:
            scaled_ref[...] = dot6(inverse_ref[...] * math.sqrt(FF), b3_ref[...])
            copies.append(pltpu.make_async_copy(scaled_ref, basis_ref, sems.at[NX]))
            copies[-1].start()
    for copy in copies:
        copy.wait()


def swap(a):
    return lax.ppermute(a, "c", [(0, 1), (1, 0)])


def pair_x(a, partner):
    return lax.ppermute(a, "x", [(x, partner(x)) for x in range(NX)])


def lead(a, step, idle):
    places = [(y, z, x) for y in range(NY) for z in range(NZ) for x in range(NX)]
    number = {place: i * NC for i, place in enumerate(places)}
    pairs = [(number[p] + c, number[move(*p)] + c) for p in places for c, move in ((0, idle), (1, step))]
    return lax.ppermute(a, ("y", "z", "x", "c"), pairs)


def one_hop(first, second, k):
    axis, hop = {1: (first, 1), 3: (first, -1), 2: (second, 1)}[k]
    return lambda y, z, x: ((y + hop * (axis == "y")) % NY, (z + hop * (axis == "z")) % NZ, (x + hop * (axis == "x")) % NX)


def lead_shift(a, axis, k):
    if axis == "x":
        return lead(a, lambda y, z, x: (y, z, (x + k) % NX), one_hop("y", "z", k))
    if axis == "y":
        return lead(a, lambda y, z, x: ((y + k) % NY, z, x), one_hop("x", "z", k))
    return lead(a, lambda y, z, x: (y, (z + 2 * k) % NZ, x), one_hop("x", "y", k))


def both_shift(a, axis, k):
    return lead(a, lambda y, z, x: ((y + k) % NY, z, x), lambda y, z, x: (y, z, (x + k) % NX))


def lead_swap_z(a):
    return lead(a, lambda y, z, x: (y, z ^ 1, x), lambda y, z, x: (y, z, x ^ 1))


def swap_z(a):
    return lax.ppermute(a, "z", [(i, i ^ 1) for i in range(NZ)])


def shift(a, axis, k):
    size, step = {"y": (NY, 1), "z": (NZ, 2), "x": (NX, 1)}[axis]
    return lax.ppermute(a, axis, [(i, (i + k * step) % size) for i in range(size)])


def deal(blocks, axis, shift=shift):
    return [blocks[0]] + [shift(block, axis, k) for k, block in zip(DEALT[1:], blocks[1:], strict=True)]


def share(block, axis, shift=shift):
    return [block] + [shift(block, axis, k) for k in (1, 3, 2)]


def shards(hidden, cotangent, error_buf, q_start):
    qt = q_start.T
    dma, half = pltpu.SemaphoreType.DMA, RANK // 2
    pinned = [pltpu.with_memory_space_constraint(a, pltpu.HBM) for a in (q_start.T, cotangent, hidden, error_buf)]
    other = swap(cotangent)
    q3, q_own, cot = call(
        factor_kernel, [((3 * RANK, D), bf16), ((RANK, EB), f32), ((TB, D), bf16)], *pinned[:2],
        scratch=[pltpu.VMEM((RANK, D), f32), dma((6,))], hbm=(0, 1),
    )
    proj, both = call(project_kernel, [((TB, 2 * RANK), f32), ((2 * TB, D), bf16)], cot, other, q3)
    hid, err = call(
        fetch_kernel, [((TOK, FB), bf16), ((FB, EB), bf16)], *pinned[2:], proj, scratch=[dma((2,))], hbm=(0, 1), unread=(2,)
    )
    pair = call(join_x_kernel, ((2, TB, 2 * RANK), f32), proj, pair_x(proj, lambda x: x ^ 1))
    quarter, eighth = ((RANK // NY, FB), f32), ((RANK // NY // 2, FB), f32)
    parts = call(
        left_kernel, [quarter] * 4, pair, pair_x(pair, lambda x: NX - 1 - x), hid, err, q_own,
        scratch=[pltpu.VMEM((2, 2, TB, 2 * RANK), f32), pltpu.VMEM((RANK, FB), f32)],
    )

    parts = deal(parts, "y")
    blocks = call(columns_kernel, [((2 * TB, CB), bf16)] * NX, both, parts[2], unread=(1,))
    cot = deal(blocks, "x")
    keep, send = call(
        halve_kernel, [eighth, eighth], *parts, cot[0], scratch=[pltpu.VMEM((4, *quarter[0]), f32), pltpu.VMEM(*quarter)], unread=(4,)
    )
    p = call(add_kernel, eighth, keep, swap_z(send))
    p = call(
        sum_z_after_kernel, eighth, *share(p, "z"), cot[2], cot[3], scratch=[pltpu.VMEM((4, *eighth[0]), f32)], unread=(4, 5)
    )
    p = call(join_z_kernel, quarter, p, swap_z(p))

    mix, small = ((3 * RANK + half, EB), f32), ((half, 2 * RANK), f32)
    p3, mixed = call(
        mixed_kernel, [((3 * RANK, FB), bf16), mix], *share(p, "y"), hid, err, cot[1], scratch=[pltpu.VMEM((RANK, FB), f32)], unread=(6,)
    )
    mixed = call(add_kernel, mix, mixed, swap(mixed))
    mixed, gram = call(sum_x_kernel, [mix, small], *share(mixed, "x", lead_shift), scratch=[pltpu.VMEM((4, *mix[0]), f32)])

    piece, slots = ((RANK // NY, CB), f32), pltpu.VMEM((4, RANK // NY, CB), f32)
    parts = call(
        right_kernel, [piece] * 4, mixed, *cot, scratch=[pltpu.VMEM((4, 2 * TB, CB), bf16), pltpu.VMEM((RANK, CB), f32)]
    )
    gram_other = swap(gram)
    s = call(sum_y_kernel, piece, *deal(parts, "y", lead_shift), gram_other, scratch=[slots], unread=(4,))
    inverse = call(first_kernel, ((RANK, RANK), f32), gram, gram_other, s, unread=(2,))
    s = call(add_after_kernel, piece, s, lead_swap_z(s), inverse, unread=(2,))
    b3, gram = call(basis_kernel, [((3 * RANK, FB), bf16), small], inverse, p3, s, unread=(2,))
    s = call(sum_z_gram_kernel, piece, *share(s, "z", lead_shift), gram, swap(gram), scratch=[slots])
    quarters, square, whole = share(s, "y", both_shift), ((RANK, RANK), f32), ((RANK, CB), f32)
    s = call(block_kernel, whole, *quarters)
    second = call(second_kernel, square, *quarters, scratch=[pltpu.VMEM((4, RANK // NY, 4 * RANK), f32)])
    total, second = call(total_kernel, [square, square], second, swap(second), inverse)
    blocks = share(s, "x", lead_shift)
    blocks += [swap(b) for b in blocks]
    q_new, scaled = call(
        new_kernel, [((RANK, D), f32), ((RANK, FB), f32)], *blocks, total, second, b3,
        scratch=[pltpu.VMEM((NX, RANK, CB), f32), pltpu.VMEM((RANK, FB), f32), dma((NX + 1,))], out_hbm=True,
    )
    return scaled.T, q_new.T


def solution(mesh):
    fine = Mesh(mesh.devices.reshape(NY, NZ, NX, NC), ("y", "z", "x", "c"))
    dp, tensor = ("y", "z"), ("x", "c")
    placed = (P(dp, tensor), P(dp + tensor, None), P(tensor, dp), P())
    return jax.shard_map(
        shards, mesh=fine, in_specs=placed, out_specs=(P(tensor, None), P()), check_vma=False
    )
```

```python
import functools
import math

import jax
import jax.numpy as jnp
from jax import lax
from jax.experimental import pallas as pl
from jax.experimental.pallas import tpu as pltpu
from jax.sharding import Mesh
from jax.sharding import PartitionSpec as P

FF = 14336
D = 4096
RANK = 64
N_DP = 32
TOK = 256
NY, NZ, NX, NC = 4, 8, 4, 2
FB = FF // (NX * NC)
CB = D // NX
EB = D // N_DP
TB = TOK // (NX * NC)
f32, bf16 = jnp.float32, jnp.bfloat16
HIGHEST = lax.Precision.HIGHEST
NN = (((1,), (0,)), ((), ()))
NT = (((1,), (1,)), ((), ()))


def split3(a):
    hi = a.astype(bf16)
    rest = a - hi.astype(f32)
    mid = rest.astype(bf16)
    low = (rest - mid.astype(f32)).astype(bf16)
    return jnp.concatenate([hi, mid, low], axis=0)


def add3(a):
    n = a.shape[0] // 3
    return a[:n] + (a[n : 2 * n] + a[2 * n :])


def dot3(a, b, dims):
    return add3(lax.dot_general(a, b, dims, preferred_element_type=f32))


def gram3(a3):
    g = lax.dot_general(a3, a3, NT, preferred_element_type=f32)
    r = RANK
    g00, g01, g02 = g[:r, :r], g[:r, r : 2 * r], g[:r, 2 * r :]
    g10, g11, g20 = g[r : 2 * r, :r], g[r : 2 * r, r : 2 * r], g[2 * r :, :r]
    return g00 + ((g01 + g10) + (g11 + (g02 + g20)))


def wide(column):
    return jnp.broadcast_to(column, (8, 2 * RANK))


def inverse_factor(gram):
    rows = lax.broadcasted_iota(jnp.int32, (RANK, RANK), 0)
    cols = lax.broadcasted_iota(jnp.int32, (RANK, RANK), 1)
    both = jnp.concatenate([gram, jnp.where(rows == cols, 1.0, 0.0).astype(f32)], axis=1)
    sub = lax.broadcasted_iota(jnp.int32, (8, 2 * RANK), 0)
    count = RANK // 8
    tiles = [both[8 * i : 8 * i + 8] for i in range(count)]
    for p in range(count):
        columns = [[wide(tiles[i][:, 8 * p + j : 8 * p + j + 1]) for j in range(8)] for i in range(p, count)]
        panel, own, pivots, scales = tiles[p], columns[0], jnp.ones((8, 2 * RANK), f32), []
        for s in range(8):
            pivot = own[s][s : s + 1]
            scales.append(1.0 / pivot)
            pivots = jnp.where(sub == s, pivot, pivots)
            factor = jnp.where(sub > s, own[s] * scales[s], 0.0)
            panel = panel - factor * panel[s : s + 1]
            for j in range(s + 1, 8):
                own[j] = own[j] - factor * own[j][s : s + 1]
        for i in range(p + 1, count):
            below, tile = columns[i - p], tiles[i]
            for s in range(8):
                factor = below[s] * scales[s]
                tile = tile - factor * panel[s : s + 1]
                for j in range(s + 1, 8):
                    below[j] = below[j] - factor * own[j][s : s + 1]
            tiles[i] = tile
        tiles[p] = panel * lax.rsqrt(pivots)
    return jnp.concatenate(tiles, axis=0)[:, RANK:]


def near_inverse_factor(off):
    rows = lax.broadcasted_iota(jnp.int32, (RANK, RANK), 0)
    cols = lax.broadcasted_iota(jnp.int32, (RANK, RANK), 1)
    lower = jnp.where(rows > cols, 1.0, jnp.where(rows == cols, 0.5, 0.0)).astype(f32)
    first = off * lower
    second = -lower * lax.dot_general(first, first, NT, precision=HIGHEST, preferred_element_type=f32)
    square = jnp.dot(first, first, precision=HIGHEST, preferred_element_type=f32)
    eye = jnp.where(rows == cols, 1.0, 0.0).astype(f32)
    return eye - first + (square - second)


def dot6(a, b3):
    hi = a.astype(bf16).astype(f32)
    mid = (a - hi).astype(bf16).astype(f32)
    low = a - hi - mid
    one = jnp.concatenate([hi, hi, hi, mid], axis=1).astype(bf16)
    two = jnp.concatenate([mid, low], axis=1).astype(bf16)
    high, middle = b3[:RANK], b3[RANK : 2 * RANK]
    out = jnp.dot(one, jnp.concatenate([b3, high], axis=0), preferred_element_type=f32)
    return out + jnp.dot(two, jnp.concatenate([middle, high], axis=0), preferred_element_type=f32)


def pack(square):
    return jnp.concatenate([square[: RANK // 2], square[RANK // 2 :]], axis=1)


def unpack(packed):
    return jnp.concatenate([packed[:, :RANK], packed[:, RANK:]], axis=0)


def call(kernel, out_shape, *args, scratch=(), hbm=(), unread=(), out_hbm=False):
    vmem, far, anywhere = (pl.BlockSpec(memory_space=m) for m in (pltpu.VMEM, pltpu.HBM, pl.ANY))
    many = isinstance(out_shape, list)
    shapes = [jax.ShapeDtypeStruct(*s) for s in (out_shape if many else [out_shape])]
    return pl.pallas_call(
        kernel,
        out_shape=shapes if many else shapes[0],
        in_specs=[far if i in hbm else anywhere if i in unread else vmem for i in range(len(args))],
        out_specs=[far if out_hbm else vmem] * len(shapes) if many else vmem,
        scratch_shapes=list(scratch),
        compiler_params=pltpu.CompilerParams(vmem_limit_bytes=32 * 1024 * 1024),
    )(*args)


DEALT = (0, 2, 1, 3)


def rows_at(index, size):
    return pl.ds(pl.multiple_of(index * size, size), size)


def in_order(index, refs, ks=(0, 1, 3, 2)):
    for k, ref in zip(ks, refs, strict=True):
        yield lax.rem(index + 4 - k, 4), ref


def sum_in_order(slots_ref, index, refs, ks=(0, 1, 3, 2)):
    for place, ref in in_order(index, refs, ks):
        slots_ref[place] = ref[...]
    return (slots_ref[0] + slots_ref[1]) + (slots_ref[2] + slots_ref[3])


def scatter(whole_ref, index, refs):
    size = whole_ref.shape[0] // 4
    for k, ref in zip(DEALT, refs, strict=True):
        ref[...] = whole_ref[rows_at(lax.rem(index + k, 4), size), :]


def factor_kernel(qt_ref, cot_ref, q3_ref, own_ref, cot_out_ref, qt, sems):
    at, cut = lax.axis_index("y") * NZ + lax.axis_index("z"), 1024
    pairs = [(qt_ref.at[:, i : i + cut], qt.at[:, i : i + cut]) for i in range(0, D, cut)]
    pairs += [(qt_ref.at[:, rows_at(at, EB)], own_ref), (cot_ref, cot_out_ref)]
    copies = [pltpu.make_async_copy(a, b, sems.at[i]) for i, (a, b) in enumerate(pairs)]
    for copy in copies:
        copy.start()
    for i in range(D // cut):
        copies[i].wait()
        q3_ref[:, i * cut : (i + 1) * cut] = split3(qt[:, i * cut : (i + 1) * cut])
    copies[-2].wait()
    copies[-1].wait()


def project_kernel(cot_ref, other_ref, q3_ref, out_ref, both_ref):
    c = lax.axis_index("c")
    both_ref[rows_at(c, TB), :] = cot_ref[...]
    both_ref[rows_at(1 - c, TB), :] = other_ref[...]
    got = lax.dot_general(both_ref[...], q3_ref[...], NT, preferred_element_type=f32)
    got = got[:, :RANK] + (got[:, RANK : 2 * RANK] + got[:, 2 * RANK :])
    part = TB // 2
    for i in range(NC):
        own = got[i * TB : (i + 1) * TB]
        out_ref[i * part : (i + 1) * part, :] = jnp.concatenate([own[:part], own[part:]], axis=1)


def fetch_kernel(hidden_ref, err_ref, after_ref, h_ref, e_ref, sems):
    copies = [pltpu.make_async_copy(a, b, sems.at[i]) for i, (a, b) in enumerate(((hidden_ref, h_ref), (err_ref, e_ref)))]
    for copy in copies:
        copy.start()
    for copy in copies:
        copy.wait()


def columns_kernel(both_ref, after_ref, *out_refs):
    x = lax.axis_index("x")
    for k, ref in zip(DEALT, out_refs, strict=True):
        ref[...] = both_ref[:, rows_at(lax.rem(x + k, NX), CB)]


def join_x_kernel(own_ref, other_ref, out_ref):
    bit = lax.rem(lax.axis_index("x"), 2)
    out_ref[bit] = own_ref[...]
    out_ref[1 - bit] = other_ref[...]


def left_kernel(pair_ref, far_ref, hidden_ref, err_ref, q_ref, own_ref, a_ref, b_ref, c_ref, slots_ref, whole_ref):
    at = lax.axis_index("x") // 2
    slots_ref[at] = pair_ref[...]
    slots_ref[1 - at] = far_ref[...]
    packed = slots_ref[...].reshape(TOK // 2, 2 * RANK).T
    proj = jnp.concatenate([packed[:RANK], packed[RANK:]], axis=1)
    h = hidden_ref[...].reshape(NX * NC, 2, TB // 2, FB)
    h = jnp.concatenate([h[:, 0].reshape(TOK // 2, FB), h[:, 1].reshape(TOK // 2, FB)], axis=0)
    whole_ref[...] = dot3(split3(proj), h, NN) + dot3(split3(q_ref[...]), err_ref[...], NT)
    scatter(whole_ref, lax.axis_index("y"), (own_ref, a_ref, b_ref, c_ref))


def halve_kernel(own_ref, a_ref, b_ref, c_ref, after_ref, keep_ref, send_ref, slots_ref, both_ref):
    both_ref[...] = sum_in_order(slots_ref, lax.axis_index("y"), (own_ref, a_ref, b_ref, c_ref), DEALT)
    bit, half = lax.rem(lax.axis_index("z"), 2), keep_ref.shape[0]
    keep_ref[...] = both_ref[rows_at(bit, half), :]
    send_ref[...] = both_ref[rows_at(1 - bit, half), :]


def add_kernel(a_ref, b_ref, out_ref):
    out_ref[...] = a_ref[...] + b_ref[...]


def sum_z_kernel(own_ref, a_ref, b_ref, c_ref, out_ref, slots_ref):
    out_ref[...] = sum_in_order(slots_ref, lax.axis_index("z") // 2, (own_ref, a_ref, b_ref, c_ref))


def sum_z_after_kernel(own_ref, a_ref, b_ref, c_ref, *rest):
    sum_z_kernel(own_ref, a_ref, b_ref, c_ref, *rest[-2:])


def sum_x_kernel(own_ref, a_ref, b_ref, c_ref, out_ref, gram_ref, slots_ref):
    out_ref[...] = sum_in_order(slots_ref, lax.axis_index("x"), (own_ref, a_ref, b_ref, c_ref))
    gram_ref[...] = out_ref[3 * RANK :, :]


def join_z_kernel(own_ref, other_ref, out_ref):
    bit, half = lax.rem(lax.axis_index("z"), 2), own_ref.shape[0]
    out_ref[rows_at(bit, half), :] = own_ref[...]
    out_ref[rows_at(1 - bit, half), :] = other_ref[...]


def mixed_kernel(own_ref, a_ref, b_ref, c_ref, hidden_ref, err_ref, after_ref, p3_ref, all_ref, p_ref):
    for place, ref in in_order(lax.axis_index("y"), (own_ref, a_ref, b_ref, c_ref)):
        p_ref[rows_at(place, RANK // NY), :] = ref[...]
    p3 = split3(p_ref[...])
    p3_ref[...] = p3
    mixed = dot3(p3, hidden_ref[...], NT)
    all_ref[:RANK, :] = mixed[:, :EB]
    all_ref[RANK : 2 * RANK, :] = mixed[:, EB:]
    all_ref[2 * RANK : 3 * RANK, :] = dot3(p3, err_ref[...], NN)
    all_ref[3 * RANK :, :] = pack(gram3(p3))


def right_kernel(mixed_ref, cot_ref, a_cot_ref, b_cot_ref, c_cot_ref, own_ref, a_ref, b_ref, c_ref, slots_ref, whole_ref):
    x, at = lax.axis_index("x"), lax.axis_index("y") * NZ + lax.axis_index("z")
    for place, ref in in_order(x, (cot_ref, a_cot_ref, b_cot_ref, c_cot_ref), DEALT):
        slots_ref[place] = ref[...]
    mixed = jnp.concatenate([mixed_ref[:RANK, :], mixed_ref[RANK : 2 * RANK, :]], axis=1)
    part = dot3(split3(mixed), slots_ref[...].reshape(TOK, CB), NN)
    err_q = mixed_ref[2 * RANK : 3 * RANK, :]
    here = [jnp.where(at == x * (CB // EB) + i, err_q, 0.0) for i in range(CB // EB)]
    whole_ref[...] = part + jnp.concatenate(here, axis=1)
    scatter(whole_ref, lax.axis_index("y"), (own_ref, a_ref, b_ref, c_ref))


def first_kernel(own_ref, other_ref, after_ref, inv_ref):
    inv_ref[...] = inverse_factor(unpack(jnp.where(lax.axis_index("c") == 1, own_ref[...], other_ref[...])))


def basis_kernel(inv_ref, p3_ref, b3_ref, gram_ref):
    b3 = split3(dot6(inv_ref[...], p3_ref[...]))
    b3_ref[...] = b3
    gram_ref[...] = pack(gram3(b3))


def sum_y_kernel(own_ref, a_ref, b_ref, c_ref, after_ref, out_ref, slots_ref):
    out_ref[...] = sum_in_order(slots_ref, lax.axis_index("y"), (own_ref, a_ref, b_ref, c_ref), DEALT)


def add_after_kernel(a_ref, b_ref, after_ref, out_ref):
    out_ref[...] = a_ref[...] + b_ref[...]


def block_kernel(own_ref, a_ref, b_ref, c_ref, gram_ref, other_ref, out_ref):
    for place, ref in in_order(lax.axis_index("y"), (own_ref, a_ref, b_ref, c_ref)):
        out_ref[rows_at(place, RANK // NY), :CB] = ref[...]
    out_ref[: RANK // 2, CB:] = gram_ref[...] + other_ref[...]
    out_ref[RANK // 2 :, CB:] = jnp.zeros((RANK // 2, 2 * RANK), f32)


def second_kernel(*refs):
    inv_ref, total_ref, inverse_ref, slots_ref = refs[2 * NX :]
    core = lax.axis_index("c") == 1
    for k, (place, ref) in enumerate(in_order(lax.axis_index("x"), refs[:NX])):
        slots_ref[place] = jnp.where(core, ref[: RANK // 2, CB:], refs[NX + k][: RANK // 2, CB:])
    gram = unpack((slots_ref[0] + slots_ref[1]) + (slots_ref[2] + slots_ref[3]))
    rows = lax.broadcasted_iota(jnp.int32, (RANK, RANK), 0)
    cols = lax.broadcasted_iota(jnp.int32, (RANK, RANK), 1)
    off = gram - jnp.where(rows == cols, 1.0, 0.0).astype(f32)
    near = jnp.max(jnp.abs(off)) < 1e-3

    @pl.when(near)
    def _():
        inverse_ref[...] = near_inverse_factor(off)

    @pl.when(jnp.logical_not(near))
    def _():
        inverse_ref[...] = inverse_factor(gram)

    inverse = inverse_ref[...]
    total_ref[...] = jnp.dot(inverse, inv_ref[...], precision=HIGHEST, preferred_element_type=f32) * (1.0 / N_DP)


def new_kernel(*refs):
    total_ref, inverse_ref, b3_ref, out_ref, basis_ref, whole_ref, scaled_ref, sems = refs[2 * NX :]
    x, core, total, copies = lax.axis_index("x"), lax.axis_index("c") == 1, total_ref[...], []
    for k, (place, ref) in enumerate(in_order(x, refs[:NX])):
        block = jnp.where(core, ref[:, :CB], refs[NX + k][:, :CB])
        whole_ref[k] = dot6(total, split3(block))
        cols = rows_at(place, CB)
        copies.append(pltpu.make_async_copy(whole_ref.at[k], out_ref.at[:, cols], sems.at[k]))
        copies[-1].start()
        if k == 0:
            scaled_ref[...] = dot6(inverse_ref[...] * math.sqrt(FF), b3_ref[...])
            copies.append(pltpu.make_async_copy(scaled_ref, basis_ref, sems.at[NX]))
            copies[-1].start()
    for copy in copies:
        copy.wait()


def swap(a):
    return lax.ppermute(a, "c", [(0, 1), (1, 0)])


def pair_x(a, partner):
    return lax.ppermute(a, "x", [(x, partner(x)) for x in range(NX)])


def lead(a, step, idle):
    places = [(y, z, x) for y in range(NY) for z in range(NZ) for x in range(NX)]
    number = {place: i * NC for i, place in enumerate(places)}
    pairs = [(number[p] + c, number[move(*p)] + c) for p in places for c, move in ((0, idle), (1, step))]
    return lax.ppermute(a, ("y", "z", "x", "c"), pairs)


def one_hop(first, second, k):
    axis, hop = {1: (first, 1), 3: (first, -1), 2: (second, 1)}[k]
    return lambda y, z, x: ((y + hop * (axis == "y")) % NY, (z + hop * (axis == "z")) % NZ, (x + hop * (axis == "x")) % NX)


def lead_shift(a, axis, k):
    if axis == "x":
        return lead(a, lambda y, z, x: (y, z, (x + k) % NX), one_hop("y", "z", k))
    if axis == "y":
        return lead(a, lambda y, z, x: ((y + k) % NY, z, x), one_hop("x", "z", k))
    return lead(a, lambda y, z, x: (y, (z + 2 * k) % NZ, x), one_hop("x", "y", k))


def lead_swap_z(a):
    return lead(a, lambda y, z, x: (y, z ^ 1, x), lambda y, z, x: (y, z, x ^ 1))


def swap_z(a):
    return lax.ppermute(a, "z", [(i, i ^ 1) for i in range(NZ)])


def shift(a, axis, k):
    size, step = {"y": (NY, 1), "z": (NZ, 2), "x": (NX, 1)}[axis]
    return lax.ppermute(a, axis, [(i, (i + k * step) % size) for i in range(size)])


def deal(blocks, axis, shift=shift):
    return [blocks[0]] + [shift(block, axis, k) for k, block in zip(DEALT[1:], blocks[1:], strict=True)]


def share(block, axis, shift=shift):
    return [block] + [shift(block, axis, k) for k in (1, 3, 2)]


def shards(hidden, cotangent, error_buf, q_start):
    qt = q_start.T
    dma, half = pltpu.SemaphoreType.DMA, RANK // 2
    pinned = [pltpu.with_memory_space_constraint(a, pltpu.HBM) for a in (q_start.T, cotangent, hidden, error_buf)]
    other = swap(cotangent)
    q3, q_own, cot = call(
        factor_kernel, [((3 * RANK, D), bf16), ((RANK, EB), f32), ((TB, D), bf16)], *pinned[:2],
        scratch=[pltpu.VMEM((RANK, D), f32), dma((6,))], hbm=(0, 1),
    )
    proj, both = call(project_kernel, [((TB, 2 * RANK), f32), ((2 * TB, D), bf16)], cot, other, q3)
    hid, err = call(
        fetch_kernel, [((TOK, FB), bf16), ((FB, EB), bf16)], *pinned[2:], proj, scratch=[dma((2,))], hbm=(0, 1), unread=(2,)
    )
    pair = call(join_x_kernel, ((2, TB, 2 * RANK), f32), proj, pair_x(proj, lambda x: x ^ 1))
    quarter, eighth = ((RANK // NY, FB), f32), ((RANK // NY // 2, FB), f32)
    parts = call(
        left_kernel, [quarter] * 4, pair, pair_x(pair, lambda x: NX - 1 - x), hid, err, q_own,
        scratch=[pltpu.VMEM((2, 2, TB, 2 * RANK), f32), pltpu.VMEM((RANK, FB), f32)],
    )

    parts = deal(parts, "y")
    blocks = call(columns_kernel, [((2 * TB, CB), bf16)] * NX, both, parts[2], unread=(1,))
    cot = deal(blocks, "x")
    keep, send = call(
        halve_kernel, [eighth, eighth], *parts, cot[0], scratch=[pltpu.VMEM((4, *quarter[0]), f32), pltpu.VMEM(*quarter)], unread=(4,)
    )
    p = call(add_kernel, eighth, keep, swap_z(send))
    p = call(
        sum_z_after_kernel, eighth, *share(p, "z"), cot[2], cot[3], scratch=[pltpu.VMEM((4, *eighth[0]), f32)], unread=(4, 5)
    )
    p = call(join_z_kernel, quarter, p, swap_z(p))

    mix, small = ((3 * RANK + half, EB), f32), ((half, 2 * RANK), f32)
    p3, mixed = call(
        mixed_kernel, [((3 * RANK, FB), bf16), mix], *share(p, "y"), hid, err, cot[1], scratch=[pltpu.VMEM((RANK, FB), f32)], unread=(6,)
    )
    mixed = call(add_kernel, mix, mixed, swap(mixed))
    mixed, gram = call(sum_x_kernel, [mix, small], *share(mixed, "x", lead_shift), scratch=[pltpu.VMEM((4, *mix[0]), f32)])

    piece, slots = ((RANK // NY, CB), f32), pltpu.VMEM((4, RANK // NY, CB), f32)
    parts = call(
        right_kernel, [piece] * 4, mixed, *cot, scratch=[pltpu.VMEM((4, 2 * TB, CB), bf16), pltpu.VMEM((RANK, CB), f32)]
    )
    inverse = call(first_kernel, ((RANK, RANK), f32), gram, swap(gram), parts[0], unread=(2,))
    s = call(sum_y_kernel, piece, *deal(parts, "y", lead_shift), inverse, scratch=[slots], unread=(4,))
    b3, gram = call(basis_kernel, [((3 * RANK, FB), bf16), small], inverse, p3)
    s = call(add_after_kernel, piece, s, lead_swap_z(s), gram, unread=(2,))
    s = call(sum_z_kernel, piece, *share(s, "z", lead_shift), scratch=[slots])
    s = call(block_kernel, ((RANK, CB + 2 * RANK), f32), *share(s, "y", lead_shift), gram, swap(gram))
    blocks = share(s, "x", lead_shift)
    blocks += [swap(b) for b in blocks]
    square = ((RANK, RANK), f32)
    total, second = call(second_kernel, [square, square], *blocks, inverse, scratch=[pltpu.VMEM((4, *small[0]), f32)])
    q_new, scaled = call(
        new_kernel, [((RANK, D), f32), ((RANK, FB), f32)], *blocks, total, second, b3,
        scratch=[pltpu.VMEM((NX, RANK, CB), f32), pltpu.VMEM((RANK, FB), f32), dma((NX + 1,))], out_hbm=True,
    )
    return scaled.T, q_new.T


def solution(mesh):
    fine = Mesh(mesh.devices.reshape(NY, NZ, NX, NC), ("y", "z", "x", "c"))
    dp, tensor = ("y", "z"), ("x", "c")
    placed = (P(dp, tensor), P(dp + tensor, None), P(tensor, dp), P())
    return jax.shard_map(
        shards, mesh=fine, in_specs=placed, out_specs=(P(tensor, None), P()), check_vma=False
    )
```
